128 devices in a mesh: rows: 4 (over z), lat: 32 (over x, y, core).
Axes of the slice: x: 4, y: 4, z: 4, core: 2. Of those that a mesh axis runs over, the one named last changes fastest.
Arguments:
- mlp_inputs: bfloat16 [512, 8192], P(None, 'rows'), may hold values from -6 to 6
- enc_weight: bfloat16 [8192, 16384], P('rows', 'lat'), may hold values from -0.0625 to 0.0625
- enc_bias: float32 [16384], P('lat'), may hold values from -3 to 3
- active: int32 [512, 16384], P(None, 'lat'), may hold values from 0 to 1, as said below
- dec_weight: bfloat16 [3, 16384, 8192], P(None, 'lat', 'rows'), may hold values from -0.625 to 0.625
- target: bfloat16 [3, 512, 8192], P(None, 'lat', 'rows'), may hold values from -6 to 6
Outputs:
- enc_grad: bfloat16 [8192, 16384], P('rows', 'lat')
- bias_grad: float32 [16384], P('lat')
- dec_grad: bfloat16 [3, 16384, 8192], P(None, 'lat', 'rows')
The draws below stay inside these ranges and needn't reach their ends.
Inputs may be any that keep to these rules, and one draw needn't show every extreme that they name: active[r, f] is 1 where latent f fires on row r.
All inputs are finite; a program needn't handle non-finite values.
Results may differ from the reference program's by a relative error of at most 0.0062.
Values may be sent and summed in bfloat16 or wider, within the bound.
No kernel may reach another device: no remote copies, remote signals or barrier semaphores. Data moves between devices by JAX's collectives and lax.ppermute only.
A program may use at most 128 MiB of HBM per device.

```python
import math
import jax
import jax.numpy as jnp
from jax import lax

D = 8192
F = 16384
TARGETS = 3
ROWS = 512


def draw_active(key, part):
    key = jax.random.fold_in(key, 7)
    group_key, cell_key = jax.random.split(key)
    levels = jax.random.randint(group_key, (F // 16,), 2, 21)
    cutoff = jnp.repeat(levels, 16)
    samples = jax.random.randint(cell_key, (ROWS, F), 0, F // 8)
    return (samples < cutoff[None, :]).astype(jnp.int32)


def block_scale(rng, dims, cuts, smallest, top_value):
    gain = 1.0
    for position, parts in cuts:
        heights = jax.random.uniform(jax.random.fold_in(jax.random.fold_in(rng, 6), position), (parts,), jnp.float32, smallest / len(cuts), top_value / len(cuts))
        gain = gain * jnp.repeat(jnp.exp(heights), dims[position] // parts).reshape((-1,) + (1,) * (len(dims) - 1 - position))
    return gain


def centred(stream_key, dims, width, reach, cuts=(), dtype=jnp.bfloat16):
    entries = jax.random.normal(stream_key, dims, jnp.float32) * width
    if len(cuts) > 0:
        entries = block_scale(stream_key, dims, cuts, -0.22, 0.18) * entries
    return jnp.clip(entries, min=-reach, max=reach).astype(dtype)


def setup_inputs(seed: int = 0) -> dict:
    key_of = jax.random.split(jax.random.key(seed), 7)
    return {
        "mlp_inputs": centred(key_of[0], (ROWS, D), 1.0, 6.0, ((1, 4),)),
        "enc_weight": centred(key_of[1], (D, F), D ** -0.5, 0.0625, ((0, 4), (1, 32))),
        "enc_bias": centred(key_of[2], (F,), 0.5, 3.0, ((0, 32),), jnp.float32),
        "active": draw_active(jax.random.fold_in(key_of[6], 71), 0),
        "dec_weight": centred(key_of[4], (TARGETS, F, D), (max(F // 160, 16)) ** -0.5, 0.625, ((1, 32), (2, 4))),
        "target": centred(key_of[5], (TARGETS, ROWS, D), 1.0, 6.0, ((1, 32), (2, 4))),
    }


def reference(mlp_inputs, enc_weight, enc_bias, active, dec_weight, target):
    preact = jnp.dot(mlp_inputs, enc_weight, preferred_element_type=jnp.float32) + enc_bias
    latents = jnp.where(active > 0, preact, jnp.zeros_like(preact)).astype(jnp.bfloat16)
    error_scale = 1.0 / math.sqrt(ROWS)
    latent_grad = jnp.zeros(preact.shape, jnp.float32)
    dec_parts = []
    for target_id in range(TARGETS):
        rebuilt = jnp.dot(latents, dec_weight[target_id], preferred_element_type=jnp.float32)
        scaled_error = ((rebuilt - target[target_id]) * error_scale).astype(jnp.bfloat16)
        dec_parts.append(jnp.dot(latents.T, scaled_error, preferred_element_type=jnp.float32).astype(jnp.bfloat16))
        latent_grad = latent_grad + jnp.dot(scaled_error, dec_weight[target_id].T, preferred_element_type=jnp.float32)
    pre_grad = jnp.where(active > 0, latent_grad, jnp.zeros_like(latent_grad)).astype(jnp.bfloat16)
    enc_grad = jnp.dot(mlp_inputs.T, pre_grad, preferred_element_type=jnp.float32).astype(jnp.bfloat16)
    bias_grad = lax.optimization_barrier(jnp.sum(pre_grad.astype(jnp.float32), axis=0))
    return (enc_grad, bias_grad, jnp.stack(dec_parts))
```

```python
import math

import jax
import jax.numpy as jnp
from jax import lax
from jax.sharding import Mesh, PartitionSpec as P

TARGETS = 3
BF = jnp.bfloat16
F32 = jnp.float32


def shift(value, axis, step):
    size = lax.axis_size(axis)
    return lax.ppermute(value, axis, [(i, (i + step) % size) for i in range(size)])


def pick(value, index, axis):
    return lax.dynamic_index_in_dim(value, index, axis, keepdims=False)


def scatter_sum(blocks, axis, dim):
    size = lax.axis_size(axis)
    me = lax.axis_index(axis)
    got = [
        shift(pick(blocks, lax.rem(me + k, size), dim).astype(BF), axis, k)
        for k in (2, 1, 3)
    ]
    total = pick(blocks, me, dim).astype(F32)
    for piece in got:
        total = total + piece.astype(F32)
    return total


def gather(value, axis, dim):
    size = lax.axis_size(axis)
    me = lax.axis_index(axis)
    got = [value] + [shift(value, axis, k) for k in range(1, size)]
    order = [pick(jnp.stack([got[(p - j) % size] for p in range(size)]), me, 0) for j in range(size)]
    return jnp.stack(order, axis=dim)


def per_device(mlp_inputs, enc_weight, enc_bias, active, dec_weight, target):
    rows = mlp_inputs.shape[0]
    zs, xs, ys = lax.axis_size("z"), lax.axis_size("x"), lax.axis_size("y")
    z, x, y, c = (lax.axis_index(a) for a in "zxyc")
    own = rows // zs
    lat_n = enc_weight.shape[1]
    half = dec_weight.shape[2] // 2
    scale = 1.0 / math.sqrt(rows)

    sent = lax.dynamic_slice_in_dim(dec_weight, (1 - c) * half, half, 2)
    dec_sib = shift(sent, "c", 1)
    dec_own = lax.dynamic_slice_in_dim(dec_weight, c * half, half, 2)
    dec = jnp.concatenate([dec_own, dec_sib], axis=1)
    tgt_sent = lax.dynamic_slice_in_dim(target, (1 - c) * half, half, 2)
    tgt_own = lax.dynamic_slice_in_dim(target, c * half, half, 2)
    tgt_sib = shift(tgt_sent, "c", 1)
    tgt = jnp.where(
        c == 0,
        jnp.concatenate([tgt_own, tgt_sib], axis=1),
        jnp.concatenate([tgt_sib, tgt_own], axis=1),
    )

    def z_sum(value):
        got = lax.all_to_all(value.astype(BF).reshape(zs, own, lat_n), "z", 0, 0)
        return jnp.sum(got.astype(F32), axis=0)

    def z_gather(value):
        got = lax.all_to_all(jnp.broadcast_to(value[None], (zs,) + value.shape), "z", 0, 0)
        return got.reshape(rows, lat_n)

    mask = lax.dynamic_slice_in_dim(active, z * own, own, 0) > 0
    pre = z_sum(jnp.dot(mlp_inputs, enc_weight, preferred_element_type=F32)) + enc_bias
    lat_own = z_gather(jnp.where(mask, pre, 0.0).astype(BF))
    latents = jnp.concatenate([lat_own, shift(lat_own, "c", 1)], axis=1)

    parts = [jnp.dot(latents, dec[t], preferred_element_type=F32).astype(BF) for t in range(TARGETS)]
    rebuilt = jnp.stack(parts).reshape(TARGETS, xs, ys, rows // (xs * ys), half)
    q = half // 2
    sum_a = scatter_sum(rebuilt[..., :q], "x", 1)
    sum_b = scatter_sum(rebuilt[..., q:], "y", 2)
    sum_a = scatter_sum(sum_a, "y", 1)
    sum_b = scatter_sum(sum_b, "x", 1)
    err_a = ((sum_a - tgt[..., :q].astype(F32)) * scale).astype(BF)
    err_b = ((sum_b - tgt[..., q:].astype(F32)) * scale).astype(BF)
    err_a = gather(err_a, "y", 1)
    err_b = gather(err_b, "x", 1)
    err_a = gather(err_a, "x", 1).reshape(TARGETS, rows, q)
    err_b = gather(err_b, "y", 2).reshape(TARGETS, rows, q)
    err = jnp.concatenate([err_a, err_b], axis=2)

    lat_grad = jnp.zeros((rows, 2 * lat_n), F32)
    for t in range(TARGETS):
        lat_grad = lat_grad + jnp.einsum("rd,fd->rf", err[t], dec[t], preferred_element_type=F32)
    lat_grad = lat_grad[:, :lat_n] + shift(lat_grad[:, lat_n:].astype(BF), "c", 1).astype(F32)
    grad_own = jnp.where(mask, z_sum(lat_grad), 0.0).astype(BF)
    pre_grad = z_gather(grad_own)
    enc_grad = jnp.einsum("rd,rf->df", mlp_inputs, pre_grad, preferred_element_type=F32).astype(BF)
    bias_grad = jnp.sum(pre_grad.astype(F32), axis=0)

    dec_parts = []
    for t in range(TARGETS):
        total = jnp.einsum("rf,rd->fd", latents, err[t], preferred_element_type=F32).astype(BF)
        mine, other = total[:lat_n], shift(total[lat_n:], "c", 1)
        dec_parts.append(
            jnp.where(
                c == 0,
                jnp.concatenate([mine, other], axis=1),
                jnp.concatenate([other, mine], axis=1),
            )
        )
    return enc_grad, bias_grad, jnp.stack(dec_parts)


def solution(mesh):
    grid = Mesh(mesh.devices.reshape(4, 4, 4, 2), ("z", "x", "y", "c"))
    lat = ("x", "y", "c")
    in_specs = (
        P(None, "z"),
        P("z", lat),
        P(lat),
        P(None, lat),
        P(None, lat, "z"),
        P(None, lat, "z"),
    )
    out_specs = (P("z", lat), P(lat), P(None, lat, "z"))
    return jax.shard_map(
        per_device, mesh=grid, in_specs=in_specs, out_specs=out_specs, check_vma=False
    )
```

```python
import functools
import math

import jax
import jax.numpy as jnp
from jax import lax
from jax.experimental import pallas as pl
from jax.experimental.pallas import tpu as pltpu
from jax.sharding import Mesh, PartitionSpec as P

BF = jnp.bfloat16
F32 = jnp.float32
VMEM_LIMIT = 16 * 1024 * 1024
SIDE = 4


def dot(a, b, ca, cb):
    return lax.dot_general(a, b, (((ca,), (cb,)), ((), ())), preferred_element_type=F32)


def call(body, name, grid, ins, outs, shapes, args, flops, moved, scratch=(), core=None):
    spec = dict(grid=grid, in_specs=ins, out_specs=outs, scratch_shapes=list(scratch))
    if core is not None:
        spec = dict(grid_spec=pltpu.PrefetchScalarGridSpec(num_scalar_prefetch=1, **spec))
        args = (core,) + tuple(args)
    return pl.pallas_call(
        body,
        out_shape=shapes,
        compiler_params=pltpu.CompilerParams(
            dimension_semantics=("arbitrary",) * len(grid), vmem_limit_bytes=VMEM_LIMIT
        ),
        cost_estimate=pl.CostEstimate(
            flops=int(flops), bytes_accessed=int(moved), transcendentals=0
        ),
        name=name,
        **spec,
    )(*args)


def pre_kernel(x_ref, w_ref, a_ref, b_ref, acc):
    k = pl.program_id(0)
    part = jnp.dot(x_ref[...], w_ref[...], preferred_element_type=F32)

    @pl.when(k == 0)
    def _():
        acc[...] = part

    @pl.when(k > 0)
    def _():
        acc[...] += part

    @pl.when(k == pl.num_programs(0) - 1)
    def _():
        n = a_ref.shape[0]
        a_ref[...] = acc[:n, :].astype(BF)
        b_ref[...] = acc[n:, :].astype(BF)


def pre_call(x, w):
    rows, depth = x.shape
    lats = w.shape[1]
    step = 512
    part = pl.BlockSpec((rows // 2, lats), lambda k: (0, 0))
    return call(
        pre_kernel,
        "pre",
        (depth // step,),
        [
            pl.BlockSpec((rows, step), lambda k: (0, k)),
            pl.BlockSpec((step, lats), lambda k: (k, 0)),
        ],
        [part, part],
        [jax.ShapeDtypeStruct((rows // 2, lats), BF)] * 2,
        (x, w),
        2 * rows * depth * lats,
        2 * (rows + lats) * depth,
        [pltpu.VMEM((rows, lats), F32)],
    )


def pick_kernel(p_ref, dec_ref, after_ref, out_ref):
    out_ref[...] = dec_ref[...]


def pick_call(place, dec, after):
    targets, lats, wide = dec.shape
    half = wide // 2
    return call(
        pick_kernel,
        "pick_half",
        (targets,),
        [
            pl.BlockSpec((1, lats, half), lambda t, p: (t, 0, 1 - p[2])),
            pl.BlockSpec(memory_space=pl.ANY),
        ],
        pl.BlockSpec((1, lats, half), lambda t, p: (t, 0, 0)),
        jax.ShapeDtypeStruct((targets, lats, half), BF),
        (dec, after),
        0,
        4 * targets * lats * half,
        core=place,
    )


def rebuild_a_kernel(p_ref, lat_ref, sib_ref, dec_ref, got_ref, out_ref):
    total = jnp.dot(lat_ref[...], dec_ref[0], preferred_element_type=F32)
    total += jnp.dot(sib_ref[...], got_ref[0], preferred_element_type=F32)
    out_ref[:, 0] = total.astype(BF).reshape(SIDE, SIDE, out_ref.shape[3], out_ref.shape[4])


def rebuild_b_kernel(p_ref, lat_ref, sib_ref, dec_ref, got_ref, *refs):
    outs, held = refs[:SIDE], refs[SIDE]
    total = jnp.dot(lat_ref[...], dec_ref[0], preferred_element_type=F32)
    total += jnp.dot(sib_ref[...], got_ref[0], preferred_element_type=F32)
    held[...] = total.astype(BF).reshape(held.shape)
    for k in range(SIDE):
        y = lax.rem(p_ref[1] + k, SIDE)
        for x in range(SIDE):
            outs[k][x, 0] = held[x * SIDE + y]


def rebuild_call(second, place, lat, sib, dec, got):
    rows, lats = lat.shape
    targets, _, half = got.shape
    q = half // 2
    piece = rows // (SIDE * SIDE)
    whole = pl.BlockSpec((rows, lats), lambda t, p: (0, 0))
    if second:
        outs = [pl.BlockSpec((SIDE, 1, piece, q), lambda t, p: (0, t, 0, 0))] * SIDE
        shapes = [jax.ShapeDtypeStruct((SIDE, targets, piece, q), BF)] * SIDE
        scratch = [pltpu.VMEM((SIDE * SIDE, piece, q), BF)]
    else:
        outs = pl.BlockSpec((SIDE, 1, SIDE, piece, q), lambda t, p: (0, t, 0, 0, 0))
        shapes = jax.ShapeDtypeStruct((SIDE, targets, SIDE, piece, q), BF)
        scratch = []
    return call(
        rebuild_b_kernel if second else rebuild_a_kernel,
        "rebuild_b" if second else "rebuild_a",
        (targets,),
        [
            whole,
            whole,
            pl.BlockSpec((1, lats, q), lambda t, p: (t, 0, 2 * p[2] + second)),
            pl.BlockSpec((1, lats, q), lambda t, p: (t, 0, second)),
        ],
        outs,
        shapes,
        (lat, sib, dec, got),
        4 * rows * lats * q * targets,
        6e6,
        scratch,
        core=place,
    )


def sum_a_kernel(parts_ref, out_ref):
    total = parts_ref[0, 0].astype(F32)
    for p in range(1, SIDE):
        total += parts_ref[p, 0].astype(F32)
    out_ref[:, 0] = total.astype(BF)


def sum_a_call(parts):
    _, targets, _, piece, q = parts.shape
    return call(
        sum_a_kernel,
        "sum_a",
        (targets,),
        [pl.BlockSpec((SIDE, 1, SIDE, piece, q), lambda t: (0, t, 0, 0, 0))],
        pl.BlockSpec((SIDE, 1, piece, q), lambda t: (0, t, 0, 0)),
        jax.ShapeDtypeStruct((SIDE, targets, piece, q), BF),
        (parts,),
        parts.size,
        2.5 * parts.size,
    )


def sum_b_kernel(p_ref, *refs):
    parts, outs, held = refs[:SIDE], refs[SIDE : 2 * SIDE], refs[2 * SIDE]
    total = parts[0][:, 0].astype(F32)
    for part in parts[1:]:
        total += part[:, 0].astype(F32)
    held[...] = total.astype(BF)
    for k in range(SIDE):
        outs[k][0] = held[lax.rem(p_ref[0] + k, SIDE)]


def sum_b_call(place, parts):
    _, targets, piece, q = parts[0].shape
    return call(
        sum_b_kernel,
        "sum_b",
        (targets,),
        [pl.BlockSpec((SIDE, 1, piece, q), lambda t, p: (0, t, 0, 0))] * SIDE,
        [pl.BlockSpec((1, piece, q), lambda t, p: (t, 0, 0))] * SIDE,
        [jax.ShapeDtypeStruct((targets, piece, q), BF)] * SIDE,
        tuple(parts),
        4 * parts[0].size,
        10 * parts[0].size,
        [pltpu.VMEM((SIDE, piece, q), BF)],
        core=place,
    )


def error_kernel(scale, target_ref, a_ref, *refs):
    parts, (a_out, b_out) = refs[:SIDE], refs[SIDE:]
    q = b_out.shape[2]
    total = a_ref[0, 0].astype(F32)
    for p in range(1, SIDE):
        total += a_ref[p, 0].astype(F32)
    err = ((total - target_ref[0, :, :q].astype(F32)) * scale).astype(BF)
    for p in range(SIDE):
        a_out[p, 0] = err
    total = parts[0][0].astype(F32)
    for part in parts[1:]:
        total += part[0].astype(F32)
    b_out[0] = ((total - target_ref[0, :, q:].astype(F32)) * scale).astype(BF)


def error_call(scale, target, a, parts):
    _, targets, piece, q = a.shape
    four = pl.BlockSpec((SIDE, 1, piece, q), lambda t: (0, t, 0, 0))
    one = pl.BlockSpec((1, piece, q), lambda t: (t, 0, 0))
    return call(
        functools.partial(error_kernel, scale),
        "error",
        (targets,),
        [pl.BlockSpec((1, piece, 2 * q), lambda t: (t, 0, 0)), four] + [one] * SIDE,
        [four, one],
        [
            jax.ShapeDtypeStruct((SIDE, targets, piece, q), BF),
            jax.ShapeDtypeStruct((targets, piece, q), BF),
        ],
        (target, a, *parts),
        8 * targets * piece * q,
        2e6,
    )


def join_kernel(p_ref, *refs):
    parts, out_ref = refs[:SIDE], refs[SIDE]
    for k in range(SIDE):
        x = lax.rem(p_ref[0] + SIDE - k, SIDE)
        for y in range(SIDE):
            out_ref[y, x, 0] = parts[k][0]


def join_call(place, parts):
    targets, piece, q = parts[0].shape
    return call(
        join_kernel,
        "join",
        (targets,),
        [pl.BlockSpec((1, piece, q), lambda t, p: (t, 0, 0))] * SIDE,
        pl.BlockSpec((SIDE, SIDE, 1, piece, q), lambda t, p: (0, 0, t, 0, 0)),
        jax.ShapeDtypeStruct((SIDE, SIDE, targets, piece, q), BF),
        tuple(parts),
        0,
        2e6,
        core=place,
    )


def back_dot(err, dec_ref, out_ref, acc):
    t = pl.program_id(0)
    part = dot(err, dec_ref[0], 1, 1)

    @pl.when(t == 0)
    def _():
        acc[...] = part

    @pl.when(t > 0)
    def _():
        acc[...] += part

    @pl.when(t == pl.num_programs(0) - 1)
    def _():
        out_ref[...] = acc[...].astype(out_ref.dtype)


def back_sib_kernel(p_ref, dec_ref, after_ref, b_ref, *refs):
    parts, (err_ref, out_ref, acc) = refs[:SIDE], refs[SIDE:]
    piece, q = b_ref.shape[3:]
    strip = SIDE * piece
    for k in range(SIDE):
        x = lax.rem(p_ref[0] + SIDE - k, SIDE)
        at = pl.ds(pl.multiple_of(x * strip, strip), strip)
        err_ref[0, at, :q] = parts[k][:, 0].reshape(strip, q)
    for x in range(SIDE):
        for y in range(SIDE):
            at = (x * SIDE + y) * piece
            err_ref[0, at : at + piece, q:] = b_ref[y, x, 0]
    back_dot(err_ref[0], dec_ref, out_ref, acc)


def back_sib_call(place, a_parts, b, dec, after):
    _, _, targets, piece, q = b.shape
    lats, half = dec.shape[1:]
    rows = SIDE * SIDE * piece
    return call(
        back_sib_kernel,
        "back_sib",
        (targets,),
        [
            pl.BlockSpec((1, lats, half), lambda t, p: (t, 0, 0)),
            pl.BlockSpec(memory_space=pl.ANY),
            pl.BlockSpec((SIDE, SIDE, 1, piece, q), lambda t, p: (0, 0, t, 0, 0)),
        ]
        + [pl.BlockSpec((SIDE, 1, piece, q), lambda t, p: (0, t, 0, 0))] * SIDE,
        [
            pl.BlockSpec((1, rows, half), lambda t, p: (t, 0, 0)),
            pl.BlockSpec((rows, lats), lambda t, p: (0, 0)),
        ],
        [
            jax.ShapeDtypeStruct((targets, rows, half), BF),
            jax.ShapeDtypeStruct((rows, lats), BF),
        ],
        (dec, after, b, *a_parts),
        2 * rows * lats * half * targets,
        10e6,
        [pltpu.VMEM((rows, lats), F32)],
        core=place,
    )


def back_own_kernel(p_ref, err_ref, dec_ref, out_ref, acc):
    back_dot(err_ref[0], dec_ref, out_ref, acc)


def back_own_call(place, err, dec):
    targets, rows, half = err.shape
    lats = dec.shape[1]
    return call(
        back_own_kernel,
        "back_own",
        (targets,),
        [
            pl.BlockSpec((1, rows, half), lambda t, p: (t, 0, 0)),
            pl.BlockSpec((1, lats, half), lambda t, p: (t, 0, p[2])),
        ],
        pl.BlockSpec((rows, lats), lambda t, p: (0, 0)),
        jax.ShapeDtypeStruct((rows, lats), F32),
        (err, dec),
        2 * rows * lats * half * targets,
        7e6,
        [pltpu.VMEM((rows, lats), F32)],
        core=place,
    )


def turn_kernel(x_ref, lat_ref, sib_ref, after_ref, x_out, lat_out, sib_out):
    x_out[...] = x_ref[...].T

    @pl.when(pl.program_id(0) == 0)
    def _():
        lat_out[...] = lat_ref[...].T
        sib_out[...] = sib_ref[...].T


def turn_call(x, lat, sib, after):
    rows, depth = x.shape
    lats = lat.shape[1]
    step = 512
    whole = pl.BlockSpec((rows, lats), lambda i: (0, 0))
    turned = pl.BlockSpec((lats, rows), lambda i: (0, 0))
    return call(
        turn_kernel,
        "turn",
        (depth // step,),
        [
            pl.BlockSpec((rows, step), lambda i: (0, i)),
            whole,
            whole,
            pl.BlockSpec(memory_space=pl.ANY),
        ],
        [pl.BlockSpec((step, rows), lambda i: (i, 0)), turned, turned],
        [jax.ShapeDtypeStruct((depth, rows), BF)] + [jax.ShapeDtypeStruct((lats, rows), BF)] * 2,
        (x, lat, sib, after),
        0,
        6e6,
    )


def dec_sib_kernel(lat_ref, err_ref, after_ref, out_ref):
    out_ref[0] = dot(lat_ref[...], err_ref[0], 1, 0).astype(BF)


def dec_sib_call(lat, err, after):
    targets, rows, half = err.shape
    lats = lat.shape[0]
    return call(
        dec_sib_kernel,
        "dec_sib",
        (targets,),
        [
            pl.BlockSpec((lats, rows), lambda t: (0, 0)),
            pl.BlockSpec((1, rows, half), lambda t: (t, 0, 0)),
            pl.BlockSpec(memory_space=pl.ANY),
        ],
        pl.BlockSpec((1, lats, half), lambda t: (t, 0, 0)),
        jax.ShapeDtypeStruct((targets, lats, half), BF),
        (lat, err, after),
        2 * rows * lats * half * targets,
        7e6,
    )


def dec_kernel(p_ref, lat_ref, err_ref, got_ref, out_ref):
    j = pl.program_id(1)

    @pl.when(j == 0)
    def _():
        out_ref[0] = dot(lat_ref[...], err_ref[0], 1, 0).astype(BF)

    @pl.when(j == 1)
    def _():
        out_ref[...] = got_ref[...]


def dec_call(place, lat, err, got):
    targets, rows, half = err.shape
    lats = lat.shape[0]
    return call(
        dec_kernel,
        "dec_grad",
        (targets, 2),
        [
            pl.BlockSpec((lats, rows), lambda t, j, p: (0, 0)),
            pl.BlockSpec((1, rows, half), lambda t, j, p: (t, 0, 0)),
            pl.BlockSpec((1, lats, half), lambda t, j, p: (t, 0, 0)),
        ],
        pl.BlockSpec((1, lats, half), lambda t, j, p: (t, 0, (j + p[2]) % 2)),
        jax.ShapeDtypeStruct((targets, lats, 2 * half), BF),
        (lat, err, got),
        2 * rows * lats * half * targets,
        13e6,
        core=place,
    )


def enc_kernel(x_ref, active_ref, after_ref, *refs):
    parts, (enc_ref, bias_ref, grad) = refs[:4], refs[4:]

    @pl.when(pl.program_id(0) == 0)
    def _():
        n = parts[0].shape[0]
        sums = jnp.zeros(bias_ref.shape, F32)
        for i in range(2):
            total = parts[2 * i][...].astype(F32) + parts[2 * i + 1][...].astype(F32)
            on = active_ref[i * n : (i + 1) * n, :] > 0
            kept = jnp.where(on, total, 0.0).astype(BF)
            grad[i * n : (i + 1) * n, :] = kept
            sums += jnp.sum(kept.astype(F32), axis=0, keepdims=True)
        bias_ref[...] = sums

    enc_ref[...] = dot(x_ref[...], grad[...], 1, 0).astype(BF)


def enc_call(x, active, after, parts):
    depth, rows = x.shape
    lats = active.shape[1]
    step = 512
    part = pl.BlockSpec((rows // 2, lats), lambda i: (0, 0))
    return call(
        enc_kernel,
        "enc_grad",
        (depth // step,),
        [
            pl.BlockSpec((step, rows), lambda i: (i, 0)),
            pl.BlockSpec((rows, lats), lambda i: (0, 0)),
            pl.BlockSpec(memory_space=pl.ANY),
            part,
            part,
            part,
            part,
        ],
        [
            pl.BlockSpec((step, lats), lambda i: (i, 0)),
            pl.BlockSpec((1, lats), lambda i: (0, 0)),
        ],
        [jax.ShapeDtypeStruct((depth, lats), BF), jax.ShapeDtypeStruct((1, lats), F32)],
        (x, active, after, *parts),
        2 * rows * depth * lats,
        7e6,
        [pltpu.VMEM((rows, lats), BF)],
    )


def swap(value):
    return lax.ppermute(value, "c", [(0, 1), (1, 0)])


EVEN = [(0, 1), (1, 0), (2, 3), (3, 2)]
ODD = [(1, 2), (2, 1), (3, 0), (0, 3)]


def z_pairs(a, b):
    a_got = lax.ppermute(a, "z", EVEN)
    b_got = lax.ppermute(b, "z", ODD)
    a = (a.astype(F32) + a_got.astype(F32)).astype(BF)
    b = (b.astype(F32) + b_got.astype(F32)).astype(BF)
    return a, lax.ppermute(a, "z", ODD), b, lax.ppermute(b, "z", EVEN)


def shift(value, axis, step):
    size = lax.axis_size(axis)
    return lax.ppermute(value, axis, [(i, (i + step) % size) for i in range(size)])


def per_device(mlp_inputs, enc_weight, enc_bias, active, dec_weight, target):
    rows = mlp_inputs.shape[0]
    core = lax.axis_index("c")
    place = jnp.stack([lax.axis_index(a) for a in "xyc"]).astype(jnp.int32)
    half = dec_weight.shape[2] // 2
    scale = 1.0 / math.sqrt(rows)
    mid = rows // 2

    pre_a, pre_b = pre_call(mlp_inputs, enc_weight)
    dec_got = swap(pick_call(place, dec_weight, pre_a))
    tgt_own = lax.dynamic_slice_in_dim(target, core * half, half, 2)
    tgt_got = swap(lax.dynamic_slice_in_dim(target, (1 - core) * half, half, 2))
    tgt = jnp.where(
        core == 0,
        jnp.concatenate([tgt_own, tgt_got], axis=1),
        jnp.concatenate([tgt_got, tgt_own], axis=1),
    )

    a, a_got, b, b_got = z_pairs(pre_a, pre_b)
    pre = jnp.concatenate(
        [a.astype(F32) + a_got.astype(F32), b.astype(F32) + b_got.astype(F32)], axis=0
    )
    lat = jnp.where(active > 0, pre + enc_bias, 0.0).astype(BF)
    lat_sib = swap(lat)

    far = (2, 1, 3)
    a_sum = rebuild_call(0, place, lat, lat_sib, dec_weight, dec_got)
    a_sum = lax.all_to_all(a_sum, "x", 0, 0)
    b_sum = rebuild_call(1, place, lat, lat_sib, dec_weight, dec_got)
    b_sum = [b_sum[0]] + [shift(b_sum[k], "y", k) for k in far]
    a_sum = lax.all_to_all(sum_a_call(a_sum), "y", 0, 0)
    b_sum = sum_b_call(place, b_sum)
    b_sum = [b_sum[0]] + [shift(b_sum[k], "x", k) for k in far]
    a_err, b_err = error_call(scale, tgt, a_sum, b_sum)
    x_turned, lat_turned, sib_turned = turn_call(mlp_inputs, lat, lat_sib, b_err)
    a_err = lax.all_to_all(a_err, "y", 0, 0)
    b_err = join_call(place, [b_err] + [shift(b_err, "x", k) for k in (1, 2, 3)])
    b_err = lax.all_to_all(b_err, "y", 0, 0)
    a_err = [a_err] + [shift(a_err, "x", k) for k in (1, 2, 3)]

    err, grad_got = back_sib_call(place, a_err, b_err, dec_got, x_turned)
    grad_got = swap(grad_got)
    grad_own = back_own_call(place, err, dec_weight)
    grad = (grad_own + grad_got.astype(F32)).astype(BF)
    dec_part = swap(dec_sib_call(sib_turned, err, grad))
    sums = z_pairs(grad[:mid], grad[mid:])
    dec_grad = dec_call(place, lat_turned, err, dec_part)
    enc_grad, bias_grad = enc_call(x_turned, active, dec_grad, sums)
    return enc_grad, bias_grad.reshape(-1), dec_grad


def solution(mesh):
    grid = Mesh(mesh.devices.reshape(4, 4, 4, 2), ("z", "x", "y", "c"))
    lat = ("x", "y", "c")
    in_specs = (
        P(None, "z"),
        P("z", lat),
        P(lat),
        P(None, lat),
        P(None, lat, "z"),
        P(None, lat, "z"),
    )
    out_specs = (P("z", lat), P(lat), P(None, lat, "z"))
    return jax.shard_map(
        per_device, mesh=grid, in_specs=in_specs, out_specs=out_specs, check_vma=False
    )
```

```python
import functools
import math

import jax
import jax.numpy as jnp
from jax import lax
from jax.experimental import pallas as pl
from jax.experimental.pallas import tpu as pltpu
from jax.sharding import Mesh, PartitionSpec as P

BF = jnp.bfloat16
F32 = jnp.float32
VMEM_LIMIT = 16 * 1024 * 1024
PRE_LIMIT = 60 * 1024 * 1024
SIDE = 4


def dot(a, b, ca, cb):
    return lax.dot_general(a, b, (((ca,), (cb,)), ((), ())), preferred_element_type=F32)


def call(body, name, grid, ins, outs, shapes, args, flops, moved, scratch=(), core=None, limit=VMEM_LIMIT):
    spec = dict(grid=grid, in_specs=ins, out_specs=outs, scratch_shapes=list(scratch))
    if core is not None:
        spec = dict(grid_spec=pltpu.PrefetchScalarGridSpec(num_scalar_prefetch=1, **spec))
        args = (core,) + tuple(args)
    return pl.pallas_call(
        body,
        out_shape=shapes,
        compiler_params=pltpu.CompilerParams(
            dimension_semantics=("arbitrary",) * len(grid), vmem_limit_bytes=limit
        ),
        cost_estimate=pl.CostEstimate(
            flops=int(flops), bytes_accessed=int(moved), transcendentals=0
        ),
        name=name,
        **spec,
    )(*args)


def pre_kernel(p_ref, x_ref, w_ref, dec_ref, tgt_ref, part_ref, dec_out, own_ref, sent_ref, acc):
    k = pl.program_id(0)
    dec_out[...] = dec_ref[...]
    part = jnp.dot(x_ref[...], w_ref[...], preferred_element_type=F32)

    @pl.when(k == 0)
    def _():
        acc[...] = part
        half = own_ref.shape[2]
        for ref, side in ((own_ref, p_ref[2]), (sent_ref, 1 - p_ref[2])):
            ref[...] = tgt_ref[:, :, pl.ds(pl.multiple_of(side * half, half), half)]

    @pl.when(k > 0)
    def _():
        acc[...] += part

    @pl.when(k == pl.num_programs(0) - 1)
    def _():
        part_ref[...] = acc[...].astype(BF)


def pre_call(place, x, w, dec, target):
    rows, depth = x.shape
    lats = w.shape[1]
    targets, few, wide = target.shape
    half = wide // 2
    step = 512
    steps = depth // step
    goal = pl.BlockSpec((targets, few, half), lambda k, p: (0, 0, 0))
    return call(
        pre_kernel,
        "pre",
        (steps,),
        [
            pl.BlockSpec((rows, step), lambda k, p: (0, k)),
            pl.BlockSpec((step, lats), lambda k, p: (k, 0)),
            pl.BlockSpec((targets, lats // steps, half), lambda k, p: (0, k, 1 - p[2])),
            pl.BlockSpec((targets, few, wide), lambda k, p: (0, 0, 0)),
        ],
        [
            pl.BlockSpec((rows, lats), lambda k, p: (0, 0)),
            pl.BlockSpec((targets, lats // steps, half), lambda k, p: (0, k, 0)),
            goal,
            goal,
        ],
        [
            jax.ShapeDtypeStruct((rows, lats), BF),
            jax.ShapeDtypeStruct((targets, lats, half), BF),
        ]
        + [jax.ShapeDtypeStruct((targets, few, half), BF)] * 2,
        (x, w, dec, target),
        2 * rows * depth * lats,
        2 * (rows + lats) * depth,
        [pltpu.VMEM((rows, lats), F32)],
        core=place,
        limit=PRE_LIMIT,
    )


def place_of(p_ref, far, near):
    return jnp.where(p_ref[2] == 0, far * SIDE + near, near * SIDE + far)


def rebuild_kernel(p_ref, lat_ref, sib_ref, dec_ref, got_ref, *refs):
    outs, held = refs[:SIDE], refs[SIDE]
    total = jnp.dot(lat_ref[...], dec_ref[0], preferred_element_type=F32)
    total += jnp.dot(sib_ref[...], got_ref[0], preferred_element_type=F32)
    held[...] = total.reshape(held.shape)
    for k in range(SIDE):
        to = lax.rem(p_ref[3] + k, SIDE)
        for i in range(SIDE):
            outs[k][i, 0] = held[place_of(p_ref, to, i)].astype(outs[k].dtype)


def rebuild_call(place, lat, sib, dec, got):
    rows, lats = lat.shape
    targets, _, half = got.shape
    piece = rows // (SIDE * SIDE)
    whole = pl.BlockSpec((rows, lats), lambda t, p: (0, 0))
    return call(
        rebuild_kernel,
        "rebuild",
        (targets,),
        [
            whole,
            whole,
            pl.BlockSpec((1, lats, half), lambda t, p: (t, 0, p[2])),
            pl.BlockSpec((1, lats, half), lambda t, p: (t, 0, 0)),
        ],
        [pl.BlockSpec((SIDE, 1, piece, half), lambda t, p: (0, t, 0, 0))] * SIDE,
        [
            jax.ShapeDtypeStruct((SIDE, targets, piece, half), F32 if k == 0 else BF)
            for k in range(SIDE)
        ],
        (lat, sib, dec, got),
        4 * rows * lats * half * targets,
        11e6,
        [pltpu.VMEM((SIDE * SIDE, piece, half), F32)],
        core=place,
    )


def sum_kernel(p_ref, *refs):
    parts, outs, held = refs[:SIDE], refs[SIDE : 2 * SIDE], refs[2 * SIDE]
    total = parts[0][:, 0]
    for part in parts[1:]:
        total += part[:, 0].astype(F32)
    held[...] = total
    for k in range(SIDE):
        outs[k][0] = held[lax.rem(p_ref[4] + k, SIDE)].astype(outs[k].dtype)


def sum_call(place, parts):
    _, targets, piece, half = parts[0].shape
    return call(
        sum_kernel,
        "sum_first",
        (targets,),
        [pl.BlockSpec((SIDE, 1, piece, half), lambda t, p: (0, t, 0, 0))] * SIDE,
        [pl.BlockSpec((1, piece, half), lambda t, p: (t, 0, 0))] * SIDE,
        [jax.ShapeDtypeStruct((targets, piece, half), F32 if k == 0 else BF) for k in range(SIDE)],
        tuple(parts),
        4 * parts[0].size,
        12 * parts[0].size,
        [pltpu.VMEM((SIDE, piece, half), F32)],
        core=place,
    )


def error_kernel(scale, p_ref, own_ref, got_ref, *refs):
    parts, out, goal = refs[:SIDE], refs[SIDE], refs[SIDE + 1]
    few = own_ref.shape[1]
    for ref, side in ((own_ref, p_ref[2]), (got_ref, 1 - p_ref[2])):
        goal[pl.ds(pl.multiple_of(side * few, few), few), :] = ref[0].astype(F32)
    total = parts[0][0]
    for part in parts[1:]:
        total += part[0].astype(F32)
    out[0] = ((total - goal[...]) * scale).astype(BF)


def error_call(scale, place, own, got, parts):
    targets, piece, half = parts[0].shape
    one = pl.BlockSpec((1, piece, half), lambda t, p: (t, 0, 0))
    goal = pl.BlockSpec((1,) + own.shape[1:], lambda t, p: (t, 0, 0))
    return call(
        functools.partial(error_kernel, scale),
        "error",
        (targets,),
        [goal, goal] + [one] * SIDE,
        one,
        jax.ShapeDtypeStruct((targets, piece, half), BF),
        (own, got, *parts),
        8 * targets * piece * half,
        2e6,
        [pltpu.VMEM((piece, half), F32)],
        core=place,
    )


def join_kernel(p_ref, *refs):
    parts, out_ref = refs[:SIDE], refs[SIDE]
    for k in range(SIDE):
        out_ref[lax.rem(p_ref[4] + SIDE - k, SIDE), 0] = parts[k][0]


def join_call(place, parts):
    targets, piece, half = parts[0].shape
    return call(
        join_kernel,
        "join",
        (targets,),
        [pl.BlockSpec((1, piece, half), lambda t, p: (t, 0, 0))] * SIDE,
        pl.BlockSpec((SIDE, 1, piece, half), lambda t, p: (0, t, 0, 0)),
        jax.ShapeDtypeStruct((SIDE, targets, piece, half), BF),
        tuple(parts),
        0,
        8 * parts[0].size,
        core=place,
    )


def back_dot(err, dec_ref, out_ref, acc):
    t = pl.program_id(0)
    part = dot(err, dec_ref[0], 1, 1)

    @pl.when(t == 0)
    def _():
        acc[...] = part

    @pl.when(t > 0)
    def _():
        acc[...] += part

    @pl.when(t == pl.num_programs(0) - 1)
    def _():
        out_ref[...] = acc[...].astype(out_ref.dtype)


def back_sib_kernel(p_ref, dec_ref, after_ref, *refs):
    parts, (err_ref, out_ref, acc) = refs[:SIDE], refs[SIDE:]
    piece = parts[0].shape[2]
    for k in range(SIDE):
        far = lax.rem(p_ref[3] + SIDE - k, SIDE)
        for i in range(SIDE):
            at = pl.ds(pl.multiple_of(place_of(p_ref, far, i) * piece, piece), piece)
            err_ref[0, at, :] = parts[k][i, 0]
    back_dot(err_ref[0], dec_ref, out_ref, acc)


def back_sib_call(place, parts, dec, after):
    _, targets, piece, half = parts[0].shape
    lats = dec.shape[1]
    rows = SIDE * SIDE * piece
    return call(
        back_sib_kernel,
        "back_sib",
        (targets,),
        [
            pl.BlockSpec((1, lats, half), lambda t, p: (t, 0, 0)),
            pl.BlockSpec(memory_space=pl.ANY),
        ]
        + [pl.BlockSpec((SIDE, 1, piece, half), lambda t, p: (0, t, 0, 0))] * SIDE,
        [
            pl.BlockSpec((1, rows, half), lambda t, p: (t, 0, 0)),
            pl.BlockSpec((rows, lats), lambda t, p: (0, 0)),
        ],
        [
            jax.ShapeDtypeStruct((targets, rows, half), BF),
            jax.ShapeDtypeStruct((rows, lats), BF),
        ],
        (dec, after, *parts),
        2 * rows * lats * half * targets,
        10e6,
        [pltpu.VMEM((rows, lats), F32)],
        core=place,
    )


def back_own_kernel(p_ref, err_ref, dec_ref, out_ref, acc):
    back_dot(err_ref[0], dec_ref, out_ref, acc)


def back_own_call(place, err, dec):
    targets, rows, half = err.shape
    lats = dec.shape[1]
    return call(
        back_own_kernel,
        "back_own",
        (targets,),
        [
            pl.BlockSpec((1, rows, half), lambda t, p: (t, 0, 0)),
            pl.BlockSpec((1, lats, half), lambda t, p: (t, 0, p[2])),
        ],
        pl.BlockSpec((rows, lats), lambda t, p: (0, 0)),
        jax.ShapeDtypeStruct((rows, lats), F32),
        (err, dec),
        2 * rows * lats * half * targets,
        7e6,
        [pltpu.VMEM((rows, lats), F32)],
        core=place,
    )


def turn_kernel(x_ref, lat_ref, sib_ref, after_ref, x_out, lat_out, sib_out, done_ref):
    done_ref[...] = jnp.zeros(done_ref.shape, F32)
    x_out[...] = x_ref[...].T

    @pl.when(pl.program_id(0) == 0)
    def _():
        lat_out[...] = lat_ref[...].T
        sib_out[...] = sib_ref[...].T


def turn_call(x, lat, sib, after):
    rows, depth = x.shape
    lats = lat.shape[1]
    step = 512
    whole = pl.BlockSpec((rows, lats), lambda i: (0, 0))
    turned = pl.BlockSpec((lats, rows), lambda i: (0, 0))
    return call(
        turn_kernel,
        "turn",
        (depth // step,),
        [
            pl.BlockSpec((rows, step), lambda i: (0, i)),
            whole,
            whole,
            pl.BlockSpec(memory_space=pl.ANY),
        ],
        [
            pl.BlockSpec((step, rows), lambda i: (i, 0)),
            turned,
            turned,
            pl.BlockSpec((8, 128), lambda i: (0, 0)),
        ],
        [jax.ShapeDtypeStruct((depth, rows), BF)]
        + [jax.ShapeDtypeStruct((lats, rows), BF)] * 2
        + [jax.ShapeDtypeStruct((8, 128), F32)],
        (x, lat, sib, after),
        0,
        6e6,
    )


def dec_sib_kernel(lat_ref, err_ref, after_ref, out_ref):
    out_ref[0] = dot(lat_ref[...], err_ref[0], 1, 0).astype(BF)


def dec_sib_call(lat, err, after):
    targets, rows, half = err.shape
    lats = lat.shape[0]
    return call(
        dec_sib_kernel,
        "dec_sib",
        (targets,),
        [
            pl.BlockSpec((lats, rows), lambda t: (0, 0)),
            pl.BlockSpec((1, rows, half), lambda t: (t, 0, 0)),
            pl.BlockSpec(memory_space=pl.ANY),
        ],
        pl.BlockSpec((1, lats, half), lambda t: (t, 0, 0)),
        jax.ShapeDtypeStruct((targets, lats, half), BF),
        (lat, err, after),
        2 * rows * lats * half * targets,
        7e6,
    )


def dec_kernel(p_ref, lat_ref, err_ref, got_ref, out_ref, done_ref):
    j = pl.program_id(1)
    done_ref[...] = jnp.zeros(done_ref.shape, F32)

    @pl.when(j == 0)
    def _():
        out_ref[0] = dot(lat_ref[...], err_ref[0], 1, 0).astype(BF)

    @pl.when(j == 1)
    def _():
        out_ref[...] = got_ref[...]


def dec_call(place, lat, err, got):
    targets, rows, half = err.shape
    lats = lat.shape[0]
    return call(
        dec_kernel,
        "dec_grad",
        (targets, 2),
        [
            pl.BlockSpec((lats, rows), lambda t, j, p: (0, 0)),
            pl.BlockSpec((1, rows, half), lambda t, j, p: (t, 0, 0)),
            pl.BlockSpec((1, lats, half), lambda t, j, p: (t, 0, 0)),
        ],
        [
            pl.BlockSpec((1, lats, half), lambda t, j, p: (t, 0, (j + p[2]) % 2)),
            pl.BlockSpec((8, 128), lambda t, j, p: (0, 0)),
        ],
        [
            jax.ShapeDtypeStruct((targets, lats, 2 * half), BF),
            jax.ShapeDtypeStruct((8, 128), F32),
        ],
        (lat, err, got),
        2 * rows * lats * half * targets,
        13e6,
        core=place,
    )


def enc_kernel(x_ref, active_ref, after_ref, sum_ref, got_ref, enc_ref, bias_ref, grad):
    @pl.when(pl.program_id(0) == 0)
    def _():
        total = sum_ref[...] + got_ref[...].astype(F32)
        kept = jnp.where(active_ref[...] > 0, total, 0.0).astype(BF)
        grad[...] = kept
        bias_ref[...] = jnp.sum(kept.astype(F32), axis=0, keepdims=True)

    enc_ref[...] = dot(x_ref[...], grad[...], 1, 0).astype(BF)


def enc_call(x, active, after, sums, got):
    depth, rows = x.shape
    lats = active.shape[1]
    step = 512
    whole = pl.BlockSpec((rows, lats), lambda i: (0, 0))
    return call(
        enc_kernel,
        "enc_grad",
        (depth // step,),
        [
            pl.BlockSpec((step, rows), lambda i: (i, 0)),
            whole,
            pl.BlockSpec(memory_space=pl.ANY),
            whole,
            whole,
        ],
        [
            pl.BlockSpec((step, lats), lambda i: (i, 0)),
            pl.BlockSpec((1, lats), lambda i: (0, 0)),
        ],
        [jax.ShapeDtypeStruct((depth, lats), BF), jax.ShapeDtypeStruct((1, lats), F32)],
        (x, active, after, sums, got),
        2 * rows * depth * lats,
        7e6,
        [pltpu.VMEM((rows, lats), BF)],
    )


def swap(value):
    return lax.ppermute(value, "c", [(0, 1), (1, 0)])


EVEN = (1, 0, 3, 2)
ODD = (3, 2, 1, 0)


def pair(value, tables):
    moves = [(z * 2 + c, tables[c][z] * 2 + c) for z in range(SIDE) for c in range(2)]
    return lax.ppermute(value, ("z", "c"), moves)


def z_sum(part):
    first = part.astype(F32) + pair(part.astype(BF), (EVEN, ODD)).astype(F32)
    return first, pair(first.astype(BF), (ODD, EVEN))


def shift(value, second, step):
    moves = []
    for x in range(SIDE):
        for y in range(SIDE):
            for c in range(2):
                along_x = (c == 0) != second
                to = ((x + step) % SIDE, y) if along_x else (x, (y + step) % SIDE)
                moves.append(((x * SIDE + y) * 2 + c, (to[0] * SIDE + to[1]) * 2 + c))
    return lax.ppermute(value, ("x", "y", "c"), moves)


def scatter(parts, second):
    return [parts[0]] + [shift(parts[k], second, k) for k in (1, 2, 3)]


def spread(value, second):
    return [value] + [shift(value, second, k) for k in (1, 2, 3)]


def per_device(mlp_inputs, enc_weight, enc_bias, active, dec_weight, target):
    rows = mlp_inputs.shape[0]
    x, y, c = (lax.axis_index(a) for a in "xyc")
    first, second = jnp.where(c == 0, x, y), jnp.where(c == 0, y, x)
    place = jnp.stack([x, y, c, first, second]).astype(jnp.int32)
    scale = 1.0 / math.sqrt(rows)

    part, dec_sent, tgt_own, tgt_sent = pre_call(
        place, mlp_inputs, enc_weight, dec_weight, target
    )
    dec_got = swap(dec_sent)
    tgt_got = swap(tgt_sent)
    near, far = z_sum(part)
    lat = jnp.where(active > 0, near + far.astype(F32) + enc_bias, 0.0).astype(BF)
    lat_sib = swap(lat)

    parts = scatter(rebuild_call(place, lat, lat_sib, dec_weight, dec_got), False)
    parts = scatter(sum_call(place, parts), True)
    err = error_call(scale, place, tgt_own, tgt_got, parts)
    parts = spread(join_call(place, spread(err, True)), False)
    x_turned, lat_turned, sib_turned, done = turn_call(mlp_inputs, lat, lat_sib, parts[1])

    err, grad_got = back_sib_call(place, parts, dec_got, done)
    grad_got = swap(grad_got)
    near, far = z_sum(back_own_call(place, err, dec_weight) + grad_got.astype(F32))
    dec_part = swap(dec_sib_call(sib_turned, err, near))
    dec_grad, done = dec_call(place, lat_turned, err, dec_part)
    enc_grad, bias_grad = enc_call(x_turned, active, done, near, far)
    return enc_grad, bias_grad.reshape(-1), dec_grad


def solution(mesh):
    grid = Mesh(mesh.devices.reshape(4, 4, 4, 2), ("z", "x", "y", "c"))
    lat = ("x", "y", "c")
    in_specs = (
        P(None, "z"),
        P("z", lat),
        P(lat),
        P(None, lat),
        P(None, lat, "z"),
        P(None, lat, "z"),
    )
    out_specs = (P("z", lat), P(lat), P(None, lat, "z"))
    return jax.shard_map(
        per_device, mesh=grid, in_specs=in_specs, out_specs=out_specs, check_vma=False
    )
```

```python
import functools
import math

import jax
import jax.numpy as jnp
from jax import lax
from jax.experimental import pallas as pl
from jax.experimental.pallas import tpu as pltpu
from jax.sharding import Mesh, PartitionSpec as P

BF = jnp.bfloat16
F32 = jnp.float32
VMEM_LIMIT = 16 * 1024 * 1024
PRE_LIMIT = 60 * 1024 * 1024
SIDE = 4


def dot(a, b, ca, cb):
    return lax.dot_general(a, b, (((ca,), (cb,)), ((), ())), preferred_element_type=F32)


def call(body, name, grid, ins, outs, shapes, args, flops, moved, scratch=(), core=None, limit=VMEM_LIMIT, aliases=None):
    spec = dict(grid=grid, in_specs=ins, out_specs=outs, scratch_shapes=list(scratch))
    if core is not None:
        spec = dict(grid_spec=pltpu.PrefetchScalarGridSpec(num_scalar_prefetch=1, **spec))
        args = (core,) + tuple(args)
    return pl.pallas_call(
        body,
        out_shape=shapes,
        compiler_params=pltpu.CompilerParams(
            dimension_semantics=("arbitrary",) * len(grid), vmem_limit_bytes=limit
        ),
        cost_estimate=pl.CostEstimate(
            flops=int(flops), bytes_accessed=int(moved), transcendentals=0
        ),
        name=name,
        input_output_aliases=aliases or {},
        **spec,
    )(*args)


STEPS = 4


def pre_kernel(p_ref, x_ref, w_ref, dec_ref, tgt_ref, a_ref, b_ref, *refs):
    outs, (x_buf, w_buf, acc, sems) = refs[:3], refs[3:]
    depth = x_ref.shape[1]
    step = depth // STEPS
    half = outs[0].shape[2]
    copies = []
    for k in range(STEPS):
        at = slice(k * step, (k + 1) * step)
        copies.append(pltpu.make_async_copy(w_ref.at[at, :], w_buf.at[at, :], sems.at[2 * k]))
        copies.append(pltpu.make_async_copy(x_ref.at[:, at], x_buf.at[:, at], sems.at[2 * k + 1]))
    sides = ((dec_ref, 1 - p_ref[2]), (tgt_ref, p_ref[2]), (tgt_ref, 1 - p_ref[2]))
    for i, ((src, side), to) in enumerate(zip(sides, outs)):
        at = pl.ds(pl.multiple_of(side * half, half), half)
        copies.append(pltpu.make_async_copy(src.at[:, :, at], to, sems.at[2 * STEPS + i]))
    for copy in copies:
        copy.start()
    for k in range(STEPS):
        copies[2 * k].wait()
        copies[2 * k + 1].wait()
        at = slice(k * step, (k + 1) * step)
        part = jnp.dot(x_buf[:, at], w_buf[at, :], preferred_element_type=F32)
        if k == 0:
            acc[...] = part
        else:
            acc[...] += part
    n = a_ref.shape[0]
    a_ref[...] = acc[:n, :].astype(BF)
    b_ref[...] = acc[n:, :].astype(BF)
    for copy in copies[2 * STEPS :]:
        copy.wait()


def pre_call(place, x, w, dec, target):
    rows, depth = x.shape
    lats = w.shape[1]
    targets, few, wide = target.shape
    outs = [jax.ShapeDtypeStruct((rows // 2, lats), BF)] * 2
    outs += [jax.ShapeDtypeStruct((targets, lats, wide // 2), BF)]
    outs += [jax.ShapeDtypeStruct((targets, few, wide // 2), BF)] * 2
    return call(
        pre_kernel,
        "pre",
        (1,),
        [pl.BlockSpec(memory_space=pl.ANY)] * 4,
        [pl.BlockSpec(o.shape, lambda i, p, n=len(o.shape): (0,) * n) for o in outs],
        outs,
        (x, w, dec, target),
        2 * rows * depth * lats,
        2 * (rows + lats) * depth,
        [
            pltpu.VMEM((rows, depth), BF),
            pltpu.VMEM((depth, lats), BF),
            pltpu.VMEM((rows, lats), F32),
            pltpu.SemaphoreType.DMA((2 * STEPS + 3,)),
        ],
        core=place,
        limit=PRE_LIMIT,
    )


def total_kernel(own_ref, got_ref, err_ref, sum_ref, low_ref, same_ref):
    total = own_ref[...] + got_ref[...].astype(F32)
    sum_ref[...] = total
    low_ref[...] = total.astype(BF)


def total_call(own, got, err):
    whole = pl.BlockSpec(own.shape, lambda i: (0, 0))
    return call(
        total_kernel,
        "total",
        (1,),
        [whole, whole, pl.BlockSpec(memory_space=pl.ANY)],
        [whole, whole, pl.BlockSpec(memory_space=pl.ANY)],
        [
            jax.ShapeDtypeStruct(own.shape, F32),
            jax.ShapeDtypeStruct(own.shape, BF),
            jax.ShapeDtypeStruct(err.shape, BF),
        ],
        (own, got, err),
        own.size,
        12 * own.size,
        aliases={2: 2},
    )


def latent_kernel(near_a, far_a, near_b, far_b, active_ref, bias_ref, after_ref, out_ref):
    rows = near_a.shape[0]
    for r, (near, far) in enumerate(((near_a, far_a), (near_b, far_b))):
        at = slice(r * rows, (r + 1) * rows)
        total = near[...] + far[...].astype(F32) + bias_ref[...]
        out_ref[at, :] = jnp.where(active_ref[at, :] > 0, total, 0.0).astype(BF)


def latent_call(top, bottom, active, bias, after):
    rows, lats = active.shape
    part = pl.BlockSpec((rows // 2, lats), lambda i: (0, 0))
    whole = pl.BlockSpec((rows, lats), lambda i: (0, 0))
    return call(
        latent_kernel,
        "latents",
        (1,),
        [part] * 4
        + [whole, pl.BlockSpec((1, lats), lambda i: (0, 0)), pl.BlockSpec(memory_space=pl.ANY)],
        whole,
        jax.ShapeDtypeStruct((rows, lats), BF),
        (*top, *bottom, active, bias.reshape(1, lats), after),
        4 * rows * lats,
        4e6,
    )


def pick_kernel(p_ref, dec_ref, after_ref, out_ref, done_ref):
    out_ref[...] = dec_ref[...]
    done_ref[...] = jnp.zeros(done_ref.shape, F32)


def pick_call(place, dec, after):
    targets, lats, wide = dec.shape
    half = wide // 2
    return call(
        pick_kernel,
        "pick_half",
        (targets,),
        [
            pl.BlockSpec((1, lats, half), lambda t, p: (t, 0, p[2])),
            pl.BlockSpec(memory_space=pl.ANY),
        ],
        [
            pl.BlockSpec((1, lats, half), lambda t, p: (t, 0, 0)),
            pl.BlockSpec((8, 128), lambda t, p: (0, 0)),
        ],
        [
            jax.ShapeDtypeStruct((targets, lats, half), BF),
            jax.ShapeDtypeStruct((8, 128), F32),
        ],
        (dec, after),
        0,
        4 * targets * lats * half,
        core=place,
    )


def place_of(p_ref, far, near):
    return jnp.where(p_ref[2] == 0, far * SIDE + near, near * SIDE + far)


def rebuild_kernel(p_ref, lat_ref, sib_ref, dec_ref, got_ref, *refs):
    outs, held = refs[:-1], refs[-1]
    total = jnp.dot(lat_ref[...], dec_ref[0], preferred_element_type=F32)
    total += jnp.dot(sib_ref[...], got_ref[0], preferred_element_type=F32)
    held[...] = total.reshape(held.shape)
    q = held.shape[2] // 2
    for ref, (step, lo, hi) in zip(outs, CUTS):
        to = lax.rem(p_ref[3] + step, SIDE)
        for i in range(SIDE):
            block = held[place_of(p_ref, to, i)]
            ref[i, 0] = block[:, lo * q : hi * q].astype(ref.dtype)


CUTS = ((2, 0, 1), (2, 1, 2), (1, 0, 1), (1, 1, 2), (3, 0, 1), (3, 1, 2), (0, 0, 2))
KINDS = (BF, BF, F32, BF, BF, F32, F32)


def rebuild_call(place, lat, sib, dec, got):
    rows, lats = lat.shape
    targets, _, half = got.shape
    piece = rows // (SIDE * SIDE)
    widths = [(hi - lo) * half // 2 for _, lo, hi in CUTS]
    whole = pl.BlockSpec((rows, lats), lambda t, p: (0, 0))
    return call(
        rebuild_kernel,
        "rebuild",
        (targets,),
        [
            whole,
            whole,
            pl.BlockSpec((1, lats, half), lambda t, p: (t, 0, 0)),
            pl.BlockSpec((1, lats, half), lambda t, p: (t, 0, 0)),
        ],
        [pl.BlockSpec((SIDE, 1, piece, w), lambda t, p: (0, t, 0, 0)) for w in widths],
        [
            jax.ShapeDtypeStruct((SIDE, targets, piece, w), kind)
            for w, kind in zip(widths, KINDS)
        ],
        (lat, sib, dec, got),
        4 * rows * lats * half * targets,
        11e6,
        [pltpu.VMEM((SIDE * SIDE, piece, half), F32)],
        core=place,
    )


def sum_kernel(p_ref, own_ref, *refs):
    parts, outs, held = refs[:4], refs[4:-1], refs[-1]
    q = held.shape[2] // 2
    for h in range(2):
        cols = slice(h * q, (h + 1) * q)
        total = own_ref[:, 0, :, cols]
        for part in parts[2 * h : 2 * h + 2]:
            total += part[:, 0].astype(F32)
        held[:, :, cols] = total
    for k in range(SIDE):
        outs[k][0] = held[lax.rem(p_ref[4] + k, SIDE)].astype(outs[k].dtype)


def sum_call(place, own, parts):
    _, targets, piece, half = own.shape
    block = pl.BlockSpec((SIDE, 1, piece, half // 2), lambda t, p: (0, t, 0, 0))
    return call(
        sum_kernel,
        "sum_first",
        (targets,),
        [pl.BlockSpec((SIDE, 1, piece, half), lambda t, p: (0, t, 0, 0))] + [block] * 4,
        [pl.BlockSpec((1, piece, half), lambda t, p: (t, 0, 0))] * SIDE,
        [jax.ShapeDtypeStruct((targets, piece, half), F32 if k == 0 else BF) for k in range(SIDE)],
        (own, *parts),
        4 * own.size,
        12 * own.size,
        [pltpu.VMEM((SIDE, piece, half), F32)],
        core=place,
    )


def error_kernel(scale, p_ref, own_ref, got_ref, *refs):
    parts, out, goal = refs[:SIDE], refs[SIDE], refs[SIDE + 1]
    few = own_ref.shape[1]
    for ref, side in ((own_ref, p_ref[2]), (got_ref, 1 - p_ref[2])):
        goal[pl.ds(pl.multiple_of(side * few, few), few), :] = ref[0].astype(F32)
    total = parts[0][0]
    for part in parts[1:]:
        total += part[0].astype(F32)
    out[0] = ((total - goal[...]) * scale).astype(BF)


def error_call(scale, place, own, got, parts):
    targets, piece, half = parts[0].shape
    one = pl.BlockSpec((1, piece, half), lambda t, p: (t, 0, 0))
    goal = pl.BlockSpec((1,) + own.shape[1:], lambda t, p: (t, 0, 0))
    return call(
        functools.partial(error_kernel, scale),
        "error",
        (targets,),
        [goal, goal] + [one] * SIDE,
        one,
        jax.ShapeDtypeStruct((targets, piece, half), BF),
        (own, got, *parts),
        8 * targets * piece * half,
        2e6,
        [pltpu.VMEM((piece, half), F32)],
        core=place,
    )


def join_kernel(p_ref, *refs):
    parts, outs = refs[:SIDE], refs[SIDE:]
    q = outs[0].shape[3]
    for k in range(SIDE):
        at = lax.rem(p_ref[4] + SIDE - k, SIDE)
        for h in range(2):
            outs[h][at, 0] = parts[k][0, :, h * q : (h + 1) * q]


def join_call(place, parts):
    targets, piece, half = parts[0].shape
    return call(
        join_kernel,
        "join",
        (targets,),
        [pl.BlockSpec((1, piece, half), lambda t, p: (t, 0, 0))] * SIDE,
        [pl.BlockSpec((SIDE, 1, piece, half // 2), lambda t, p: (0, t, 0, 0))] * 2,
        [jax.ShapeDtypeStruct((SIDE, targets, piece, half // 2), BF)] * 2,
        tuple(parts),
        0,
        8 * parts[0].size,
        core=place,
    )


def back_dot(err, dec_ref, out_ref, acc):
    t = pl.program_id(0)
    part = dot(err, dec_ref[0], 1, 1)

    @pl.when(t == 0)
    def _():
        acc[...] = part

    @pl.when(t > 0)
    def _():
        acc[...] += part

    @pl.when(t == pl.num_programs(0) - 1)
    def _():
        out_ref[...] = acc[...].astype(out_ref.dtype)


def back_sib_kernel(p_ref, dec_ref, after_ref, *refs):
    parts, (err_ref, out_ref, acc) = refs[: 2 * SIDE], refs[2 * SIDE :]
    piece, q = parts[0].shape[2:]
    for k in range(SIDE):
        far = lax.rem(p_ref[3] + SIDE - k, SIDE)
        for i in range(SIDE):
            at = pl.ds(pl.multiple_of(place_of(p_ref, far, i) * piece, piece), piece)
            for h in range(2):
                err_ref[0, at, h * q : (h + 1) * q] = parts[2 * k + h][i, 0]
    back_dot(err_ref[0], dec_ref, out_ref, acc)


def back_sib_call(place, parts, dec, after):
    _, targets, piece, q = parts[0].shape
    lats, half = dec.shape[1:]
    rows = SIDE * SIDE * piece
    return call(
        back_sib_kernel,
        "back_sib",
        (targets,),
        [
            pl.BlockSpec((1, lats, half), lambda t, p: (t, 0, 0)),
            pl.BlockSpec(memory_space=pl.ANY),
        ]
        + [pl.BlockSpec((SIDE, 1, piece, q), lambda t, p: (0, t, 0, 0))] * (2 * SIDE),
        [
            pl.BlockSpec((1, rows, half), lambda t, p: (t, 0, 0)),
            pl.BlockSpec((rows, lats), lambda t, p: (0, 0)),
        ],
        [
            jax.ShapeDtypeStruct((targets, rows, half), BF),
            jax.ShapeDtypeStruct((rows, lats), BF),
        ],
        (dec, after, *parts),
        2 * rows * lats * half * targets,
        10e6,
        [pltpu.VMEM((rows, lats), F32)],
        core=place,
    )


def back_own_kernel(p_ref, err_ref, dec_ref, out_ref, acc):
    back_dot(err_ref[0], dec_ref, out_ref, acc)


def back_own_call(place, err, dec):
    targets, rows, half = err.shape
    lats = dec.shape[1]
    return call(
        back_own_kernel,
        "back_own",
        (targets,),
        [
            pl.BlockSpec((1, rows, half), lambda t, p: (t, 0, 0)),
            pl.BlockSpec((1, lats, half), lambda t, p: (t, 0, 0)),
        ],
        pl.BlockSpec((rows, lats), lambda t, p: (0, 0)),
        jax.ShapeDtypeStruct((rows, lats), F32),
        (err, dec),
        2 * rows * lats * half * targets,
        7e6,
        [pltpu.VMEM((rows, lats), F32)],
        core=place,
    )


def turn_kernel(x_ref, lat_ref, after_ref, x_out, lat_out, done_ref):
    done_ref[...] = jnp.zeros(done_ref.shape, F32)
    x_out[...] = x_ref[...].T

    @pl.when(pl.program_id(0) == 0)
    def _():
        lat_out[...] = lat_ref[...].T


def turn_call(x, lat, after):
    rows, depth = x.shape
    lats = lat.shape[1]
    step = 512
    whole = pl.BlockSpec((rows, lats), lambda i: (0, 0))
    turned = pl.BlockSpec((lats, rows), lambda i: (0, 0))
    return call(
        turn_kernel,
        "turn",
        (depth // step,),
        [
            pl.BlockSpec((rows, step), lambda i: (0, i)),
            whole,
            pl.BlockSpec(memory_space=pl.ANY),
        ],
        [
            pl.BlockSpec((step, rows), lambda i: (i, 0)),
            turned,
            pl.BlockSpec((8, 128), lambda i: (0, 0)),
        ],
        [jax.ShapeDtypeStruct((depth, rows), BF)]
        + [jax.ShapeDtypeStruct((lats, rows), BF)]
        + [jax.ShapeDtypeStruct((8, 128), F32)],
        (x, lat, after),
        0,
        6e6,
    )


def dec_kernel(p_ref, lat_ref, err_ref, got_ref, out_ref, done_ref):
    j = pl.program_id(1)
    done_ref[...] = jnp.zeros(done_ref.shape, F32)

    @pl.when(j == 0)
    def _():
        out_ref[0] = dot(lat_ref[...], err_ref[0], 1, 0).astype(BF)

    @pl.when(j == 1)
    def _():
        out_ref[0] = dot(lat_ref[...], got_ref[0], 1, 0).astype(BF)


def dec_call(place, lat, err, got):
    targets, rows, half = err.shape
    lats = lat.shape[0]
    return call(
        dec_kernel,
        "dec_grad",
        (targets, 2),
        [
            pl.BlockSpec((lats, rows), lambda t, j, p: (0, 0)),
            pl.BlockSpec((1, rows, half), lambda t, j, p: (t, 0, 0)),
            pl.BlockSpec((1, rows, half), lambda t, j, p: (t, 0, 0)),
        ],
        [
            pl.BlockSpec((1, lats, half), lambda t, j, p: (t, 0, (j + p[2]) % 2)),
            pl.BlockSpec((8, 128), lambda t, j, p: (0, 0)),
        ],
        [
            jax.ShapeDtypeStruct((targets, lats, 2 * half), BF),
            jax.ShapeDtypeStruct((8, 128), F32),
        ],
        (lat, err, got),
        4 * rows * lats * half * targets,
        13e6,
        core=place,
    )


def enc_kernel(x_ref, active_ref, after_ref, sum_ref, got_ref, enc_ref, bias_ref, grad):
    @pl.when(pl.program_id(0) == 0)
    def _():
        total = sum_ref[...] + got_ref[...].astype(F32)
        kept = jnp.where(active_ref[...] > 0, total, 0.0).astype(BF)
        grad[...] = kept
        bias_ref[...] = jnp.sum(kept.astype(F32), axis=0, keepdims=True)

    enc_ref[...] = dot(x_ref[...], grad[...], 1, 0).astype(BF)


def enc_call(x, active, after, sums, got):
    depth, rows = x.shape
    lats = active.shape[1]
    step = 512
    whole = pl.BlockSpec((rows, lats), lambda i: (0, 0))
    return call(
        enc_kernel,
        "enc_grad",
        (depth // step,),
        [
            pl.BlockSpec((step, rows), lambda i: (i, 0)),
            whole,
            pl.BlockSpec(memory_space=pl.ANY),
            whole,
            whole,
        ],
        [
            pl.BlockSpec((step, lats), lambda i: (i, 0)),
            pl.BlockSpec((1, lats), lambda i: (0, 0)),
        ],
        [jax.ShapeDtypeStruct((depth, lats), BF), jax.ShapeDtypeStruct((1, lats), F32)],
        (x, active, after, sums, got),
        2 * rows * depth * lats,
        7e6,
        [pltpu.VMEM((rows, lats), BF)],
    )


def swap(value):
    return lax.ppermute(value, "c", [(0, 1), (1, 0)])


EVEN = (1, 0, 3, 2)
ODD = (3, 2, 1, 0)


def pair(value, tables):
    moves = [(z * 2 + c, tables[c][z] * 2 + c) for z in range(SIDE) for c in range(2)]
    return lax.ppermute(value, ("z", "c"), moves)


def z_sum(part, low):
    first = part.astype(F32) + pair(low, (EVEN, ODD)).astype(F32)
    return first, pair(first.astype(BF), (ODD, EVEN))


def shift(value, second, step):
    moves = []
    for x in range(SIDE):
        for y in range(SIDE):
            for c in range(2):
                along_x = (c == 0) != second
                to = ((x + step) % SIDE, y) if along_x else (x, (y + step) % SIDE)
                moves.append(((x * SIDE + y) * 2 + c, (to[0] * SIDE + to[1]) * 2 + c))
    return lax.ppermute(value, ("x", "y", "c"), moves)


def plus(a, b):
    return (a + b.astype(F32)).astype(BF)


def ring_sum(cuts):
    far_a, far_b, up_a, up_b, down_a, down_b, own = cuts
    met_a, met_b = shift(far_a, False, 1), shift(far_b, False, 3)
    from_b, from_a = shift(up_b, False, 1), shift(down_a, False, 3)
    ring_a = shift(plus(up_a, met_a), False, 1)
    ring_b = shift(plus(down_b, met_b), False, 3)
    return own, (ring_a, from_a, from_b, ring_b)


def ring_gather(a, b):
    below_a, above_b = shift(a, False, 1), shift(b, False, 3)
    below_b, above_a = shift(b, False, 1), shift(a, False, 3)
    far_a, far_b = shift(below_a, False, 1), shift(above_b, False, 3)
    return a, b, below_a, below_b, far_a, far_b, above_a, above_b


def scatter(parts):
    return [parts[0]] + [shift(parts[k], True, k) for k in (1, 2, 3)]


def spread(value):
    return [value] + [shift(value, True, k) for k in (1, 2, 3)]


def per_device(mlp_inputs, enc_weight, enc_bias, active, dec_weight, target):
    rows = mlp_inputs.shape[0]
    x, y, c = (lax.axis_index(a) for a in "xyc")
    first, second = jnp.where(c == 0, x, y), jnp.where(c == 0, y, x)
    place = jnp.stack([x, y, c, first, second]).astype(jnp.int32)
    scale = 1.0 / math.sqrt(rows)

    top, bottom, dec_sent, tgt_own, tgt_sent = pre_call(
        place, mlp_inputs, enc_weight, dec_weight, target
    )
    top, bottom = z_sum(top, top), z_sum(bottom, bottom)
    dec_got = swap(dec_sent)
    tgt_got = swap(tgt_sent)
    dec_own, done = pick_call(place, dec_weight, bottom[0])
    lat = latent_call(top, bottom, active, enc_bias, done)
    lat_sib = swap(lat)

    own, parts = ring_sum(rebuild_call(place, lat, lat_sib, dec_own, dec_got))
    parts = scatter(sum_call(place, own, parts))
    err = error_call(scale, place, tgt_own, tgt_got, parts)
    parts = ring_gather(*join_call(place, spread(err)))
    x_turned, lat_turned, done = turn_call(mlp_inputs, lat, parts[2])

    err, grad_got = back_sib_call(place, parts, dec_got, done)
    grad_got = swap(grad_got)
    grad, low, err = total_call(back_own_call(place, err, dec_own), grad_got, err)
    near, far = z_sum(grad, low)
    dec_grad, done = dec_call(place, lat_turned, err, swap(err))
    enc_grad, bias_grad = enc_call(x_turned, active, done, near, far)
    return enc_grad, bias_grad.reshape(-1), dec_grad


def solution(mesh):
    grid = Mesh(mesh.devices.reshape(4, 4, 4, 2), ("z", "x", "y", "c"))
    lat = ("x", "y", "c")
    in_specs = (
        P(None, "z"),
        P("z", lat),
        P(lat),
        P(None, lat),
        P(None, lat, "z"),
        P(None, lat, "z"),
    )
    out_specs = (P("z", lat), P(lat), P(None, lat, "z"))
    return jax.shard_map(
        per_device, mesh=grid, in_specs=in_specs, out_specs=out_specs, check_vma=False
    )
```

```python
import functools
import math

import jax
import jax.numpy as jnp
from jax import lax
from jax.experimental import pallas as pl
from jax.experimental.pallas import tpu as pltpu
from jax.sharding import Mesh, PartitionSpec as P

BF = jnp.bfloat16
F32 = jnp.float32
VMEM_LIMIT = 16 * 1024 * 1024
PRE_LIMIT = 52 * 1024 * 1024
SIDE = 4


def dot(a, b, ca, cb):
    return lax.dot_general(a, b, (((ca,), (cb,)), ((), ())), preferred_element_type=F32)


def call(body, name, grid, ins, outs, shapes, args, flops, moved, scratch=(), core=None, limit=VMEM_LIMIT, aliases=None):
    spec = dict(grid=grid, in_specs=ins, out_specs=outs, scratch_shapes=list(scratch))
    if core is not None:
        spec = dict(grid_spec=pltpu.PrefetchScalarGridSpec(num_scalar_prefetch=1, **spec))
        args = (core,) + tuple(args)
    return pl.pallas_call(
        body,
        out_shape=shapes,
        compiler_params=pltpu.CompilerParams(
            dimension_semantics=("arbitrary",) * len(grid), vmem_limit_bytes=limit
        ),
        cost_estimate=pl.CostEstimate(
            flops=int(flops), bytes_accessed=int(moved), transcendentals=0
        ),
        name=name,
        input_output_aliases=aliases or {},
        **spec,
    )(*args)


STEPS = 4


def pre_kernel(p_ref, x_ref, w_ref, dec_ref, tgt_ref, a_ref, b_ref, *refs):
    outs, (x_buf, w_buf, acc, sems) = refs[:3], refs[3:]
    depth = x_ref.shape[1]
    step = depth // STEPS
    half = outs[0].shape[2]
    copies = []
    for k in range(STEPS):
        at = slice(k * step, (k + 1) * step)
        copies.append(pltpu.make_async_copy(w_ref.at[at, :], w_buf.at[at, :], sems.at[2 * k]))
        copies.append(pltpu.make_async_copy(x_ref.at[:, at], x_buf.at[:, at], sems.at[2 * k + 1]))
    sides = ((dec_ref, 1 - p_ref[2]), (tgt_ref, p_ref[2]), (tgt_ref, 1 - p_ref[2]))
    for i, ((src, side), to) in enumerate(zip(sides, outs)):
        at = pl.ds(pl.multiple_of(side * half, half), half)
        copies.append(pltpu.make_async_copy(src.at[:, :, at], to, sems.at[2 * STEPS + i]))
    for copy in copies:
        copy.start()
    for k in range(STEPS):
        copies[2 * k].wait()
        copies[2 * k + 1].wait()
        at = slice(k * step, (k + 1) * step)
        part = jnp.dot(x_buf[:, at], w_buf[at, :], preferred_element_type=F32)
        if k == 0:
            acc[...] = part
        else:
            acc[...] += part
    n = a_ref.shape[0]
    a_ref[...] = acc[:n, :].astype(BF)
    b_ref[...] = acc[n:, :].astype(BF)
    for copy in copies[2 * STEPS :]:
        copy.wait()


def pre_call(place, x, w, dec, target):
    rows, depth = x.shape
    lats = w.shape[1]
    targets, few, wide = target.shape
    part = pl.BlockSpec((rows // 2, lats), lambda i, p: (0, 0))
    outs = [pltpu.VMEM((rows // 2, lats), BF)] * 2
    outs += [pltpu.VMEM((targets, lats, wide // 2), BF)]
    outs += [pltpu.VMEM((targets, few, wide // 2), BF)] * 2
    return call(
        pre_kernel,
        "pre",
        (1,),
        [pl.BlockSpec(memory_space=pl.ANY)] * 4,
        [part, part] + [pl.BlockSpec(memory_space=pl.ANY)] * 3,
        outs,
        (x, w, dec, target),
        2 * rows * depth * lats,
        2 * (rows + lats) * depth,
        [
            pltpu.VMEM((rows, depth), BF),
            pltpu.VMEM((depth, lats), BF),
            pltpu.VMEM((rows, lats), F32),
            pltpu.SemaphoreType.DMA((2 * STEPS + 3,)),
        ],
        core=place,
        limit=PRE_LIMIT,
    )


def total_kernel(own_ref, got_ref, err_ref, sum_ref, low_ref, same_ref):
    total = own_ref[...] + got_ref[...].astype(F32)
    sum_ref[...] = total
    low_ref[...] = total.astype(BF)


def total_call(own, got, err):
    whole = pl.BlockSpec(own.shape, lambda i: (0, 0))
    return call(
        total_kernel,
        "total",
        (1,),
        [whole, whole, pl.BlockSpec(memory_space=pl.ANY)],
        [whole, whole, pl.BlockSpec(memory_space=pl.ANY)],
        [
            jax.ShapeDtypeStruct(own.shape, F32),
            jax.ShapeDtypeStruct(own.shape, BF),
            jax.ShapeDtypeStruct(err.shape, BF),
        ],
        (own, got, err),
        own.size,
        12 * own.size,
        aliases={2: 2},
    )


def latent_kernel(near_a, far_a, near_b, far_b, active_ref, bias_ref, after_ref, out_ref):
    rows = near_a.shape[0]
    for r, (near, far) in enumerate(((near_a, far_a), (near_b, far_b))):
        at = slice(r * rows, (r + 1) * rows)
        total = near[...] + far[...].astype(F32) + bias_ref[...]
        out_ref[at, :] = jnp.where(active_ref[at, :] > 0, total, 0.0).astype(BF)


def latent_call(top, bottom, active, bias, after):
    rows, lats = active.shape
    part = pl.BlockSpec((rows // 2, lats), lambda i: (0, 0))
    whole = pl.BlockSpec((rows, lats), lambda i: (0, 0))
    return call(
        latent_kernel,
        "latents",
        (1,),
        [part] * 4
        + [whole, pl.BlockSpec((1, lats), lambda i: (0, 0)), pl.BlockSpec(memory_space=pl.ANY)],
        whole,
        jax.ShapeDtypeStruct((rows, lats), BF),
        (*top, *bottom, active, bias.reshape(1, lats), after),
        4 * rows * lats,
        4e6,
    )


def pick_kernel(p_ref, dec_ref, after_ref, out_ref, done_ref):
    out_ref[...] = dec_ref[...]
    done_ref[...] = jnp.zeros(done_ref.shape, F32)


def pick_call(place, dec, after):
    targets, lats, wide = dec.shape
    half = wide // 2
    return call(
        pick_kernel,
        "pick_half",
        (targets,),
        [
            pl.BlockSpec((1, lats, half), lambda t, p: (t, 0, p[2])),
            pl.BlockSpec(memory_space=pl.ANY),
        ],
        [
            pl.BlockSpec((1, lats, half), lambda t, p: (t, 0, 0)),
            pl.BlockSpec((8, 128), lambda t, p: (0, 0)),
        ],
        [
            jax.ShapeDtypeStruct((targets, lats, half), BF),
            jax.ShapeDtypeStruct((8, 128), F32),
        ],
        (dec, after),
        0,
        4 * targets * lats * half,
        core=place,
    )


def place_of(p_ref, far, near):
    return jnp.where(p_ref[2] == 0, far * SIDE + near, near * SIDE + far)


def rebuild_kernel(p_ref, lat_ref, sib_ref, dec_ref, got_ref, *refs):
    outs, held = refs[:-1], refs[-1]
    total = jnp.dot(lat_ref[...], dec_ref[0], preferred_element_type=F32)
    total += jnp.dot(sib_ref[...], got_ref[0], preferred_element_type=F32)
    held[...] = total.reshape(held.shape)
    q = held.shape[2] // 2
    for ref, (step, lo, hi) in zip(outs, CUTS):
        to = lax.rem(p_ref[3] + step, SIDE)
        for i in range(SIDE):
            block = held[place_of(p_ref, to, i)]
            ref[i, 0] = block[:, lo * q : hi * q].astype(ref.dtype)


CUTS = ((2, 0, 1), (2, 1, 2), (1, 0, 1), (1, 1, 2), (3, 0, 1), (3, 1, 2), (0, 0, 2))
KINDS = (BF, BF, F32, BF, BF, F32, F32)


def rebuild_call(place, lat, sib, dec, got):
    rows, lats = lat.shape
    targets, _, half = got.shape
    piece = rows // (SIDE * SIDE)
    widths = [(hi - lo) * half // 2 for _, lo, hi in CUTS]
    whole = pl.BlockSpec((rows, lats), lambda t, p: (0, 0))
    return call(
        rebuild_kernel,
        "rebuild",
        (targets,),
        [
            whole,
            whole,
            pl.BlockSpec((1, lats, half), lambda t, p: (t, 0, 0)),
            pl.BlockSpec((1, lats, half), lambda t, p: (t, 0, 0)),
        ],
        [pl.BlockSpec((SIDE, 1, piece, w), lambda t, p: (0, t, 0, 0)) for w in widths],
        [
            jax.ShapeDtypeStruct((SIDE, targets, piece, w), kind)
            for w, kind in zip(widths, KINDS)
        ],
        (lat, sib, dec, got),
        4 * rows * lats * half * targets,
        11e6,
        [pltpu.VMEM((SIDE * SIDE, piece, half), F32)],
        core=place,
    )


def sum_kernel(p_ref, own_ref, *refs):
    parts, outs, held = refs[:4], refs[4:-1], refs[-1]
    q = held.shape[2] // 2
    for h in range(2):
        cols = slice(h * q, (h + 1) * q)
        total = own_ref[:, 0, :, cols]
        for part in parts[2 * h : 2 * h + 2]:
            total += part[:, 0].astype(F32)
        held[:, :, cols] = total
    for k in range(SIDE):
        outs[k][0] = held[lax.rem(p_ref[4] + k, SIDE)].astype(outs[k].dtype)


def sum_call(place, own, parts):
    _, targets, piece, half = own.shape
    block = pl.BlockSpec((SIDE, 1, piece, half // 2), lambda t, p: (0, t, 0, 0))
    return call(
        sum_kernel,
        "sum_first",
        (targets,),
        [pl.BlockSpec((SIDE, 1, piece, half), lambda t, p: (0, t, 0, 0))] + [block] * 4,
        [pl.BlockSpec((1, piece, half), lambda t, p: (t, 0, 0))] * SIDE,
        [jax.ShapeDtypeStruct((targets, piece, half), F32 if k == 0 else BF) for k in range(SIDE)],
        (own, *parts),
        4 * own.size,
        12 * own.size,
        [pltpu.VMEM((SIDE, piece, half), F32)],
        core=place,
    )


def error_kernel(scale, p_ref, own_ref, got_ref, *refs):
    parts, out, goal = refs[:SIDE], refs[SIDE], refs[SIDE + 1]
    few = own_ref.shape[1]
    for ref, side in ((own_ref, p_ref[2]), (got_ref, 1 - p_ref[2])):
        goal[pl.ds(pl.multiple_of(side * few, few), few), :] = ref[0].astype(F32)
    total = parts[0][0]
    for part in parts[1:]:
        total += part[0].astype(F32)
    out[0] = ((total - goal[...]) * scale).astype(BF)


def error_call(scale, place, own, got, parts):
    targets, piece, half = parts[0].shape
    one = pl.BlockSpec((1, piece, half), lambda t, p: (t, 0, 0))
    goal = pl.BlockSpec((1,) + own.shape[1:], lambda t, p: (t, 0, 0))
    return call(
        functools.partial(error_kernel, scale),
        "error",
        (targets,),
        [goal, goal] + [one] * SIDE,
        one,
        jax.ShapeDtypeStruct((targets, piece, half), BF),
        (own, got, *parts),
        8 * targets * piece * half,
        2e6,
        [pltpu.VMEM((piece, half), F32)],
        core=place,
    )


def join_kernel(p_ref, *refs):
    parts, outs = refs[:SIDE], refs[SIDE:]
    q = outs[0].shape[3]
    for k in range(SIDE):
        at = lax.rem(p_ref[4] + SIDE - k, SIDE)
        for h in range(2):
            outs[h][at, 0] = parts[k][0, :, h * q : (h + 1) * q]


def join_call(place, parts):
    targets, piece, half = parts[0].shape
    return call(
        join_kernel,
        "join",
        (targets,),
        [pl.BlockSpec((1, piece, half), lambda t, p: (t, 0, 0))] * SIDE,
        [pl.BlockSpec((SIDE, 1, piece, half // 2), lambda t, p: (0, t, 0, 0))] * 2,
        [jax.ShapeDtypeStruct((SIDE, targets, piece, half // 2), BF)] * 2,
        tuple(parts),
        0,
        8 * parts[0].size,
        core=place,
    )


def back_dot(err, dec_ref, out_ref, acc):
    t = pl.program_id(0)
    part = dot(err, dec_ref[0], 1, 1)

    @pl.when(t == 0)
    def _():
        acc[...] = part

    @pl.when(t > 0)
    def _():
        acc[...] += part

    @pl.when(t == pl.num_programs(0) - 1)
    def _():
        out_ref[...] = acc[...].astype(out_ref.dtype)


def back_sib_kernel(p_ref, dec_ref, after_ref, *refs):
    parts, (err_ref, out_ref, acc) = refs[: 2 * SIDE], refs[2 * SIDE :]
    piece, q = parts[0].shape[2:]
    for k in range(SIDE):
        far = lax.rem(p_ref[3] + SIDE - k, SIDE)
        for i in range(SIDE):
            at = pl.ds(pl.multiple_of(place_of(p_ref, far, i) * piece, piece), piece)
            for h in range(2):
                err_ref[0, at, h * q : (h + 1) * q] = parts[2 * k + h][i, 0]
    back_dot(err_ref[0], dec_ref, out_ref, acc)


def back_sib_call(place, parts, dec, after):
    _, targets, piece, q = parts[0].shape
    lats, half = dec.shape[1:]
    rows = SIDE * SIDE * piece
    return call(
        back_sib_kernel,
        "back_sib",
        (targets,),
        [
            pl.BlockSpec((1, lats, half), lambda t, p: (t, 0, 0)),
            pl.BlockSpec(memory_space=pl.ANY),
        ]
        + [pl.BlockSpec((SIDE, 1, piece, q), lambda t, p: (0, t, 0, 0))] * (2 * SIDE),
        [
            pl.BlockSpec((1, rows, half), lambda t, p: (t, 0, 0)),
            pl.BlockSpec((rows, lats), lambda t, p: (0, 0)),
        ],
        [
            jax.ShapeDtypeStruct((targets, rows, half), BF),
            jax.ShapeDtypeStruct((rows, lats), BF),
        ],
        (dec, after, *parts),
        2 * rows * lats * half * targets,
        10e6,
        [pltpu.VMEM((rows, lats), F32)],
        core=place,
    )


def back_own_kernel(p_ref, err_ref, dec_ref, out_ref, acc):
    back_dot(err_ref[0], dec_ref, out_ref, acc)


def back_own_call(place, err, dec):
    targets, rows, half = err.shape
    lats = dec.shape[1]
    return call(
        back_own_kernel,
        "back_own",
        (targets,),
        [
            pl.BlockSpec((1, rows, half), lambda t, p: (t, 0, 0)),
            pl.BlockSpec((1, lats, half), lambda t, p: (t, 0, 0)),
        ],
        pl.BlockSpec((rows, lats), lambda t, p: (0, 0)),
        jax.ShapeDtypeStruct((rows, lats), F32),
        (err, dec),
        2 * rows * lats * half * targets,
        7e6,
        [pltpu.VMEM((rows, lats), F32)],
        core=place,
    )


def turn_kernel(x_ref, lat_ref, after_ref, x_out, lat_out, done_ref):
    done_ref[...] = jnp.zeros(done_ref.shape, F32)
    x_out[...] = x_ref[...].T

    @pl.when(pl.program_id(0) == 0)
    def _():
        lat_out[...] = lat_ref[...].T


def turn_call(x, lat, after):
    rows, depth = x.shape
    lats = lat.shape[1]
    step = 512
    whole = pl.BlockSpec((rows, lats), lambda i: (0, 0))
    turned = pl.BlockSpec((lats, rows), lambda i: (0, 0))
    return call(
        turn_kernel,
        "turn",
        (depth // step,),
        [
            pl.BlockSpec((rows, step), lambda i: (0, i)),
            whole,
            pl.BlockSpec(memory_space=pl.ANY),
        ],
        [
            pl.BlockSpec((step, rows), lambda i: (i, 0)),
            turned,
            pl.BlockSpec((8, 128), lambda i: (0, 0)),
        ],
        [jax.ShapeDtypeStruct((depth, rows), BF)]
        + [jax.ShapeDtypeStruct((lats, rows), BF)]
        + [jax.ShapeDtypeStruct((8, 128), F32)],
        (x, lat, after),
        0,
        6e6,
    )


def dec_kernel(p_ref, lat_ref, err_ref, got_ref, out_ref, done_ref):
    j = pl.program_id(1)
    done_ref[...] = jnp.zeros(done_ref.shape, F32)

    @pl.when(j == 0)
    def _():
        out_ref[0] = dot(lat_ref[...], err_ref[0], 1, 0).astype(BF)

    @pl.when(j == 1)
    def _():
        out_ref[0] = dot(lat_ref[...], got_ref[0], 1, 0).astype(BF)


def dec_call(place, lat, err, got):
    targets, rows, half = err.shape
    lats = lat.shape[0]
    return call(
        dec_kernel,
        "dec_grad",
        (targets, 2),
        [
            pl.BlockSpec((lats, rows), lambda t, j, p: (0, 0)),
            pl.BlockSpec((1, rows, half), lambda t, j, p: (t, 0, 0)),
            pl.BlockSpec((1, rows, half), lambda t, j, p: (t, 0, 0)),
        ],
        [
            pl.BlockSpec((1, lats, half), lambda t, j, p: (t, 0, (j + p[2]) % 2)),
            pl.BlockSpec((8, 128), lambda t, j, p: (0, 0)),
        ],
        [
            jax.ShapeDtypeStruct((targets, lats, 2 * half), BF),
            jax.ShapeDtypeStruct((8, 128), F32),
        ],
        (lat, err, got),
        4 * rows * lats * half * targets,
        13e6,
        core=place,
    )


def enc_kernel(x_ref, active_ref, after_ref, sum_ref, got_ref, enc_ref, bias_ref, grad):
    @pl.when(pl.program_id(0) == 0)
    def _():
        total = sum_ref[...] + got_ref[...].astype(F32)
        kept = jnp.where(active_ref[...] > 0, total, 0.0).astype(BF)
        grad[...] = kept
        bias_ref[...] = jnp.sum(kept.astype(F32), axis=0, keepdims=True)

    enc_ref[...] = dot(x_ref[...], grad[...], 1, 0).astype(BF)


def enc_call(x, active, after, sums, got):
    depth, rows = x.shape
    lats = active.shape[1]
    step = 512
    whole = pl.BlockSpec((rows, lats), lambda i: (0, 0))
    return call(
        enc_kernel,
        "enc_grad",
        (depth // step,),
        [
            pl.BlockSpec((step, rows), lambda i: (i, 0)),
            whole,
            pl.BlockSpec(memory_space=pl.ANY),
            whole,
            whole,
        ],
        [
            pl.BlockSpec((step, lats), lambda i: (i, 0)),
            pl.BlockSpec((1, lats), lambda i: (0, 0)),
        ],
        [jax.ShapeDtypeStruct((depth, lats), BF), jax.ShapeDtypeStruct((1, lats), F32)],
        (x, active, after, sums, got),
        2 * rows * depth * lats,
        7e6,
        [pltpu.VMEM((rows, lats), BF)],
    )


def swap(value):
    return lax.ppermute(value, "c", [(0, 1), (1, 0)])


EVEN = (1, 0, 3, 2)
ODD = (3, 2, 1, 0)


def pair(value, tables):
    moves = [(z * 2 + c, tables[c][z] * 2 + c) for z in range(SIDE) for c in range(2)]
    return lax.ppermute(value, ("z", "c"), moves)


def z_sum(part, low):
    first = part.astype(F32) + pair(low, (EVEN, ODD)).astype(F32)
    return first, pair(first.astype(BF), (ODD, EVEN))


def shift(value, second, step):
    moves = []
    for x in range(SIDE):
        for y in range(SIDE):
            for c in range(2):
                along_x = (c == 0) != second
                to = ((x + step) % SIDE, y) if along_x else (x, (y + step) % SIDE)
                moves.append(((x * SIDE + y) * 2 + c, (to[0] * SIDE + to[1]) * 2 + c))
    return lax.ppermute(value, ("x", "y", "c"), moves)


def plus(a, b):
    return (a + b.astype(F32)).astype(BF)


def ring_sum(cuts):
    far_a, far_b, up_a, up_b, down_a, down_b, own = cuts
    met_a, met_b = shift(far_a, False, 1), shift(far_b, False, 3)
    from_b, from_a = shift(up_b, False, 1), shift(down_a, False, 3)
    ring_a = shift(plus(up_a, met_a), False, 1)
    ring_b = shift(plus(down_b, met_b), False, 3)
    return own, (ring_a, from_a, from_b, ring_b)


def ring_gather(a, b):
    below_a, above_b = shift(a, False, 1), shift(b, False, 3)
    below_b, above_a = shift(b, False, 1), shift(a, False, 3)
    far_a, far_b = shift(below_a, False, 1), shift(above_b, False, 3)
    return a, b, below_a, below_b, far_a, far_b, above_a, above_b


def scatter(parts):
    return [parts[0]] + [shift(parts[k], True, k) for k in (1, 2, 3)]


def spread(value):
    return [value] + [shift(value, True, k) for k in (1, 2, 3)]


def per_device(mlp_inputs, enc_weight, enc_bias, active, dec_weight, target):
    rows = mlp_inputs.shape[0]
    x, y, c = (lax.axis_index(a) for a in "xyc")
    first, second = jnp.where(c == 0, x, y), jnp.where(c == 0, y, x)
    place = jnp.stack([x, y, c, first, second]).astype(jnp.int32)
    scale = 1.0 / math.sqrt(rows)

    top, bottom, dec_sent, tgt_own, tgt_sent = pre_call(
        place, mlp_inputs, enc_weight, dec_weight, target
    )
    top, bottom = z_sum(top, top), z_sum(bottom, bottom)
    dec_got = swap(dec_sent)
    tgt_got = swap(tgt_sent)
    dec_own, done = pick_call(place, dec_weight, bottom[0])
    lat = latent_call(top, bottom, active, enc_bias, done)
    lat_sib = swap(lat)

    own, parts = ring_sum(rebuild_call(place, lat, lat_sib, dec_own, dec_got))
    parts = scatter(sum_call(place, own, parts))
    err = error_call(scale, place, tgt_own, tgt_got, parts)
    parts = ring_gather(*join_call(place, spread(err)))
    x_turned, lat_turned, done = turn_call(mlp_inputs, lat, parts[2])

    err, grad_got = back_sib_call(place, parts, dec_got, done)
    grad_got = swap(grad_got)
    grad, low, err = total_call(back_own_call(place, err, dec_own), grad_got, err)
    near, far = z_sum(grad, low)
    dec_grad, done = dec_call(place, lat_turned, err, swap(err))
    enc_grad, bias_grad = enc_call(x_turned, active, done, near, far)
    return enc_grad, bias_grad.reshape(-1), dec_grad


def solution(mesh):
    grid = Mesh(mesh.devices.reshape(4, 4, 4, 2), ("z", "x", "y", "c"))
    lat = ("x", "y", "c")
    in_specs = (
        P(None, "z"),
        P("z", lat),
        P(lat),
        P(None, lat),
        P(None, lat, "z"),
        P(None, lat, "z"),
    )
    out_specs = (P("z", lat), P(lat), P(None, lat, "z"))
    return jax.shard_map(
        per_device, mesh=grid, in_specs=in_specs, out_specs=out_specs, check_vma=False
    )
```

```python
import functools
import math

import jax
import jax.numpy as jnp
from jax import lax
from jax.experimental import pallas as pl
from jax.experimental.pallas import tpu as pltpu
from jax.sharding import Mesh, PartitionSpec as P

BF = jnp.bfloat16
F32 = jnp.float32
VMEM_LIMIT = 16 * 1024 * 1024
PRE_LIMIT = 52 * 1024 * 1024
SIDE = 4


def dot(a, b, ca, cb):
    return lax.dot_general(a, b, (((ca,), (cb,)), ((), ())), preferred_element_type=F32)


def call(body, name, grid, ins, outs, shapes, args, flops, moved, scratch=(), core=None, limit=VMEM_LIMIT, aliases=None):
    spec = dict(grid=grid, in_specs=ins, out_specs=outs, scratch_shapes=list(scratch))
    if core is not None:
        spec = dict(grid_spec=pltpu.PrefetchScalarGridSpec(num_scalar_prefetch=1, **spec))
        args = (core,) + tuple(args)
    return pl.pallas_call(
        body,
        out_shape=shapes,
        compiler_params=pltpu.CompilerParams(
            dimension_semantics=("arbitrary",) * len(grid), vmem_limit_bytes=limit
        ),
        cost_estimate=pl.CostEstimate(
            flops=int(flops), bytes_accessed=int(moved), transcendentals=0
        ),
        name=name,
        input_output_aliases=aliases or {},
        **spec,
    )(*args)


STEPS = 4


def pre_kernel(p_ref, x_ref, w_ref, dec_ref, tgt_ref, a_ref, b_ref, *refs):
    outs, (x_buf, w_buf, acc, sems) = refs[:3], refs[3:]
    depth = x_ref.shape[1]
    step = depth // STEPS
    half = outs[0].shape[2]
    copies = []
    for k in range(STEPS):
        at = slice(k * step, (k + 1) * step)
        copies.append(pltpu.make_async_copy(w_ref.at[at, :], w_buf.at[at, :], sems.at[2 * k]))
        copies.append(pltpu.make_async_copy(x_ref.at[:, at], x_buf.at[:, at], sems.at[2 * k + 1]))
    sides = ((dec_ref, 1 - p_ref[2]), (tgt_ref, p_ref[2]), (tgt_ref, 1 - p_ref[2]))
    for i, ((src, side), to) in enumerate(zip(sides, outs)):
        at = pl.ds(pl.multiple_of(side * half, half), half)
        copies.append(pltpu.make_async_copy(src.at[:, :, at], to, sems.at[2 * STEPS + i]))
    for copy in copies:
        copy.start()
    for k in range(STEPS):
        copies[2 * k].wait()
        copies[2 * k + 1].wait()
        at = slice(k * step, (k + 1) * step)
        part = jnp.dot(x_buf[:, at], w_buf[at, :], preferred_element_type=F32)
        if k == 0:
            acc[...] = part
        else:
            acc[...] += part
    n = a_ref.shape[0]
    a_ref[...] = acc[:n, :].astype(BF)
    b_ref[...] = acc[n:, :].astype(BF)
    for copy in copies[2 * STEPS :]:
        copy.wait()


def pre_call(place, x, w, dec, target):
    rows, depth = x.shape
    lats = w.shape[1]
    targets, few, wide = target.shape
    part = pl.BlockSpec((rows // 2, lats), lambda i, p: (0, 0))
    outs = [pltpu.VMEM((rows // 2, lats), BF)] * 2
    outs += [pltpu.VMEM((targets, lats, wide // 2), BF)]
    outs += [pltpu.VMEM((targets, few, wide // 2), BF)] * 2
    return call(
        pre_kernel,
        "pre",
        (1,),
        [pl.BlockSpec(memory_space=pl.ANY)] * 4,
        [part, part] + [pl.BlockSpec(memory_space=pl.ANY)] * 3,
        outs,
        (x, w, dec, target),
        2 * rows * depth * lats,
        2 * (rows + lats) * depth,
        [
            pltpu.VMEM((rows, depth), BF),
            pltpu.VMEM((depth, lats), BF),
            pltpu.VMEM((rows, lats), F32),
            pltpu.SemaphoreType.DMA((2 * STEPS + 3,)),
        ],
        core=place,
        limit=PRE_LIMIT,
    )


def total_kernel(own_ref, got_ref, err_ref, *refs):
    rows = own_ref.shape[0] // 2
    for r in range(2):
        at = slice(r * rows, (r + 1) * rows)
        total = own_ref[at, :] + got_ref[at, :].astype(F32)
        refs[2 * r][...] = total
        refs[2 * r + 1][...] = total.astype(BF)


def total_call(own, got, err):
    rows, lats = own.shape
    whole = pl.BlockSpec(own.shape, lambda i: (0, 0))
    part = pl.BlockSpec((rows // 2, lats), lambda i: (0, 0))
    kept = [jax.ShapeDtypeStruct((rows // 2, lats), kind) for kind in (F32, BF)]
    return call(
        total_kernel,
        "total",
        (1,),
        [whole, whole, pl.BlockSpec(memory_space=pl.ANY)],
        [part] * 4 + [pl.BlockSpec(memory_space=pl.ANY)],
        kept * 2 + [jax.ShapeDtypeStruct(err.shape, BF)],
        (own, got, err),
        own.size,
        12 * own.size,
        aliases={2: 4},
    )


def latent_kernel(near_a, far_a, near_b, far_b, active_ref, bias_ref, after_ref, out_ref):
    rows = near_a.shape[0]
    for r, (near, far) in enumerate(((near_a, far_a), (near_b, far_b))):
        at = slice(r * rows, (r + 1) * rows)
        total = near[...] + far[...].astype(F32) + bias_ref[...]
        out_ref[at, :] = jnp.where(active_ref[at, :] > 0, total, 0.0).astype(BF)


def latent_call(top, bottom, active, bias, after):
    rows, lats = active.shape
    part = pl.BlockSpec((rows // 2, lats), lambda i: (0, 0))
    whole = pl.BlockSpec((rows, lats), lambda i: (0, 0))
    return call(
        latent_kernel,
        "latents",
        (1,),
        [part] * 4
        + [whole, pl.BlockSpec((1, lats), lambda i: (0, 0)), pl.BlockSpec(memory_space=pl.ANY)],
        whole,
        jax.ShapeDtypeStruct((rows, lats), BF),
        (*top, *bottom, active, bias.reshape(1, lats), after),
        4 * rows * lats,
        4e6,
    )


def pick_kernel(p_ref, dec_ref, after_ref, out_ref, done_ref):
    out_ref[...] = dec_ref[...]
    done_ref[...] = jnp.zeros(done_ref.shape, F32)


def pick_call(place, dec, after):
    targets, lats, wide = dec.shape
    half = wide // 2
    return call(
        pick_kernel,
        "pick_half",
        (targets,),
        [
            pl.BlockSpec((1, lats, half), lambda t, p: (t, 0, p[2])),
            pl.BlockSpec(memory_space=pl.ANY),
        ],
        [
            pl.BlockSpec((1, lats, half), lambda t, p: (t, 0, 0)),
            pl.BlockSpec((8, 128), lambda t, p: (0, 0)),
        ],
        [
            jax.ShapeDtypeStruct((targets, lats, half), BF),
            jax.ShapeDtypeStruct((8, 128), F32),
        ],
        (dec, after),
        0,
        4 * targets * lats * half,
        core=place,
    )


def place_of(p_ref, far, near):
    return jnp.where(p_ref[2] == 0, far * SIDE + near, near * SIDE + far)


def rebuild_kernel(p_ref, lat_ref, sib_ref, dec_ref, got_ref, *refs):
    outs, held = refs[:-1], refs[-1]
    total = jnp.dot(lat_ref[...], dec_ref[0], preferred_element_type=F32)
    total += jnp.dot(sib_ref[...], got_ref[0], preferred_element_type=F32)
    held[...] = total.reshape(held.shape)
    q = held.shape[2] // 2
    for ref, (step, lo, hi) in zip(outs, CUTS):
        to = lax.rem(p_ref[3] + step, SIDE)
        for i in range(SIDE):
            block = held[place_of(p_ref, to, i)]
            ref[i, 0] = block[:, lo * q : hi * q].astype(ref.dtype)


CUTS = ((2, 0, 1), (2, 1, 2), (1, 0, 1), (1, 1, 2), (3, 0, 1), (3, 1, 2), (0, 0, 2))
KINDS = (BF, BF, F32, BF, BF, F32, F32)


def rebuild_call(place, lat, sib, dec, got):
    rows, lats = lat.shape
    targets, _, half = got.shape
    piece = rows // (SIDE * SIDE)
    widths = [(hi - lo) * half // 2 for _, lo, hi in CUTS]
    whole = pl.BlockSpec((rows, lats), lambda t, p: (0, 0))
    return call(
        rebuild_kernel,
        "rebuild",
        (targets,),
        [
            whole,
            whole,
            pl.BlockSpec((1, lats, half), lambda t, p: (t, 0, 0)),
            pl.BlockSpec((1, lats, half), lambda t, p: (t, 0, 0)),
        ],
        [pl.BlockSpec((SIDE, 1, piece, w), lambda t, p: (0, t, 0, 0)) for w in widths],
        [
            jax.ShapeDtypeStruct((SIDE, targets, piece, w), kind)
            for w, kind in zip(widths, KINDS)
        ],
        (lat, sib, dec, got),
        4 * rows * lats * half * targets,
        11e6,
        [pltpu.VMEM((SIDE * SIDE, piece, half), F32)],
        core=place,
    )


def sum_kernel(p_ref, own_ref, *refs):
    parts, outs, held = refs[:4], refs[4:-1], refs[-1]
    q = held.shape[2] // 2
    for h in range(2):
        cols = slice(h * q, (h + 1) * q)
        total = own_ref[:, 0, :, cols]
        for part in parts[2 * h : 2 * h + 2]:
            total += part[:, 0].astype(F32)
        held[:, :, cols] = total
    for k in range(SIDE):
        outs[k][0] = held[lax.rem(p_ref[4] + k, SIDE)].astype(outs[k].dtype)


def sum_call(place, own, parts):
    _, targets, piece, half = own.shape
    block = pl.BlockSpec((SIDE, 1, piece, half // 2), lambda t, p: (0, t, 0, 0))
    return call(
        sum_kernel,
        "sum_first",
        (targets,),
        [pl.BlockSpec((SIDE, 1, piece, half), lambda t, p: (0, t, 0, 0))] + [block] * 4,
        [pl.BlockSpec((1, piece, half), lambda t, p: (t, 0, 0))] * SIDE,
        [jax.ShapeDtypeStruct((targets, piece, half), F32 if k == 0 else BF) for k in range(SIDE)],
        (own, *parts),
        4 * own.size,
        12 * own.size,
        [pltpu.VMEM((SIDE, piece, half), F32)],
        core=place,
    )


def error_kernel(scale, p_ref, own_ref, got_ref, *refs):
    parts, out, goal = refs[:SIDE], refs[SIDE], refs[SIDE + 1]
    few = own_ref.shape[1]
    for ref, side in ((own_ref, p_ref[2]), (got_ref, 1 - p_ref[2])):
        goal[pl.ds(pl.multiple_of(side * few, few), few), :] = ref[0].astype(F32)
    total = parts[0][0]
    for part in parts[1:]:
        total += part[0].astype(F32)
    out[0] = ((total - goal[...]) * scale).astype(BF)


def error_call(scale, place, own, got, parts):
    targets, piece, half = parts[0].shape
    one = pl.BlockSpec((1, piece, half), lambda t, p: (t, 0, 0))
    goal = pl.BlockSpec((1,) + own.shape[1:], lambda t, p: (t, 0, 0))
    return call(
        functools.partial(error_kernel, scale),
        "error",
        (targets,),
        [goal, goal] + [one] * SIDE,
        one,
        jax.ShapeDtypeStruct((targets, piece, half), BF),
        (own, got, *parts),
        8 * targets * piece * half,
        2e6,
        [pltpu.VMEM((piece, half), F32)],
        core=place,
    )


def join_kernel(p_ref, after_ref, *refs):
    parts, outs = refs[:SIDE], refs[SIDE:]
    q = outs[0].shape[3]
    for k in range(SIDE):
        at = lax.rem(p_ref[4] + SIDE - k, SIDE)
        for h in range(2):
            outs[h][at, 0] = parts[k][0, :, h * q : (h + 1) * q]


def join_call(place, parts, after):
    targets, piece, half = parts[0].shape
    return call(
        join_kernel,
        "join",
        (targets,),
        [pl.BlockSpec(memory_space=pl.ANY)]
        + [pl.BlockSpec((1, piece, half), lambda t, p: (t, 0, 0))] * SIDE,
        [pl.BlockSpec((SIDE, 1, piece, half // 2), lambda t, p: (0, t, 0, 0))] * 2,
        [jax.ShapeDtypeStruct((SIDE, targets, piece, half // 2), BF)] * 2,
        (after, *parts),
        0,
        8 * parts[0].size,
        core=place,
    )


def back_dot(err, dec_ref, out_ref, acc):
    t = pl.program_id(0)
    part = dot(err, dec_ref[0], 1, 0)

    @pl.when(t == 0)
    def _():
        acc[...] = part

    @pl.when(t > 0)
    def _():
        acc[...] += part

    @pl.when(t == pl.num_programs(0) - 1)
    def _():
        out_ref[...] = acc[...].astype(out_ref.dtype)


def back_sib_kernel(p_ref, dec_ref, *refs):
    parts, (err_ref, out_ref, acc) = refs[: 2 * SIDE], refs[2 * SIDE :]
    piece, q = parts[0].shape[2:]
    for k in range(SIDE):
        far = lax.rem(p_ref[3] + SIDE - k, SIDE)
        for i in range(SIDE):
            at = pl.ds(pl.multiple_of(place_of(p_ref, far, i) * piece, piece), piece)
            for h in range(2):
                err_ref[0, at, h * q : (h + 1) * q] = parts[2 * k + h][i, 0]
    back_dot(err_ref[0], dec_ref, out_ref, acc)


def back_sib_call(place, parts, dec):
    _, targets, piece, q = parts[0].shape
    half, lats = dec.shape[1:]
    rows = SIDE * SIDE * piece
    return call(
        back_sib_kernel,
        "back_sib",
        (targets,),
        [
            pl.BlockSpec((1, half, lats), lambda t, p: (t, 0, 0)),
        ]
        + [pl.BlockSpec((SIDE, 1, piece, q), lambda t, p: (0, t, 0, 0))] * (2 * SIDE),
        [
            pl.BlockSpec((1, rows, half), lambda t, p: (t, 0, 0)),
            pl.BlockSpec((rows, lats), lambda t, p: (0, 0)),
        ],
        [
            jax.ShapeDtypeStruct((targets, rows, half), BF),
            jax.ShapeDtypeStruct((rows, lats), BF),
        ],
        (dec, *parts),
        2 * rows * lats * half * targets,
        10e6,
        [pltpu.VMEM((rows, lats), F32)],
        core=place,
    )


def back_own_kernel(p_ref, err_ref, dec_ref, out_ref, acc):
    back_dot(err_ref[0], dec_ref, out_ref, acc)


def back_own_call(place, err, dec):
    targets, rows, half = err.shape
    lats = dec.shape[2]
    return call(
        back_own_kernel,
        "back_own",
        (targets,),
        [
            pl.BlockSpec((1, rows, half), lambda t, p: (t, 0, 0)),
            pl.BlockSpec((1, half, lats), lambda t, p: (t, 0, 0)),
        ],
        pl.BlockSpec((rows, lats), lambda t, p: (0, 0)),
        jax.ShapeDtypeStruct((rows, lats), F32),
        (err, dec),
        2 * rows * lats * half * targets,
        7e6,
        [pltpu.VMEM((rows, lats), F32)],
        core=place,
    )


def turn_kernel(x_ref, lat_ref, after_ref, x_out, lat_out, done_ref):
    done_ref[...] = jnp.zeros(done_ref.shape, F32)
    x_out[...] = x_ref[...].T

    @pl.when(pl.program_id(0) == 0)
    def _():
        lat_out[...] = lat_ref[...].T


def turn_call(x, lat, after):
    rows, depth = x.shape
    lats = lat.shape[1]
    step = 512
    whole = pl.BlockSpec((rows, lats), lambda i: (0, 0))
    turned = pl.BlockSpec((lats, rows), lambda i: (0, 0))
    return call(
        turn_kernel,
        "turn",
        (depth // step,),
        [
            pl.BlockSpec((rows, step), lambda i: (0, i)),
            whole,
            pl.BlockSpec(memory_space=pl.ANY),
        ],
        [
            pl.BlockSpec((step, rows), lambda i: (i, 0)),
            turned,
            pl.BlockSpec((8, 128), lambda i: (0, 0)),
        ],
        [jax.ShapeDtypeStruct((depth, rows), BF)]
        + [jax.ShapeDtypeStruct((lats, rows), BF)]
        + [jax.ShapeDtypeStruct((8, 128), F32)],
        (x, lat, after),
        0,
        6e6,
    )


def turn_dec_kernel(own_ref, got_ref, after_ref, own_out, got_out, done_ref):
    done_ref[...] = jnp.zeros(done_ref.shape, F32)
    own_out[0] = own_ref[0].T
    got_out[0] = got_ref[0].T


def turn_dec_call(own, got, after):
    targets, lats, half = own.shape
    plain = pl.BlockSpec((1, lats, half), lambda t: (t, 0, 0))
    turned = pl.BlockSpec((1, half, lats), lambda t: (t, 0, 0))
    return call(
        turn_dec_kernel,
        "turn_dec",
        (targets,),
        [plain, plain, pl.BlockSpec(memory_space=pl.ANY)],
        [turned, turned, pl.BlockSpec((8, 128), lambda t: (0, 0))],
        [jax.ShapeDtypeStruct((targets, half, lats), BF)] * 2
        + [jax.ShapeDtypeStruct((8, 128), F32)],
        (own, got, after),
        0,
        12e6,
    )


def dec_kernel(p_ref, lat_ref, err_ref, *refs):
    out_ref, done_ref = refs[-2:]
    done_ref[...] = jnp.zeros(done_ref.shape, F32)
    out_ref[0] = dot(lat_ref[...], err_ref[0], 1, 0).astype(BF)


def dec_call(place, lat, err, grad=None):
    targets, rows, half = err.shape
    lats = lat.shape[0]
    own = grad is None
    return call(
        dec_kernel,
        "dec_grad_own" if own else "dec_grad_sib",
        (targets,),
        [
            pl.BlockSpec((lats, rows), lambda t, p: (0, 0)),
            pl.BlockSpec((1, rows, half), lambda t, p: (t, 0, 0)),
        ]
        + ([] if own else [pl.BlockSpec(memory_space=pl.ANY)]),
        [
            pl.BlockSpec((1, lats, half), lambda t, p: (t, 0, p[2] if own else 1 - p[2])),
            pl.BlockSpec((8, 128), lambda t, p: (0, 0)),
        ],
        [
            jax.ShapeDtypeStruct((targets, lats, 2 * half), BF),
            jax.ShapeDtypeStruct((8, 128), F32),
        ],
        (lat, err) if own else (lat, err, grad),
        2 * rows * lats * half * targets,
        7e6,
        core=place,
        aliases=None if own else {3: 0},
    )


def enc_kernel(x_ref, active_ref, after_ref, near_a, far_a, near_b, far_b, enc_ref, bias_ref, grad):
    @pl.when(pl.program_id(0) == 0)
    def _():
        rows = near_a.shape[0]
        sums = jnp.zeros(bias_ref.shape, F32)
        for r, (near, far) in enumerate(((near_a, far_a), (near_b, far_b))):
            at = slice(r * rows, (r + 1) * rows)
            total = near[...] + far[...].astype(F32)
            kept = jnp.where(active_ref[at, :] > 0, total, 0.0).astype(BF)
            grad[at, :] = kept
            sums += jnp.sum(kept.astype(F32), axis=0, keepdims=True)
        bias_ref[...] = sums

    enc_ref[...] = dot(x_ref[...], grad[...], 1, 0).astype(BF)


def enc_call(x, active, after, top, bottom):
    depth, rows = x.shape
    lats = active.shape[1]
    step = 512
    return call(
        enc_kernel,
        "enc_grad",
        (depth // step,),
        [
            pl.BlockSpec((step, rows), lambda i: (i, 0)),
            pl.BlockSpec((rows, lats), lambda i: (0, 0)),
            pl.BlockSpec(memory_space=pl.ANY),
        ]
        + [pl.BlockSpec((rows // 2, lats), lambda i: (0, 0))] * 4,
        [
            pl.BlockSpec((step, lats), lambda i: (i, 0)),
            pl.BlockSpec((1, lats), lambda i: (0, 0)),
        ],
        [jax.ShapeDtypeStruct((depth, lats), BF), jax.ShapeDtypeStruct((1, lats), F32)],
        (x, active, after, *top, *bottom),
        2 * rows * depth * lats,
        7e6,
        [pltpu.VMEM((rows, lats), BF)],
    )


def swap(value):
    return lax.ppermute(value, "c", [(0, 1), (1, 0)])


def pair_kernel(own_ref, got_ref, after_ref, sum_ref, low_ref):
    total = own_ref[...] + got_ref[...].astype(F32)
    sum_ref[...] = total
    low_ref[...] = total.astype(BF)


def pair_call(own, got, after):
    whole = pl.BlockSpec(own.shape, lambda i: (0, 0))
    return call(
        pair_kernel,
        "pair_sum",
        (1,),
        [whole, whole, pl.BlockSpec(memory_space=pl.ANY)],
        [whole, whole],
        [jax.ShapeDtypeStruct(own.shape, kind) for kind in (F32, BF)],
        (own, got, after),
        own.size,
        12 * own.size,
    )


EVEN = (1, 0, 3, 2)
ODD = (3, 2, 1, 0)


def pair(value, tables):
    moves = [(z * 2 + c, tables[c][z] * 2 + c) for z in range(SIDE) for c in range(2)]
    return lax.ppermute(value, ("z", "c"), moves)


def z_sum(part, low, after=None):
    got = pair(low, (EVEN, ODD))
    if after is None:
        first = part.astype(F32) + got.astype(F32)
        return first, pair(first.astype(BF), (ODD, EVEN))
    first, low = pair_call(part, got, after)
    return first, pair(low, (ODD, EVEN))


def shift(value, second, step):
    moves = []
    for x in range(SIDE):
        for y in range(SIDE):
            for c in range(2):
                along_x = (c == 0) != second
                to = ((x + step) % SIDE, y) if along_x else (x, (y + step) % SIDE)
                moves.append(((x * SIDE + y) * 2 + c, (to[0] * SIDE + to[1]) * 2 + c))
    return lax.ppermute(value, ("x", "y", "c"), moves)


def plus(a, b):
    return (a + b.astype(F32)).astype(BF)


def ring_sum(cuts):
    far_a, far_b, up_a, up_b, down_a, down_b, own = cuts
    met_a, met_b = shift(far_a, False, 1), shift(far_b, False, 3)
    from_b, from_a = shift(up_b, False, 1), shift(down_a, False, 3)
    ring_a = shift(plus(up_a, met_a), False, 1)
    ring_b = shift(plus(down_b, met_b), False, 3)
    return own, (ring_a, from_a, from_b, ring_b)


def ring_gather(a, b):
    below_a, above_b = shift(a, False, 1), shift(b, False, 3)
    below_b, above_a = shift(b, False, 1), shift(a, False, 3)
    far_a, far_b = shift(below_a, False, 1), shift(above_b, False, 3)
    return a, b, below_a, below_b, far_a, far_b, above_a, above_b


def scatter(parts):
    return [parts[0]] + [shift(parts[k], True, k) for k in (1, 2, 3)]


def spread(value):
    return [value] + [shift(value, True, k) for k in (1, 2, 3)]


def per_device(mlp_inputs, enc_weight, enc_bias, active, dec_weight, target):
    rows = mlp_inputs.shape[0]
    x, y, c = (lax.axis_index(a) for a in "xyc")
    first, second = jnp.where(c == 0, x, y), jnp.where(c == 0, y, x)
    place = jnp.stack([x, y, c, first, second]).astype(jnp.int32)
    scale = 1.0 / math.sqrt(rows)

    top, bottom, dec_sent, tgt_own, tgt_sent = pre_call(
        place, mlp_inputs, enc_weight, dec_weight, target
    )
    top, bottom = z_sum(top, top), z_sum(bottom, bottom)
    dec_got = swap(dec_sent)
    tgt_got = swap(tgt_sent)
    dec_own, done = pick_call(place, dec_weight, bottom[0])
    lat = latent_call(top, bottom, active, enc_bias, done)
    lat_sib = swap(lat)

    own, parts = ring_sum(rebuild_call(place, lat, lat_sib, dec_own, dec_got))
    parts = scatter(sum_call(place, own, parts))
    err = error_call(scale, place, tgt_own, tgt_got, parts)
    x_turned, lat_turned, done = turn_call(mlp_inputs, lat, err)
    own_turned, got_turned, done = turn_dec_call(dec_own, dec_got, done)
    parts = ring_gather(*join_call(place, spread(err), done))

    err, grad_got = back_sib_call(place, parts, got_turned)
    grad_got = swap(grad_got)
    top, low_top, bottom, low_bottom, err = total_call(
        back_own_call(place, err, own_turned), grad_got, err
    )
    dec_grad, done = dec_call(place, lat_turned, err)
    top, bottom = z_sum(top, low_top, done), z_sum(bottom, low_bottom, done)
    dec_grad, done = dec_call(place, lat_turned, swap(err), dec_grad)
    enc_grad, bias_grad = enc_call(x_turned, active, done, top, bottom)
    return enc_grad, bias_grad.reshape(-1), dec_grad


def solution(mesh):
    grid = Mesh(mesh.devices.reshape(4, 4, 4, 2), ("z", "x", "y", "c"))
    lat = ("x", "y", "c")
    in_specs = (
        P(None, "z"),
        P("z", lat),
        P(lat),
        P(None, lat),
        P(None, lat, "z"),
        P(None, lat, "z"),
    )
    out_specs = (P("z", lat), P(lat), P(None, lat, "z"))
    return jax.shard_map(
        per_device, mesh=grid, in_specs=in_specs, out_specs=out_specs, check_vma=False
    )
```

```python
import functools
import math

import jax
import jax.numpy as jnp
from jax import lax
from jax.experimental import pallas as pl
from jax.experimental.pallas import tpu as pltpu
from jax.sharding import Mesh, PartitionSpec as P

BF = jnp.bfloat16
F32 = jnp.float32
VMEM_LIMIT = 16 * 1024 * 1024
PRE_LIMIT = 52 * 1024 * 1024
SIDE = 4


def dot(a, b, ca, cb):
    return lax.dot_general(a, b, (((ca,), (cb,)), ((), ())), preferred_element_type=F32)


def call(body, name, grid, ins, outs, shapes, args, flops, moved, scratch=(), core=None, limit=VMEM_LIMIT, aliases=None):
    spec = dict(grid=grid, in_specs=ins, out_specs=outs, scratch_shapes=list(scratch))
    if core is not None:
        spec = dict(grid_spec=pltpu.PrefetchScalarGridSpec(num_scalar_prefetch=1, **spec))
        args = (core,) + tuple(args)
    return pl.pallas_call(
        body,
        out_shape=shapes,
        compiler_params=pltpu.CompilerParams(
            dimension_semantics=("arbitrary",) * len(grid), vmem_limit_bytes=limit
        ),
        cost_estimate=pl.CostEstimate(
            flops=int(flops), bytes_accessed=int(moved), transcendentals=0
        ),
        name=name,
        input_output_aliases=aliases or {},
        **spec,
    )(*args)


STEPS = 4


def pre_kernel(p_ref, x_ref, w_ref, dec_ref, tgt_ref, a_ref, b_ref, *refs):
    outs, (x_buf, w_buf, acc, sems) = refs[:3], refs[3:]
    depth = x_ref.shape[1]
    step = depth // STEPS
    half = outs[0].shape[2]
    copies = []
    for k in range(STEPS):
        at = slice(k * step, (k + 1) * step)
        copies.append(pltpu.make_async_copy(w_ref.at[at, :], w_buf.at[at, :], sems.at[2 * k]))
        copies.append(pltpu.make_async_copy(x_ref.at[:, at], x_buf.at[:, at], sems.at[2 * k + 1]))
    sides = ((dec_ref, 1 - p_ref[2]), (tgt_ref, p_ref[2]), (tgt_ref, 1 - p_ref[2]))
    for i, ((src, side), to) in enumerate(zip(sides, outs)):
        at = pl.ds(pl.multiple_of(side * half, half), half)
        copies.append(pltpu.make_async_copy(src.at[:, :, at], to, sems.at[2 * STEPS + i]))
    for copy in copies:
        copy.start()
    for k in range(STEPS):
        copies[2 * k].wait()
        copies[2 * k + 1].wait()
        at = slice(k * step, (k + 1) * step)
        part = jnp.dot(x_buf[:, at], w_buf[at, :], preferred_element_type=F32)
        if k == 0:
            acc[...] = part
        else:
            acc[...] += part
    n = a_ref.shape[0]
    a_ref[...] = acc[:n, :].astype(BF)
    b_ref[...] = acc[n:, :].astype(BF)
    for copy in copies[2 * STEPS :]:
        copy.wait()


def pre_call(place, x, w, dec, target):
    rows, depth = x.shape
    lats = w.shape[1]
    targets, few, wide = target.shape
    part = pl.BlockSpec((rows // 2, lats), lambda i, p: (0, 0))
    outs = [pltpu.VMEM((rows // 2, lats), BF)] * 2
    outs += [pltpu.VMEM((targets, lats, wide // 2), BF)]
    outs += [pltpu.VMEM((targets, few, wide // 2), BF)] * 2
    return call(
        pre_kernel,
        "pre",
        (1,),
        [pl.BlockSpec(memory_space=pl.ANY)] * 4,
        [part, part] + [pl.BlockSpec(memory_space=pl.ANY)] * 3,
        outs,
        (x, w, dec, target),
        2 * rows * depth * lats,
        2 * (rows + lats) * depth,
        [
            pltpu.VMEM((rows, depth), BF),
            pltpu.VMEM((depth, lats), BF),
            pltpu.VMEM((rows, lats), F32),
            pltpu.SemaphoreType.DMA((2 * STEPS + 3,)),
        ],
        core=place,
        limit=PRE_LIMIT,
    )


def total_kernel(own_ref, got_ref, err_ref, *refs):
    rows = own_ref.shape[0] // 2
    for r in range(2):
        at = slice(r * rows, (r + 1) * rows)
        total = own_ref[at, :] + got_ref[at, :].astype(F32)
        refs[2 * r][...] = total
        refs[2 * r + 1][...] = total.astype(BF)


def total_call(own, got, err):
    rows, lats = own.shape
    whole = pl.BlockSpec(own.shape, lambda i: (0, 0))
    part = pl.BlockSpec((rows // 2, lats), lambda i: (0, 0))
    kept = [jax.ShapeDtypeStruct((rows // 2, lats), kind) for kind in (F32, BF)]
    return call(
        total_kernel,
        "total",
        (1,),
        [whole, whole, pl.BlockSpec(memory_space=pl.ANY)],
        [part] * 4 + [pl.BlockSpec(memory_space=pl.ANY)],
        kept * 2 + [jax.ShapeDtypeStruct(err.shape, BF)],
        (own, got, err),
        own.size,
        12 * own.size,
        aliases={2: 4},
    )


def latent_kernel(near_a, far_a, near_b, far_b, active_ref, bias_ref, after_ref, out_ref):
    rows = near_a.shape[0]
    for r, (near, far) in enumerate(((near_a, far_a), (near_b, far_b))):
        at = slice(r * rows, (r + 1) * rows)
        total = near[...] + far[...].astype(F32) + bias_ref[...]
        out_ref[at, :] = jnp.where(active_ref[at, :] > 0, total, 0.0).astype(BF)


def latent_call(top, bottom, active, bias, after):
    rows, lats = active.shape
    part = pl.BlockSpec((rows // 2, lats), lambda i: (0, 0))
    whole = pl.BlockSpec((rows, lats), lambda i: (0, 0))
    return call(
        latent_kernel,
        "latents",
        (1,),
        [part] * 4
        + [whole, pl.BlockSpec((1, lats), lambda i: (0, 0)), pl.BlockSpec(memory_space=pl.ANY)],
        whole,
        jax.ShapeDtypeStruct((rows, lats), BF),
        (*top, *bottom, active, bias.reshape(1, lats), after),
        4 * rows * lats,
        4e6,
    )


def pick_kernel(p_ref, dec_ref, after_ref, out_ref, done_ref):
    out_ref[...] = dec_ref[...]
    done_ref[...] = jnp.zeros(done_ref.shape, F32)


def pick_call(place, dec, after):
    targets, lats, wide = dec.shape
    half = wide // 2
    return call(
        pick_kernel,
        "pick_half",
        (targets,),
        [
            pl.BlockSpec((1, lats, half), lambda t, p: (t, 0, p[2])),
            pl.BlockSpec(memory_space=pl.ANY),
        ],
        [
            pl.BlockSpec((1, lats, half), lambda t, p: (t, 0, 0)),
            pl.BlockSpec((8, 128), lambda t, p: (0, 0)),
        ],
        [
            jax.ShapeDtypeStruct((targets, lats, half), BF),
            jax.ShapeDtypeStruct((8, 128), F32),
        ],
        (dec, after),
        0,
        4 * targets * lats * half,
        core=place,
    )


def place_of(p_ref, far, near):
    return jnp.where(p_ref[2] == 0, far * SIDE + near, near * SIDE + far)


def rebuild_kernel(p_ref, lat_ref, sib_ref, dec_ref, got_ref, *refs):
    outs, (lat, sib) = refs[:-2], refs[-2:]
    piece, half = outs[-1].shape[2:]
    strip, q = SIDE * piece, half // 2

    @pl.when(pl.program_id(0) == 0)
    def _():
        for step in range(SIDE):
            to = lax.rem(p_ref[3] + step, SIDE)
            for i in range(SIDE):
                src = pl.ds(pl.multiple_of(place_of(p_ref, to, i) * piece, piece), piece)
                at = step * strip + i * piece
                lat[at : at + piece, :] = lat_ref[src, :]
                sib[at : at + piece, :] = sib_ref[src, :]

    total = jnp.dot(lat[...], dec_ref[0], preferred_element_type=F32)
    total += jnp.dot(sib[...], got_ref[0], preferred_element_type=F32)
    for ref, (step, lo, hi) in zip(outs, CUTS):
        block = total[step * strip : (step + 1) * strip, lo * q : hi * q]
        ref[:, 0] = block.astype(ref.dtype).reshape(SIDE, piece, (hi - lo) * q)


CUTS = ((2, 0, 1), (2, 1, 2), (1, 0, 1), (1, 1, 2), (3, 0, 1), (3, 1, 2), (0, 0, 2))
KINDS = (BF, BF, F32, BF, BF, F32, F32)


def rebuild_call(place, lat, sib, dec, got):
    rows, lats = lat.shape
    targets, _, half = got.shape
    piece = rows // (SIDE * SIDE)
    widths = [(hi - lo) * half // 2 for _, lo, hi in CUTS]
    whole = pl.BlockSpec((rows, lats), lambda t, p: (0, 0))
    return call(
        rebuild_kernel,
        "rebuild",
        (targets,),
        [
            whole,
            whole,
            pl.BlockSpec((1, lats, half), lambda t, p: (t, 0, 0)),
            pl.BlockSpec((1, lats, half), lambda t, p: (t, 0, 0)),
        ],
        [pl.BlockSpec((SIDE, 1, piece, w), lambda t, p: (0, t, 0, 0)) for w in widths],
        [
            jax.ShapeDtypeStruct((SIDE, targets, piece, w), kind)
            for w, kind in zip(widths, KINDS)
        ],
        (lat, sib, dec, got),
        4 * rows * lats * half * targets,
        11e6,
        [pltpu.VMEM((rows, lats), BF)] * 2,
        core=place,
    )


def sum_kernel(p_ref, own_ref, *refs):
    parts, outs, held = refs[:4], refs[4:-1], refs[-1]
    q = held.shape[2] // 2
    for h in range(2):
        cols = slice(h * q, (h + 1) * q)
        total = own_ref[:, 0, :, cols]
        for part in parts[2 * h : 2 * h + 2]:
            total += part[:, 0].astype(F32)
        held[:, :, cols] = total
    for k in range(SIDE):
        outs[k][0] = held[lax.rem(p_ref[4] + k, SIDE)].astype(outs[k].dtype)


def sum_call(place, own, parts):
    _, targets, piece, half = own.shape
    block = pl.BlockSpec((SIDE, 1, piece, half // 2), lambda t, p: (0, t, 0, 0))
    return call(
        sum_kernel,
        "sum_first",
        (targets,),
        [pl.BlockSpec((SIDE, 1, piece, half), lambda t, p: (0, t, 0, 0))] + [block] * 4,
        [pl.BlockSpec((1, piece, half), lambda t, p: (t, 0, 0))] * SIDE,
        [jax.ShapeDtypeStruct((targets, piece, half), F32 if k == 0 else BF) for k in range(SIDE)],
        (own, *parts),
        4 * own.size,
        12 * own.size,
        [pltpu.VMEM((SIDE, piece, half), F32)],
        core=place,
    )


def error_kernel(scale, p_ref, own_ref, got_ref, *refs):
    parts, out, goal = refs[:SIDE], refs[SIDE], refs[SIDE + 1]
    few = own_ref.shape[1]
    for ref, side in ((own_ref, p_ref[2]), (got_ref, 1 - p_ref[2])):
        goal[:, pl.ds(pl.multiple_of(side * few, few), few), :] = ref[...].astype(F32)
    total = parts[0][...]
    for part in parts[1:]:
        total += part[...].astype(F32)
    out[...] = ((total - goal[...]) * scale).astype(BF)


def error_call(scale, place, own, got, parts):
    shape = parts[0].shape
    one = pl.BlockSpec(shape, lambda t, p: (0, 0, 0))
    goal = pl.BlockSpec(own.shape, lambda t, p: (0, 0, 0))
    return call(
        functools.partial(error_kernel, scale),
        "error",
        (1,),
        [goal, goal] + [one] * SIDE,
        one,
        jax.ShapeDtypeStruct(shape, BF),
        (own, got, *parts),
        8 * parts[0].size,
        2e6,
        [pltpu.VMEM(shape, F32)],
        core=place,
    )


def join_kernel(p_ref, after_ref, *refs):
    parts, outs = refs[:SIDE], refs[SIDE:]
    q = outs[0].shape[3]
    for k in range(SIDE):
        at = lax.rem(p_ref[4] + SIDE - k, SIDE)
        for h in range(2):
            outs[h][at] = parts[k][:, :, h * q : (h + 1) * q]


def join_call(place, parts, after):
    targets, piece, half = parts[0].shape
    shape = (SIDE, targets, piece, half // 2)
    return call(
        join_kernel,
        "join",
        (1,),
        [pl.BlockSpec(memory_space=pl.ANY)]
        + [pl.BlockSpec(parts[0].shape, lambda t, p: (0, 0, 0))] * SIDE,
        [pl.BlockSpec(shape, lambda t, p: (0, 0, 0, 0))] * 2,
        [jax.ShapeDtypeStruct(shape, BF)] * 2,
        (after, *parts),
        0,
        8 * parts[0].size,
        core=place,
    )


def back_dot(err, dec_ref, out_ref, acc):
    t = pl.program_id(0)
    part = dot(err, dec_ref[0], 1, 0)

    @pl.when(t == 0)
    def _():
        acc[...] = part

    @pl.when(t > 0)
    def _():
        acc[...] += part

    @pl.when(t == pl.num_programs(0) - 1)
    def _():
        out_ref[...] = acc[...].astype(out_ref.dtype)


def back_sib_kernel(p_ref, dec_ref, *refs):
    parts, (err_ref, out_ref, acc) = refs[: 2 * SIDE], refs[2 * SIDE :]
    piece, q = parts[0].shape[2:]
    for k in range(SIDE):
        far = lax.rem(p_ref[3] + SIDE - k, SIDE)
        for i in range(SIDE):
            at = pl.ds(pl.multiple_of(place_of(p_ref, far, i) * piece, piece), piece)
            for h in range(2):
                err_ref[0, at, h * q : (h + 1) * q] = parts[2 * k + h][i, 0]
    back_dot(err_ref[0], dec_ref, out_ref, acc)


def back_sib_call(place, parts, dec):
    _, targets, piece, q = parts[0].shape
    half, lats = dec.shape[1:]
    rows = SIDE * SIDE * piece
    return call(
        back_sib_kernel,
        "back_sib",
        (targets,),
        [
            pl.BlockSpec((1, half, lats), lambda t, p: (t, 0, 0)),
        ]
        + [pl.BlockSpec((SIDE, 1, piece, q), lambda t, p: (0, t, 0, 0))] * (2 * SIDE),
        [
            pl.BlockSpec((1, rows, half), lambda t, p: (t, 0, 0)),
            pl.BlockSpec((rows, lats), lambda t, p: (0, 0)),
        ],
        [
            jax.ShapeDtypeStruct((targets, rows, half), BF),
            jax.ShapeDtypeStruct((rows, lats), BF),
        ],
        (dec, *parts),
        2 * rows * lats * half * targets,
        10e6,
        [pltpu.VMEM((rows, lats), F32)],
        core=place,
    )


def back_own_kernel(p_ref, err_ref, dec_ref, out_ref, acc):
    back_dot(err_ref[0], dec_ref, out_ref, acc)


def back_own_call(place, err, dec):
    targets, rows, half = err.shape
    lats = dec.shape[2]
    return call(
        back_own_kernel,
        "back_own",
        (targets,),
        [
            pl.BlockSpec((1, rows, half), lambda t, p: (t, 0, 0)),
            pl.BlockSpec((1, half, lats), lambda t, p: (t, 0, 0)),
        ],
        pl.BlockSpec((rows, lats), lambda t, p: (0, 0)),
        jax.ShapeDtypeStruct((rows, lats), F32),
        (err, dec),
        2 * rows * lats * half * targets,
        7e6,
        [pltpu.VMEM((rows, lats), F32)],
        core=place,
    )


def turn_kernel(x_ref, lat_ref, after_ref, x_out, lat_out, done_ref):
    done_ref[...] = jnp.zeros(done_ref.shape, F32)
    x_out[...] = x_ref[...].T

    @pl.when(pl.program_id(0) == 0)
    def _():
        lat_out[...] = lat_ref[...].T


def turn_call(x, lat, after):
    rows, depth = x.shape
    lats = lat.shape[1]
    step = 512
    whole = pl.BlockSpec((rows, lats), lambda i: (0, 0))
    turned = pl.BlockSpec((lats, rows), lambda i: (0, 0))
    return call(
        turn_kernel,
        "turn",
        (depth // step,),
        [
            pl.BlockSpec((rows, step), lambda i: (0, i)),
            whole,
            pl.BlockSpec(memory_space=pl.ANY),
        ],
        [
            pl.BlockSpec((step, rows), lambda i: (i, 0)),
            turned,
            pl.BlockSpec((8, 128), lambda i: (0, 0)),
        ],
        [jax.ShapeDtypeStruct((depth, rows), BF)]
        + [jax.ShapeDtypeStruct((lats, rows), BF)]
        + [jax.ShapeDtypeStruct((8, 128), F32)],
        (x, lat, after),
        0,
        6e6,
    )


def turn_dec_kernel(own_ref, got_ref, after_ref, own_out, got_out, done_ref):
    done_ref[...] = jnp.zeros(done_ref.shape, F32)
    own_out[0] = own_ref[0].T
    got_out[0] = got_ref[0].T


def turn_dec_call(own, got, after):
    targets, lats, half = own.shape
    plain = pl.BlockSpec((1, lats, half), lambda t: (t, 0, 0))
    turned = pl.BlockSpec((1, half, lats), lambda t: (t, 0, 0))
    return call(
        turn_dec_kernel,
        "turn_dec",
        (targets,),
        [plain, plain, pl.BlockSpec(memory_space=pl.ANY)],
        [turned, turned, pl.BlockSpec((8, 128), lambda t: (0, 0))],
        [jax.ShapeDtypeStruct((targets, half, lats), BF)] * 2
        + [jax.ShapeDtypeStruct((8, 128), F32)],
        (own, got, after),
        0,
        12e6,
    )


def dec_kernel(p_ref, lat_ref, err_ref, *refs):
    out_ref, done_ref = refs[-2:]
    done_ref[...] = jnp.zeros(done_ref.shape, F32)
    out_ref[0] = dot(lat_ref[...], err_ref[0], 1, 0).astype(BF)


def dec_call(place, lat, err, grad=None):
    targets, rows, half = err.shape
    lats = lat.shape[0]
    own = grad is None
    return call(
        dec_kernel,
        "dec_grad_own" if own else "dec_grad_sib",
        (targets,),
        [
            pl.BlockSpec((lats, rows), lambda t, p: (0, 0)),
            pl.BlockSpec((1, rows, half), lambda t, p: (t, 0, 0)),
        ]
        + ([] if own else [pl.BlockSpec(memory_space=pl.ANY)]),
        [
            pl.BlockSpec((1, lats, half), lambda t, p: (t, 0, p[2] if own else 1 - p[2])),
            pl.BlockSpec((8, 128), lambda t, p: (0, 0)),
        ],
        [
            jax.ShapeDtypeStruct((targets, lats, 2 * half), BF),
            jax.ShapeDtypeStruct((8, 128), F32),
        ],
        (lat, err) if own else (lat, err, grad),
        2 * rows * lats * half * targets,
        7e6,
        core=place,
        aliases=None if own else {3: 0},
    )


def enc_kernel(x_ref, active_ref, after_ref, near_a, far_a, near_b, far_b, enc_ref, bias_ref, grad):
    @pl.when(pl.program_id(0) == 0)
    def _():
        rows = near_a.shape[0]
        sums = jnp.zeros(bias_ref.shape, F32)
        for r, (near, far) in enumerate(((near_a, far_a), (near_b, far_b))):
            at = slice(r * rows, (r + 1) * rows)
            total = near[...] + far[...].astype(F32)
            kept = jnp.where(active_ref[at, :] > 0, total, 0.0).astype(BF)
            grad[at, :] = kept
            sums += jnp.sum(kept.astype(F32), axis=0, keepdims=True)
        bias_ref[...] = sums

    enc_ref[...] = dot(x_ref[...], grad[...], 1, 0).astype(BF)


def enc_call(x, active, after, top, bottom):
    depth, rows = x.shape
    lats = active.shape[1]
    step = 1024
    return call(
        enc_kernel,
        "enc_grad",
        (depth // step,),
        [
            pl.BlockSpec((step, rows), lambda i: (i, 0)),
            pl.BlockSpec((rows, lats), lambda i: (0, 0)),
            pl.BlockSpec(memory_space=pl.ANY),
        ]
        + [pl.BlockSpec((rows // 2, lats), lambda i: (0, 0))] * 4,
        [
            pl.BlockSpec((step, lats), lambda i: (i, 0)),
            pl.BlockSpec((1, lats), lambda i: (0, 0)),
        ],
        [jax.ShapeDtypeStruct((depth, lats), BF), jax.ShapeDtypeStruct((1, lats), F32)],
        (x, active, after, *top, *bottom),
        2 * rows * depth * lats,
        7e6,
        [pltpu.VMEM((rows, lats), BF)],
    )


def swap(value):
    return lax.ppermute(value, "c", [(0, 1), (1, 0)])


def pair_kernel(own_ref, got_ref, after_ref, sum_ref, low_ref):
    total = own_ref[...] + got_ref[...].astype(F32)
    sum_ref[...] = total
    low_ref[...] = total.astype(BF)


def pair_call(own, got, after):
    whole = pl.BlockSpec(own.shape, lambda i: (0, 0))
    return call(
        pair_kernel,
        "pair_sum",
        (1,),
        [whole, whole, pl.BlockSpec(memory_space=pl.ANY)],
        [whole, whole],
        [jax.ShapeDtypeStruct(own.shape, kind) for kind in (F32, BF)],
        (own, got, after),
        own.size,
        12 * own.size,
    )


EVEN = (1, 0, 3, 2)
ODD = (3, 2, 1, 0)


def pair(value, tables):
    moves = [(z * 2 + c, tables[c][z] * 2 + c) for z in range(SIDE) for c in range(2)]
    return lax.ppermute(value, ("z", "c"), moves)


def z_sum(part, low, after=None):
    got = pair(low, (EVEN, ODD))
    if after is None:
        first = part.astype(F32) + got.astype(F32)
        return first, pair(first.astype(BF), (ODD, EVEN))
    first, low = pair_call(part, got, after)
    return first, pair(low, (ODD, EVEN))


def shift(value, second, step):
    moves = []
    for x in range(SIDE):
        for y in range(SIDE):
            for c in range(2):
                along_x = (c == 0) != second
                to = ((x + step) % SIDE, y) if along_x else (x, (y + step) % SIDE)
                moves.append(((x * SIDE + y) * 2 + c, (to[0] * SIDE + to[1]) * 2 + c))
    return lax.ppermute(value, ("x", "y", "c"), moves)


def plus(a, b):
    return (a + b.astype(F32)).astype(BF)


def ring_sum(cuts):
    far_a, far_b, up_a, up_b, down_a, down_b, own = cuts
    met_a, met_b = shift(far_a, False, 1), shift(far_b, False, 3)
    from_b, from_a = shift(up_b, False, 1), shift(down_a, False, 3)
    ring_a = shift(plus(up_a, met_a), False, 1)
    ring_b = shift(plus(down_b, met_b), False, 3)
    return own, (ring_a, from_a, from_b, ring_b)


def ring_gather(a, b):
    below_a, above_b = shift(a, False, 1), shift(b, False, 3)
    below_b, above_a = shift(b, False, 1), shift(a, False, 3)
    far_a, far_b = shift(below_a, False, 1), shift(above_b, False, 3)
    return a, b, below_a, below_b, far_a, far_b, above_a, above_b


def scatter(parts):
    return [parts[0]] + [shift(parts[k], True, k) for k in (1, 2, 3)]


def spread(value):
    return [value] + [shift(value, True, k) for k in (1, 2, 3)]


def per_device(mlp_inputs, enc_weight, enc_bias, active, dec_weight, target):
    rows = mlp_inputs.shape[0]
    x, y, c = (lax.axis_index(a) for a in "xyc")
    first, second = jnp.where(c == 0, x, y), jnp.where(c == 0, y, x)
    place = jnp.stack([x, y, c, first, second]).astype(jnp.int32)
    scale = 1.0 / math.sqrt(rows)

    top, bottom, dec_sent, tgt_own, tgt_sent = pre_call(
        place, mlp_inputs, enc_weight, dec_weight, target
    )
    top, bottom = z_sum(top, top), z_sum(bottom, bottom)
    dec_got = swap(dec_sent)
    tgt_got = swap(tgt_sent)
    dec_own, done = pick_call(place, dec_weight, bottom[0])
    lat = latent_call(top, bottom, active, enc_bias, done)
    lat_sib = swap(lat)

    own, parts = ring_sum(rebuild_call(place, lat, lat_sib, dec_own, dec_got))
    parts = scatter(sum_call(place, own, parts))
    err = error_call(scale, place, tgt_own, tgt_got, parts)
    x_turned, lat_turned, done = turn_call(mlp_inputs, lat, err)
    own_turned, got_turned, done = turn_dec_call(dec_own, dec_got, done)
    parts = ring_gather(*join_call(place, spread(err), done))

    err, grad_got = back_sib_call(place, parts, got_turned)
    grad_got = swap(grad_got)
    top, low_top, bottom, low_bottom, err = total_call(
        back_own_call(place, err, own_turned), grad_got, err
    )
    dec_grad, done = dec_call(place, lat_turned, err)
    top, bottom = z_sum(top, low_top, done), z_sum(bottom, low_bottom, done)
    dec_grad, done = dec_call(place, lat_turned, swap(err), dec_grad)
    enc_grad, bias_grad = enc_call(x_turned, active, done, top, bottom)
    return enc_grad, bias_grad.reshape(-1), dec_grad


def solution(mesh):
    grid = Mesh(mesh.devices.reshape(4, 4, 4, 2), ("z", "x", "y", "c"))
    lat = ("x", "y", "c")
    in_specs = (
        P(None, "z"),
        P("z", lat),
        P(lat),
        P(None, lat),
        P(None, lat, "z"),
        P(None, lat, "z"),
    )
    out_specs = (P("z", lat), P(lat), P(None, lat, "z"))
    return jax.shard_map(
        per_device, mesh=grid, in_specs=in_specs, out_specs=out_specs, check_vma=False
    )
```

```python
import functools
import math

import jax
import jax.numpy as jnp
from jax import lax
from jax.experimental import pallas as pl
from jax.experimental.pallas import tpu as pltpu
from jax.sharding import Mesh, PartitionSpec as P

BF = jnp.bfloat16
F32 = jnp.float32
VMEM_LIMIT = 16 * 1024 * 1024
PRE_LIMIT = 52 * 1024 * 1024
SIDE = 4


def dot(a, b, ca, cb):
    return lax.dot_general(a, b, (((ca,), (cb,)), ((), ())), preferred_element_type=F32)


def call(body, name, grid, ins, outs, shapes, args, flops, moved, scratch=(), core=None, limit=VMEM_LIMIT, aliases=None):
    spec = dict(grid=grid, in_specs=ins, out_specs=outs, scratch_shapes=list(scratch))
    if core is not None:
        spec = dict(grid_spec=pltpu.PrefetchScalarGridSpec(num_scalar_prefetch=1, **spec))
        args = (core,) + tuple(args)
    return pl.pallas_call(
        body,
        out_shape=shapes,
        compiler_params=pltpu.CompilerParams(
            dimension_semantics=("arbitrary",) * len(grid), vmem_limit_bytes=limit
        ),
        cost_estimate=pl.CostEstimate(
            flops=int(flops), bytes_accessed=int(moved), transcendentals=0
        ),
        name=name,
        input_output_aliases=aliases or {},
        **spec,
    )(*args)


STEPS = 2


def pre_kernel(p_ref, x_ref, w_ref, dec_ref, tgt_ref, a_ref, b_ref, *refs):
    outs, (x_buf, w_buf, acc, sems) = refs[:3], refs[3:]
    depth = x_ref.shape[1]
    step = depth // STEPS
    half = outs[0].shape[2]
    copies = []
    for k in range(STEPS):
        at = slice(k * step, (k + 1) * step)
        copies.append(pltpu.make_async_copy(w_ref.at[at, :], w_buf.at[at, :], sems.at[2 * k]))
        copies.append(pltpu.make_async_copy(x_ref.at[:, at], x_buf.at[:, at], sems.at[2 * k + 1]))
    sides = ((dec_ref, 1 - p_ref[2]), (tgt_ref, p_ref[2]), (tgt_ref, 1 - p_ref[2]))
    for i, ((src, side), to) in enumerate(zip(sides, outs)):
        at = pl.ds(pl.multiple_of(side * half, half), half)
        copies.append(pltpu.make_async_copy(src.at[:, :, at], to, sems.at[2 * STEPS + i]))
    for copy in copies:
        copy.start()
    for k in range(STEPS):
        copies[2 * k].wait()
        copies[2 * k + 1].wait()
        at = slice(k * step, (k + 1) * step)
        part = jnp.dot(x_buf[:, at], w_buf[at, :], preferred_element_type=F32)
        if k == 0:
            acc[...] = part
        else:
            acc[...] += part
    n = a_ref.shape[0]
    a_ref[...] = acc[:n, :].astype(BF)
    b_ref[...] = acc[n:, :].astype(BF)
    for copy in copies[2 * STEPS :]:
        copy.wait()


def pre_call(place, x, w, dec, target):
    rows, depth = x.shape
    lats = w.shape[1]
    targets, few, wide = target.shape
    part = pl.BlockSpec((rows // 2, lats), lambda i, p: (0, 0))
    outs = [pltpu.VMEM((rows // 2, lats), BF)] * 2
    outs += [pltpu.VMEM((targets, lats, wide // 2), BF)]
    outs += [pltpu.VMEM((targets, few, wide // 2), BF)] * 2
    return call(
        pre_kernel,
        "pre",
        (1,),
        [pl.BlockSpec(memory_space=pl.ANY)] * 4,
        [part, part] + [pl.BlockSpec(memory_space=pl.ANY)] * 3,
        outs,
        (x, w, dec, target),
        2 * rows * depth * lats,
        2 * (rows + lats) * depth,
        [
            pltpu.VMEM((rows, depth), BF),
            pltpu.VMEM((depth, lats), BF),
            pltpu.VMEM((rows, lats), F32),
            pltpu.SemaphoreType.DMA((2 * STEPS + 3,)),
        ],
        core=place,
        limit=PRE_LIMIT,
    )


def total_kernel(own_ref, got_ref, err_ref, *refs):
    rows = own_ref.shape[0] // 2
    for r in range(2):
        at = slice(r * rows, (r + 1) * rows)
        total = own_ref[at, :] + got_ref[at, :].astype(F32)
        refs[2 * r][...] = total
        refs[2 * r + 1][...] = total.astype(BF)


def total_call(own, got, err):
    rows, lats = own.shape
    whole = pl.BlockSpec(own.shape, lambda i: (0, 0))
    part = pl.BlockSpec((rows // 2, lats), lambda i: (0, 0))
    kept = [jax.ShapeDtypeStruct((rows // 2, lats), kind) for kind in (F32, BF)]
    return call(
        total_kernel,
        "total",
        (1,),
        [whole, whole, pl.BlockSpec(memory_space=pl.ANY)],
        [part] * 4 + [pl.BlockSpec(memory_space=pl.ANY)],
        kept * 2 + [jax.ShapeDtypeStruct(err.shape, BF)],
        (own, got, err),
        own.size,
        12 * own.size,
        aliases={2: 4},
    )


def latent_kernel(near_ref, far_ref, active_ref, bias_ref, after_ref, out_ref):
    total = near_ref[...] + far_ref[...].astype(F32) + bias_ref[...]
    out_ref[...] = jnp.where(active_ref[...] > 0, total, 0.0).astype(BF)


def latent_call(r, terms, active, bias, after):
    rows, lats = terms[0].shape
    part = pl.BlockSpec((rows, lats), lambda i: (0, 0))
    return call(
        latent_kernel,
        f"latents_{r}",
        (1,),
        [
            part,
            part,
            pl.BlockSpec((rows, lats), lambda i: (r, 0)),
            pl.BlockSpec((1, lats), lambda i: (0, 0)),
            pl.BlockSpec(memory_space=pl.ANY),
        ],
        part,
        jax.ShapeDtypeStruct((rows, lats), BF),
        (*terms, active, bias.reshape(1, lats), after),
        4 * rows * lats,
        2e6,
    )


def pick_kernel(p_ref, dec_ref, after_ref, out_ref, done_ref):
    out_ref[...] = dec_ref[...]
    done_ref[...] = jnp.zeros(done_ref.shape, F32)


def pick_call(place, dec, after):
    targets, lats, wide = dec.shape
    half = wide // 2
    return call(
        pick_kernel,
        "pick_half",
        (targets,),
        [
            pl.BlockSpec((1, lats, half), lambda t, p: (t, 0, p[2])),
            pl.BlockSpec(memory_space=pl.ANY),
        ],
        [
            pl.BlockSpec((1, lats, half), lambda t, p: (t, 0, 0)),
            pl.BlockSpec((8, 128), lambda t, p: (0, 0)),
        ],
        [
            jax.ShapeDtypeStruct((targets, lats, half), BF),
            jax.ShapeDtypeStruct((8, 128), F32),
        ],
        (dec, after),
        0,
        4 * targets * lats * half,
        core=place,
    )


def place_of(p_ref, far, near):
    return jnp.where(p_ref[2] == 0, far * SIDE + near, near * SIDE + far)


def rebuild_kernel(p_ref, *refs):
    halves, (dec_ref, got_ref), outs, (lat, sib) = refs[:4], refs[4:6], refs[6:-2], refs[-2:]
    piece, half = outs[-1].shape[2:]
    strip, q = SIDE * piece, half // 2

    @pl.when(pl.program_id(0) == 0)
    def _():
        for x in range(SIDE):
            for y in range(SIDE):
                first, other = (jnp.where(p_ref[2] == 0, a, b) for a, b in ((x, y), (y, x)))
                spot = lax.rem(first - p_ref[3] + SIDE, SIDE) * SIDE + other
                to = pl.ds(pl.multiple_of(spot * piece, piece), piece)
                r, src = divmod((x * SIDE + y) * piece, halves[0].shape[0])
                lat[to, :] = halves[r][src : src + piece, :]
                sib[to, :] = halves[2 + r][src : src + piece, :]

    total = jnp.dot(lat[...], dec_ref[0], preferred_element_type=F32)
    total += jnp.dot(sib[...], got_ref[0], preferred_element_type=F32)
    for ref, (step, lo, hi) in zip(outs, CUTS):
        block = total[step * strip : (step + 1) * strip, lo * q : hi * q]
        ref[:, 0] = block.astype(ref.dtype).reshape(SIDE, piece, (hi - lo) * q)


CUTS = ((2, 0, 1), (2, 1, 2), (1, 0, 1), (1, 1, 2), (3, 0, 1), (3, 1, 2), (0, 0, 2))
KINDS = (BF, BF, F32, BF, BF, F32, F32)


def rebuild_call(place, lat, sib, dec, got):
    rows, lats = lat[0].shape
    rows *= 2
    targets, _, half = got.shape
    piece = rows // (SIDE * SIDE)
    widths = [(hi - lo) * half // 2 for _, lo, hi in CUTS]
    part = pl.BlockSpec((rows // 2, lats), lambda t, p: (0, 0))
    return call(
        rebuild_kernel,
        "rebuild",
        (targets,),
        [
            part,
            part,
            part,
            part,
            pl.BlockSpec((1, lats, half), lambda t, p: (t, 0, 0)),
            pl.BlockSpec((1, lats, half), lambda t, p: (t, 0, 0)),
        ],
        [pl.BlockSpec((SIDE, 1, piece, w), lambda t, p: (0, t, 0, 0)) for w in widths],
        [
            jax.ShapeDtypeStruct((SIDE, targets, piece, w), kind)
            for w, kind in zip(widths, KINDS)
        ],
        (*lat, *sib, dec, got),
        4 * rows * lats * half * targets,
        11e6,
        [pltpu.VMEM((rows, lats), BF)] * 2,
        core=place,
    )


def sum_kernel(p_ref, own_ref, *refs):
    parts, outs, held = refs[:4], refs[4:-1], refs[-1]
    q = held.shape[2] // 2
    for h in range(2):
        cols = slice(h * q, (h + 1) * q)
        total = own_ref[:, 0, :, cols]
        for part in parts[2 * h : 2 * h + 2]:
            total += part[:, 0].astype(F32)
        held[:, :, cols] = total
    for k in range(SIDE):
        outs[k][0] = held[lax.rem(p_ref[4] + k, SIDE)].astype(outs[k].dtype)


def sum_call(place, own, parts):
    _, targets, piece, half = own.shape
    block = pl.BlockSpec((SIDE, 1, piece, half // 2), lambda t, p: (0, t, 0, 0))
    return call(
        sum_kernel,
        "sum_first",
        (targets,),
        [pl.BlockSpec((SIDE, 1, piece, half), lambda t, p: (0, t, 0, 0))] + [block] * 4,
        [pl.BlockSpec((1, piece, half), lambda t, p: (t, 0, 0))] * SIDE,
        [jax.ShapeDtypeStruct((targets, piece, half), F32 if k == 0 else BF) for k in range(SIDE)],
        (own, *parts),
        4 * own.size,
        12 * own.size,
        [pltpu.VMEM((SIDE, piece, half), F32)],
        core=place,
    )


def error_kernel(scale, p_ref, own_ref, got_ref, *refs):
    parts, out, goal = refs[:SIDE], refs[SIDE], refs[SIDE + 1]
    few = own_ref.shape[1]
    for ref, side in ((own_ref, p_ref[2]), (got_ref, 1 - p_ref[2])):
        goal[:, pl.ds(pl.multiple_of(side * few, few), few), :] = ref[...].astype(F32)
    total = parts[0][...]
    for part in parts[1:]:
        total += part[...].astype(F32)
    out[...] = ((total - goal[...]) * scale).astype(BF)


def error_call(scale, place, own, got, parts):
    shape = parts[0].shape
    one = pl.BlockSpec(shape, lambda t, p: (0, 0, 0))
    goal = pl.BlockSpec(own.shape, lambda t, p: (0, 0, 0))
    return call(
        functools.partial(error_kernel, scale),
        "error",
        (1,),
        [goal, goal] + [one] * SIDE,
        one,
        jax.ShapeDtypeStruct(shape, BF),
        (own, got, *parts),
        8 * parts[0].size,
        2e6,
        [pltpu.VMEM(shape, F32)],
        core=place,
    )


def join_kernel(p_ref, after_ref, *refs):
    parts, outs = refs[:SIDE], refs[SIDE:]
    q = outs[0].shape[3]
    for k in range(SIDE):
        at = lax.rem(p_ref[4] + SIDE - k, SIDE)
        for h in range(2):
            outs[h][at] = parts[k][:, :, h * q : (h + 1) * q]


def join_call(place, parts, after):
    targets, piece, half = parts[0].shape
    shape = (SIDE, targets, piece, half // 2)
    return call(
        join_kernel,
        "join",
        (1,),
        [pl.BlockSpec(memory_space=pl.ANY)]
        + [pl.BlockSpec(parts[0].shape, lambda t, p: (0, 0, 0))] * SIDE,
        [pl.BlockSpec(shape, lambda t, p: (0, 0, 0, 0))] * 2,
        [jax.ShapeDtypeStruct(shape, BF)] * 2,
        (after, *parts),
        0,
        8 * parts[0].size,
        core=place,
    )


def back_dot(err, dec_ref, out_ref, acc):
    t = pl.program_id(0)
    part = dot(err, dec_ref[0], 1, 0)

    @pl.when(t == 0)
    def _():
        acc[...] = part

    @pl.when(t > 0)
    def _():
        acc[...] += part

    @pl.when(t == pl.num_programs(0) - 1)
    def _():
        out_ref[...] = acc[...].astype(out_ref.dtype)


def back_sib_kernel(p_ref, dec_ref, *refs):
    parts, (err_ref, out_ref, acc) = refs[: 2 * SIDE], refs[2 * SIDE :]
    piece, q = parts[0].shape[2:]
    for k in range(SIDE):
        far = lax.rem(p_ref[3] + SIDE - k, SIDE)
        for i in range(SIDE):
            at = pl.ds(pl.multiple_of(place_of(p_ref, far, i) * piece, piece), piece)
            for h in range(2):
                err_ref[0, at, h * q : (h + 1) * q] = parts[2 * k + h][i, 0]
    back_dot(err_ref[0], dec_ref, out_ref, acc)


def back_sib_call(place, parts, dec):
    _, targets, piece, q = parts[0].shape
    half, lats = dec.shape[1:]
    rows = SIDE * SIDE * piece
    return call(
        back_sib_kernel,
        "back_sib",
        (targets,),
        [
            pl.BlockSpec((1, half, lats), lambda t, p: (t, 0, 0)),
        ]
        + [pl.BlockSpec((SIDE, 1, piece, q), lambda t, p: (0, t, 0, 0))] * (2 * SIDE),
        [
            pl.BlockSpec((1, rows, half), lambda t, p: (t, 0, 0)),
            pl.BlockSpec((rows, lats), lambda t, p: (0, 0)),
        ],
        [
            jax.ShapeDtypeStruct((targets, rows, half), BF),
            jax.ShapeDtypeStruct((rows, lats), BF),
        ],
        (dec, *parts),
        2 * rows * lats * half * targets,
        10e6,
        [pltpu.VMEM((rows, lats), F32)],
        core=place,
    )


def back_own_kernel(p_ref, err_ref, dec_ref, out_ref, acc):
    back_dot(err_ref[0], dec_ref, out_ref, acc)


def back_own_call(place, err, dec):
    targets, rows, half = err.shape
    lats = dec.shape[2]
    return call(
        back_own_kernel,
        "back_own",
        (targets,),
        [
            pl.BlockSpec((1, rows, half), lambda t, p: (t, 0, 0)),
            pl.BlockSpec((1, half, lats), lambda t, p: (t, 0, 0)),
        ],
        pl.BlockSpec((rows, lats), lambda t, p: (0, 0)),
        jax.ShapeDtypeStruct((rows, lats), F32),
        (err, dec),
        2 * rows * lats * half * targets,
        7e6,
        [pltpu.VMEM((rows, lats), F32)],
        core=place,
    )


def turn_kernel(x_ref, top_ref, bottom_ref, after_ref, x_out, lat_out, done_ref):
    done_ref[...] = jnp.zeros(done_ref.shape, F32)
    x_out[...] = x_ref[...].T

    @pl.when(pl.program_id(0) == 0)
    def _():
        n = top_ref.shape[0]
        lat_out[:, :n] = top_ref[...].T
        lat_out[:, n:] = bottom_ref[...].T


def turn_call(x, lat, after):
    rows, depth = x.shape
    lats = lat[0].shape[1]
    step = 512
    part = pl.BlockSpec((rows // 2, lats), lambda i: (0, 0))
    turned = pl.BlockSpec((lats, rows), lambda i: (0, 0))
    return call(
        turn_kernel,
        "turn",
        (depth // step,),
        [
            pl.BlockSpec((rows, step), lambda i: (0, i)),
            part,
            part,
            pl.BlockSpec(memory_space=pl.ANY),
        ],
        [
            pl.BlockSpec((step, rows), lambda i: (i, 0)),
            turned,
            pl.BlockSpec((8, 128), lambda i: (0, 0)),
        ],
        [jax.ShapeDtypeStruct((depth, rows), BF)]
        + [jax.ShapeDtypeStruct((lats, rows), BF)]
        + [jax.ShapeDtypeStruct((8, 128), F32)],
        (x, *lat, after),
        0,
        6e6,
    )


def turn_dec_kernel(own_ref, got_ref, after_ref, own_out, got_out, done_ref):
    done_ref[...] = jnp.zeros(done_ref.shape, F32)
    own_out[0] = own_ref[0].T
    got_out[0] = got_ref[0].T


def turn_dec_call(own, got, after):
    targets, lats, half = own.shape
    plain = pl.BlockSpec((1, lats, half), lambda t: (t, 0, 0))
    turned = pl.BlockSpec((1, half, lats), lambda t: (t, 0, 0))
    return call(
        turn_dec_kernel,
        "turn_dec",
        (targets,),
        [plain, plain, pl.BlockSpec(memory_space=pl.ANY)],
        [turned, turned, pl.BlockSpec((8, 128), lambda t: (0, 0))],
        [jax.ShapeDtypeStruct((targets, half, lats), BF)] * 2
        + [jax.ShapeDtypeStruct((8, 128), F32)],
        (own, got, after),
        0,
        12e6,
    )


def dec_kernel(p_ref, lat_ref, err_ref, *refs):
    out_ref, done_ref = refs[-2:]
    done_ref[...] = jnp.zeros(done_ref.shape, F32)
    out_ref[0] = dot(lat_ref[...], err_ref[0], 1, 0).astype(BF)


def dec_call(place, lat, err, grad=None):
    targets, rows, half = err.shape
    lats = lat.shape[0]
    own = grad is None
    return call(
        dec_kernel,
        "dec_grad_own" if own else "dec_grad_sib",
        (targets,),
        [
            pl.BlockSpec((lats, rows), lambda t, p: (0, 0)),
            pl.BlockSpec((1, rows, half), lambda t, p: (t, 0, 0)),
        ]
        + ([] if own else [pl.BlockSpec(memory_space=pl.ANY)]),
        [
            pl.BlockSpec((1, lats, half), lambda t, p: (t, 0, p[2] if own else 1 - p[2])),
            pl.BlockSpec((8, 128), lambda t, p: (0, 0)),
        ],
        [
            jax.ShapeDtypeStruct((targets, lats, 2 * half), BF),
            jax.ShapeDtypeStruct((8, 128), F32),
        ],
        (lat, err) if own else (lat, err, grad),
        2 * rows * lats * half * targets,
        7e6,
        core=place,
        aliases=None if own else {3: 0},
    )


def enc_kernel(x_ref, active_ref, after_ref, near_a, far_a, near_b, far_b, enc_ref, bias_ref, grad):
    @pl.when(pl.program_id(0) == 0)
    def _():
        rows = near_a.shape[0]
        sums = jnp.zeros(bias_ref.shape, F32)
        for r, (near, far) in enumerate(((near_a, far_a), (near_b, far_b))):
            at = slice(r * rows, (r + 1) * rows)
            total = near[...] + far[...].astype(F32)
            kept = jnp.where(active_ref[at, :] > 0, total, 0.0).astype(BF)
            grad[at, :] = kept
            sums += jnp.sum(kept.astype(F32), axis=0, keepdims=True)
        bias_ref[...] = sums

    enc_ref[...] = dot(x_ref[...], grad[...], 1, 0).astype(BF)


def enc_call(x, active, after, top, bottom):
    depth, rows = x.shape
    lats = active.shape[1]
    step = 1024
    return call(
        enc_kernel,
        "enc_grad",
        (depth // step,),
        [
            pl.BlockSpec((step, rows), lambda i: (i, 0)),
            pl.BlockSpec((rows, lats), lambda i: (0, 0)),
            pl.BlockSpec(memory_space=pl.ANY),
        ]
        + [pl.BlockSpec((rows // 2, lats), lambda i: (0, 0))] * 4,
        [
            pl.BlockSpec((step, lats), lambda i: (i, 0)),
            pl.BlockSpec((1, lats), lambda i: (0, 0)),
        ],
        [jax.ShapeDtypeStruct((depth, lats), BF), jax.ShapeDtypeStruct((1, lats), F32)],
        (x, active, after, *top, *bottom),
        2 * rows * depth * lats,
        7e6,
        [pltpu.VMEM((rows, lats), BF)],
    )


def swap(value):
    return lax.ppermute(value, "c", [(0, 1), (1, 0)])


def pair_kernel(own_ref, got_ref, after_ref, sum_ref, low_ref):
    total = own_ref[...] + got_ref[...].astype(F32)
    sum_ref[...] = total
    low_ref[...] = total.astype(BF)


def pair_call(own, got, after):
    whole = pl.BlockSpec(own.shape, lambda i: (0, 0))
    return call(
        pair_kernel,
        "pair_sum",
        (1,),
        [whole, whole, pl.BlockSpec(memory_space=pl.ANY)],
        [whole, whole],
        [jax.ShapeDtypeStruct(own.shape, kind) for kind in (F32, BF)],
        (own, got, after),
        own.size,
        12 * own.size,
    )


EVEN = (1, 0, 3, 2)
ODD = (3, 2, 1, 0)


def pair(value, tables):
    moves = [(z * 2 + c, tables[c][z] * 2 + c) for z in range(SIDE) for c in range(2)]
    return lax.ppermute(value, ("z", "c"), moves)


def z_sum(part, low, after=None):
    got = pair(low, (EVEN, ODD))
    if after is None:
        first = part.astype(F32) + got.astype(F32)
        return first, pair(first.astype(BF), (ODD, EVEN))
    first, low = pair_call(part, got, after)
    return first, pair(low, (ODD, EVEN))


def shift(value, second, step):
    moves = []
    for x in range(SIDE):
        for y in range(SIDE):
            for c in range(2):
                along_x = (c == 0) != second
                to = ((x + step) % SIDE, y) if along_x else (x, (y + step) % SIDE)
                moves.append(((x * SIDE + y) * 2 + c, (to[0] * SIDE + to[1]) * 2 + c))
    return lax.ppermute(value, ("x", "y", "c"), moves)


def plus(a, b):
    return (a + b.astype(F32)).astype(BF)


def ring_sum(cuts):
    far_a, far_b, up_a, up_b, down_a, down_b, own = cuts
    met_a, met_b = shift(far_a, False, 1), shift(far_b, False, 3)
    from_b, from_a = shift(up_b, False, 1), shift(down_a, False, 3)
    ring_a = shift(plus(up_a, met_a), False, 1)
    ring_b = shift(plus(down_b, met_b), False, 3)
    return own, (ring_a, from_a, from_b, ring_b)


def ring_gather(a, b):
    below_a, above_b = shift(a, False, 1), shift(b, False, 3)
    below_b, above_a = shift(b, False, 1), shift(a, False, 3)
    far_a, far_b = shift(below_a, False, 1), shift(above_b, False, 3)
    return a, b, below_a, below_b, far_a, far_b, above_a, above_b


def scatter(parts):
    return [parts[0]] + [shift(parts[k], True, k) for k in (1, 2, 3)]


def spread(value):
    return [value] + [shift(value, True, k) for k in (1, 2, 3)]


def per_device(mlp_inputs, enc_weight, enc_bias, active, dec_weight, target):
    rows = mlp_inputs.shape[0]
    x, y, c = (lax.axis_index(a) for a in "xyc")
    first, second = jnp.where(c == 0, x, y), jnp.where(c == 0, y, x)
    place = jnp.stack([x, y, c, first, second]).astype(jnp.int32)
    scale = 1.0 / math.sqrt(rows)

    top, bottom, dec_sent, tgt_own, tgt_sent = pre_call(
        place, mlp_inputs, enc_weight, dec_weight, target
    )
    top, bottom = z_sum(top, top), z_sum(bottom, bottom)
    dec_got = swap(dec_sent)
    tgt_got = swap(tgt_sent)
    dec_own, done = pick_call(place, dec_weight, bottom[0])
    lat = [
        latent_call(0, top, active, enc_bias, top[0]),
        latent_call(1, bottom, active, enc_bias, done),
    ]
    lat_sib = [swap(half) for half in lat]

    own, parts = ring_sum(rebuild_call(place, lat, lat_sib, dec_own, dec_got))
    parts = scatter(sum_call(place, own, parts))
    err = error_call(scale, place, tgt_own, tgt_got, parts)
    x_turned, lat_turned, done = turn_call(mlp_inputs, lat, err)
    own_turned, got_turned, done = turn_dec_call(dec_own, dec_got, done)
    parts = ring_gather(*join_call(place, spread(err), done))

    err, grad_got = back_sib_call(place, parts, got_turned)
    grad_got = swap(grad_got)
    top, low_top, bottom, low_bottom, err = total_call(
        back_own_call(place, err, own_turned), grad_got, err
    )
    dec_grad, done = dec_call(place, lat_turned, err)
    top, bottom = z_sum(top, low_top, done), z_sum(bottom, low_bottom, done)
    dec_grad, done = dec_call(place, lat_turned, swap(err), dec_grad)
    enc_grad, bias_grad = enc_call(x_turned, active, done, top, bottom)
    return enc_grad, bias_grad.reshape(-1), dec_grad


def solution(mesh):
    grid = Mesh(mesh.devices.reshape(4, 4, 4, 2), ("z", "x", "y", "c"))
    lat = ("x", "y", "c")
    in_specs = (
        P(None, "z"),
        P("z", lat),
        P(lat),
        P(None, lat),
        P(None, lat, "z"),
        P(None, lat, "z"),
    )
    out_specs = (P("z", lat), P(lat), P(None, lat, "z"))
    return jax.shard_map(
        per_device, mesh=grid, in_specs=in_specs, out_specs=out_specs, check_vma=False
    )
```

```python
import functools
import math

import jax
import jax.numpy as jnp
from jax import lax
from jax.experimental import pallas as pl
from jax.experimental.pallas import tpu as pltpu
from jax.sharding import Mesh, PartitionSpec as P

BF = jnp.bfloat16
F32 = jnp.float32
VMEM_LIMIT = 16 * 1024 * 1024
PRE_LIMIT = 52 * 1024 * 1024
SIDE = 4


def dot(a, b, ca, cb):
    return lax.dot_general(a, b, (((ca,), (cb,)), ((), ())), preferred_element_type=F32)


def call(body, name, grid, ins, outs, shapes, args, flops, moved, scratch=(), core=None, limit=VMEM_LIMIT, aliases=None):
    spec = dict(grid=grid, in_specs=ins, out_specs=outs, scratch_shapes=list(scratch))
    if core is not None:
        spec = dict(grid_spec=pltpu.PrefetchScalarGridSpec(num_scalar_prefetch=1, **spec))
        args = (core,) + tuple(args)
    return pl.pallas_call(
        body,
        out_shape=shapes,
        compiler_params=pltpu.CompilerParams(
            dimension_semantics=("arbitrary",) * len(grid), vmem_limit_bytes=limit
        ),
        cost_estimate=pl.CostEstimate(
            flops=int(flops), bytes_accessed=int(moved), transcendentals=0
        ),
        name=name,
        input_output_aliases=aliases or {},
        **spec,
    )(*args)


STEPS = 2


def pre_kernel(p_ref, x_ref, w_ref, dec_ref, tgt_ref, a_ref, b_ref, *refs):
    outs, (x_buf, w_buf, acc, sems) = refs[:3], refs[3:]
    depth = x_ref.shape[1]
    step = depth // STEPS
    half = outs[0].shape[2]
    copies = []
    for k in range(STEPS):
        at = slice(k * step, (k + 1) * step)
        copies.append(pltpu.make_async_copy(w_ref.at[at, :], w_buf.at[at, :], sems.at[2 * k]))
        copies.append(pltpu.make_async_copy(x_ref.at[:, at], x_buf.at[:, at], sems.at[2 * k + 1]))
    sides = ((dec_ref, 1 - p_ref[2]), (tgt_ref, p_ref[2]), (tgt_ref, 1 - p_ref[2]))
    for i, ((src, side), to) in enumerate(zip(sides, outs)):
        at = pl.ds(pl.multiple_of(side * half, half), half)
        copies.append(pltpu.make_async_copy(src.at[:, :, at], to, sems.at[2 * STEPS + i]))
    for copy in copies:
        copy.start()
    for k in range(STEPS):
        copies[2 * k].wait()
        copies[2 * k + 1].wait()
        at = slice(k * step, (k + 1) * step)
        part = jnp.dot(x_buf[:, at], w_buf[at, :], preferred_element_type=F32)
        if k == 0:
            acc[...] = part
        else:
            acc[...] += part
    n = a_ref.shape[0]
    a_ref[...] = acc[:n, :].astype(BF)
    b_ref[...] = acc[n:, :].astype(BF)
    for copy in copies[2 * STEPS :]:
        copy.wait()


def pre_call(place, x, w, dec, target):
    rows, depth = x.shape
    lats = w.shape[1]
    targets, few, wide = target.shape
    part = pl.BlockSpec((rows // 2, lats), lambda i, p: (0, 0))
    outs = [pltpu.VMEM((rows // 2, lats), BF)] * 2
    outs += [pltpu.VMEM((targets, lats, wide // 2), BF)]
    outs += [pltpu.VMEM((targets, few, wide // 2), BF)] * 2
    return call(
        pre_kernel,
        "pre",
        (1,),
        [pl.BlockSpec(memory_space=pl.ANY)] * 4,
        [part, part] + [pl.BlockSpec(memory_space=pl.ANY)] * 3,
        outs,
        (x, w, dec, target),
        2 * rows * depth * lats,
        2 * (rows + lats) * depth,
        [
            pltpu.VMEM((rows, depth), BF),
            pltpu.VMEM((depth, lats), BF),
            pltpu.VMEM((rows, lats), F32),
            pltpu.SemaphoreType.DMA((2 * STEPS + 3,)),
        ],
        core=place,
        limit=PRE_LIMIT,
    )


def total_kernel(own_ref, got_ref, err_ref, *refs):
    rows = own_ref.shape[0] // 2
    for r in range(2):
        at = slice(r * rows, (r + 1) * rows)
        total = own_ref[at, :] + got_ref[at, :].astype(F32)
        refs[2 * r][...] = total
        refs[2 * r + 1][...] = total.astype(BF)


def total_call(own, got, err):
    rows, lats = own.shape
    whole = pl.BlockSpec(own.shape, lambda i: (0, 0))
    part = pl.BlockSpec((rows // 2, lats), lambda i: (0, 0))
    kept = [jax.ShapeDtypeStruct((rows // 2, lats), kind) for kind in (F32, BF)]
    return call(
        total_kernel,
        "total",
        (1,),
        [whole, whole, pl.BlockSpec(memory_space=pl.ANY)],
        [part] * 4 + [pl.BlockSpec(memory_space=pl.ANY)],
        kept * 2 + [jax.ShapeDtypeStruct(err.shape, BF)],
        (own, got, err),
        own.size,
        12 * own.size,
        aliases={2: 4},
    )


def latent_kernel(near_ref, far_ref, active_ref, bias_ref, after_ref, out_ref):
    total = near_ref[...] + far_ref[...].astype(F32) + bias_ref[...]
    out_ref[...] = jnp.where(active_ref[...] > 0, total, 0.0).astype(BF)


def latent_call(r, terms, active, bias, after):
    rows, lats = terms[0].shape
    part = pl.BlockSpec((rows, lats), lambda i: (0, 0))
    return call(
        latent_kernel,
        f"latents_{r}",
        (1,),
        [
            part,
            part,
            pl.BlockSpec((rows, lats), lambda i: (r, 0)),
            pl.BlockSpec((1, lats), lambda i: (0, 0)),
            pl.BlockSpec(memory_space=pl.ANY),
        ],
        part,
        jax.ShapeDtypeStruct((rows, lats), BF),
        (*terms, active, bias.reshape(1, lats), after),
        4 * rows * lats,
        2e6,
    )


def pick_kernel(p_ref, dec_ref, after_ref, out_ref, done_ref):
    out_ref[...] = dec_ref[...]
    done_ref[...] = jnp.zeros(done_ref.shape, F32)


def pick_call(place, dec, after):
    targets, lats, wide = dec.shape
    half = wide // 2
    return call(
        pick_kernel,
        "pick_half",
        (targets,),
        [
            pl.BlockSpec((1, lats, half), lambda t, p: (t, 0, p[2])),
            pl.BlockSpec(memory_space=pl.ANY),
        ],
        [
            pl.BlockSpec((1, lats, half), lambda t, p: (t, 0, 0)),
            pl.BlockSpec((8, 128), lambda t, p: (0, 0)),
        ],
        [
            jax.ShapeDtypeStruct((targets, lats, half), BF),
            jax.ShapeDtypeStruct((8, 128), F32),
        ],
        (dec, after),
        0,
        4 * targets * lats * half,
        core=place,
    )


def place_of(p_ref, far, near):
    return jnp.where(p_ref[2] == 1, far * SIDE + near, near * SIDE + far)


def rebuild_kernel(p_ref, *refs):
    halves, (dec_ref, got_ref), outs, (lat, sib) = refs[:4], refs[4:6], refs[6:-2], refs[-2:]
    piece, half = outs[-1].shape[2:]
    strip, q = SIDE * piece, half // 2

    @pl.when(pl.program_id(0) == 0)
    def _():
        for x in range(SIDE):
            for y in range(SIDE):
                first, other = (jnp.where(p_ref[2] == 1, a, b) for a, b in ((x, y), (y, x)))
                spot = lax.rem(first - p_ref[3] + SIDE, SIDE) * SIDE + other
                to = pl.ds(pl.multiple_of(spot * piece, piece), piece)
                r, src = divmod((x * SIDE + y) * piece, halves[0].shape[0])
                lat[to, :] = halves[r][src : src + piece, :]
                sib[to, :] = halves[2 + r][src : src + piece, :]

    total = jnp.dot(lat[...], dec_ref[0], preferred_element_type=F32)
    total += jnp.dot(sib[...], got_ref[0], preferred_element_type=F32)
    for ref, (step, lo, hi) in zip(outs, CUTS):
        block = total[step * strip : (step + 1) * strip, lo * q : hi * q]
        ref[:, 0] = block.astype(ref.dtype).reshape(SIDE, piece, (hi - lo) * q)


CUTS = ((2, 0, 1), (2, 1, 2), (1, 0, 1), (1, 1, 2), (3, 0, 1), (3, 1, 2), (0, 0, 2))
KINDS = (BF, BF, F32, BF, BF, F32, F32)


def rebuild_call(place, lat, sib, dec, got):
    rows, lats = lat[0].shape
    rows *= 2
    targets, _, half = got.shape
    piece = rows // (SIDE * SIDE)
    widths = [(hi - lo) * half // 2 for _, lo, hi in CUTS]
    part = pl.BlockSpec((rows // 2, lats), lambda t, p: (0, 0))
    return call(
        rebuild_kernel,
        "rebuild",
        (targets,),
        [
            part,
            part,
            part,
            part,
            pl.BlockSpec((1, lats, half), lambda t, p: (t, 0, 0)),
            pl.BlockSpec((1, lats, half), lambda t, p: (t, 0, 0)),
        ],
        [pl.BlockSpec((SIDE, 1, piece, w), lambda t, p: (0, t, 0, 0)) for w in widths],
        [
            jax.ShapeDtypeStruct((SIDE, targets, piece, w), kind)
            for w, kind in zip(widths, KINDS)
        ],
        (*lat, *sib, dec, got),
        4 * rows * lats * half * targets,
        11e6,
        [pltpu.VMEM((rows, lats), BF)] * 2,
        core=place,
    )


def sum_kernel(p_ref, own_ref, *refs):
    parts, outs, held = refs[:4], refs[4:-1], refs[-1]
    q = held.shape[2] // 2
    for h in range(2):
        cols = slice(h * q, (h + 1) * q)
        total = own_ref[:, 0, :, cols]
        for part in parts[2 * h : 2 * h + 2]:
            total += part[:, 0].astype(F32)
        held[:, :, cols] = total
    for k in range(SIDE):
        outs[k][0] = held[lax.rem(p_ref[4] + k, SIDE)].astype(outs[k].dtype)


def sum_call(place, own, parts):
    _, targets, piece, half = own.shape
    block = pl.BlockSpec((SIDE, 1, piece, half // 2), lambda t, p: (0, t, 0, 0))
    return call(
        sum_kernel,
        "sum_first",
        (targets,),
        [pl.BlockSpec((SIDE, 1, piece, half), lambda t, p: (0, t, 0, 0))] + [block] * 4,
        [pl.BlockSpec((1, piece, half), lambda t, p: (t, 0, 0))] * SIDE,
        [jax.ShapeDtypeStruct((targets, piece, half), F32 if k == 0 else BF) for k in range(SIDE)],
        (own, *parts),
        4 * own.size,
        12 * own.size,
        [pltpu.VMEM((SIDE, piece, half), F32)],
        core=place,
    )


def error_kernel(scale, p_ref, own_ref, got_ref, *refs):
    parts, out, goal = refs[:SIDE], refs[SIDE], refs[SIDE + 1]
    few = own_ref.shape[1]
    for ref, side in ((own_ref, p_ref[2]), (got_ref, 1 - p_ref[2])):
        goal[:, pl.ds(pl.multiple_of(side * few, few), few), :] = ref[...].astype(F32)
    total = parts[0][...]
    for part in parts[1:]:
        total += part[...].astype(F32)
    out[...] = ((total - goal[...]) * scale).astype(BF)


def error_call(scale, place, own, got, parts):
    shape = parts[0].shape
    one = pl.BlockSpec(shape, lambda t, p: (0, 0, 0))
    goal = pl.BlockSpec(own.shape, lambda t, p: (0, 0, 0))
    return call(
        functools.partial(error_kernel, scale),
        "error",
        (1,),
        [goal, goal] + [one] * SIDE,
        one,
        jax.ShapeDtypeStruct(shape, BF),
        (own, got, *parts),
        8 * parts[0].size,
        2e6,
        [pltpu.VMEM(shape, F32)],
        core=place,
    )


def join_kernel(p_ref, after_ref, *refs):
    parts, outs = refs[:SIDE], refs[SIDE:]
    q = outs[0].shape[3]
    for k in range(SIDE):
        at = lax.rem(p_ref[4] + SIDE - k, SIDE)
        for h in range(2):
            outs[h][at] = parts[k][:, :, h * q : (h + 1) * q]


def join_call(place, parts, after):
    targets, piece, half = parts[0].shape
    shape = (SIDE, targets, piece, half // 2)
    return call(
        join_kernel,
        "join",
        (1,),
        [pl.BlockSpec(memory_space=pl.ANY)]
        + [pl.BlockSpec(parts[0].shape, lambda t, p: (0, 0, 0))] * SIDE,
        [pl.BlockSpec(shape, lambda t, p: (0, 0, 0, 0))] * 2,
        [jax.ShapeDtypeStruct(shape, BF)] * 2,
        (after, *parts),
        0,
        8 * parts[0].size,
        core=place,
    )


def back_dot(err, dec_ref, out_ref, acc):
    t = pl.program_id(0)
    part = dot(err, dec_ref[0], 1, 0)

    @pl.when(t == 0)
    def _():
        acc[...] = part

    @pl.when(t > 0)
    def _():
        acc[...] += part

    @pl.when(t == pl.num_programs(0) - 1)
    def _():
        out_ref[...] = acc[...].astype(out_ref.dtype)


def back_sib_kernel(p_ref, dec_ref, *refs):
    parts, (err_ref, out_ref, acc) = refs[: 2 * SIDE], refs[2 * SIDE :]
    piece, q = parts[0].shape[2:]
    for k in range(SIDE):
        far = lax.rem(p_ref[3] + SIDE - k, SIDE)
        for i in range(SIDE):
            at = pl.ds(pl.multiple_of(place_of(p_ref, far, i) * piece, piece), piece)
            for h in range(2):
                err_ref[0, at, h * q : (h + 1) * q] = parts[2 * k + h][i, 0]
    back_dot(err_ref[0], dec_ref, out_ref, acc)


def back_sib_call(place, parts, dec):
    _, targets, piece, q = parts[0].shape
    half, lats = dec.shape[1:]
    rows = SIDE * SIDE * piece
    return call(
        back_sib_kernel,
        "back_sib",
        (targets,),
        [
            pl.BlockSpec((1, half, lats), lambda t, p: (t, 0, 0)),
        ]
        + [pl.BlockSpec((SIDE, 1, piece, q), lambda t, p: (0, t, 0, 0))] * (2 * SIDE),
        [
            pl.BlockSpec((1, rows, half), lambda t, p: (t, 0, 0)),
            pl.BlockSpec((rows, lats), lambda t, p: (0, 0)),
        ],
        [
            jax.ShapeDtypeStruct((targets, rows, half), BF),
            jax.ShapeDtypeStruct((rows, lats), BF),
        ],
        (dec, *parts),
        2 * rows * lats * half * targets,
        10e6,
        [pltpu.VMEM((rows, lats), F32)],
        core=place,
    )


def back_own_kernel(p_ref, err_ref, dec_ref, out_ref, acc):
    back_dot(err_ref[0], dec_ref, out_ref, acc)


def back_own_call(place, err, dec):
    targets, rows, half = err.shape
    lats = dec.shape[2]
    return call(
        back_own_kernel,
        "back_own",
        (targets,),
        [
            pl.BlockSpec((1, rows, half), lambda t, p: (t, 0, 0)),
            pl.BlockSpec((1, half, lats), lambda t, p: (t, 0, 0)),
        ],
        pl.BlockSpec((rows, lats), lambda t, p: (0, 0)),
        jax.ShapeDtypeStruct((rows, lats), F32),
        (err, dec),
        2 * rows * lats * half * targets,
        7e6,
        [pltpu.VMEM((rows, lats), F32)],
        core=place,
    )


def turn_kernel(x_ref, top_ref, bottom_ref, after_ref, x_out, lat_out, done_ref):
    done_ref[...] = jnp.zeros(done_ref.shape, F32)
    x_out[...] = x_ref[...].T

    @pl.when(pl.program_id(0) == 0)
    def _():
        n = top_ref.shape[0]
        lat_out[:, :n] = top_ref[...].T
        lat_out[:, n:] = bottom_ref[...].T


def turn_call(x, lat, after):
    rows, depth = x.shape
    lats = lat[0].shape[1]
    step = 512
    part = pl.BlockSpec((rows // 2, lats), lambda i: (0, 0))
    turned = pl.BlockSpec((lats, rows), lambda i: (0, 0))
    return call(
        turn_kernel,
        "turn",
        (depth // step,),
        [
            pl.BlockSpec((rows, step), lambda i: (0, i)),
            part,
            part,
            pl.BlockSpec(memory_space=pl.ANY),
        ],
        [
            pl.BlockSpec((step, rows), lambda i: (i, 0)),
            turned,
            pl.BlockSpec((8, 128), lambda i: (0, 0)),
        ],
        [jax.ShapeDtypeStruct((depth, rows), BF)]
        + [jax.ShapeDtypeStruct((lats, rows), BF)]
        + [jax.ShapeDtypeStruct((8, 128), F32)],
        (x, *lat, after),
        0,
        6e6,
    )


def turn_dec_kernel(own_ref, got_ref, after_ref, own_out, got_out, done_ref):
    done_ref[...] = jnp.zeros(done_ref.shape, F32)
    own_out[0] = own_ref[0].T
    got_out[0] = got_ref[0].T


def turn_dec_call(own, got, after):
    targets, lats, half = own.shape
    plain = pl.BlockSpec((1, lats, half), lambda t: (t, 0, 0))
    turned = pl.BlockSpec((1, half, lats), lambda t: (t, 0, 0))
    return call(
        turn_dec_kernel,
        "turn_dec",
        (targets,),
        [plain, plain, pl.BlockSpec(memory_space=pl.ANY)],
        [turned, turned, pl.BlockSpec((8, 128), lambda t: (0, 0))],
        [jax.ShapeDtypeStruct((targets, half, lats), BF)] * 2
        + [jax.ShapeDtypeStruct((8, 128), F32)],
        (own, got, after),
        0,
        12e6,
    )


def dec_kernel(p_ref, lat_ref, err_ref, *refs):
    out_ref, done_ref = refs[-2:]
    done_ref[...] = jnp.zeros(done_ref.shape, F32)
    out_ref[0] = dot(lat_ref[...], err_ref[0], 1, 0).astype(BF)


def dec_call(place, lat, err, grad=None):
    targets, rows, half = err.shape
    lats = lat.shape[0]
    own = grad is None
    return call(
        dec_kernel,
        "dec_grad_own" if own else "dec_grad_sib",
        (targets,),
        [
            pl.BlockSpec((lats, rows), lambda t, p: (0, 0)),
            pl.BlockSpec((1, rows, half), lambda t, p: (t, 0, 0)),
        ]
        + ([] if own else [pl.BlockSpec(memory_space=pl.ANY)]),
        [
            pl.BlockSpec((1, lats, half), lambda t, p: (t, 0, p[2] if own else 1 - p[2])),
            pl.BlockSpec((8, 128), lambda t, p: (0, 0)),
        ],
        [
            jax.ShapeDtypeStruct((targets, lats, 2 * half), BF),
            jax.ShapeDtypeStruct((8, 128), F32),
        ],
        (lat, err) if own else (lat, err, grad),
        2 * rows * lats * half * targets,
        7e6,
        core=place,
        aliases=None if own else {3: 0},
    )


def enc_kernel(x_ref, active_ref, after_ref, near_a, far_a, near_b, far_b, enc_ref, bias_ref, grad):
    @pl.when(pl.program_id(0) == 0)
    def _():
        rows = near_a.shape[0]
        sums = jnp.zeros(bias_ref.shape, F32)
        for r, (near, far) in enumerate(((near_a, far_a), (near_b, far_b))):
            at = slice(r * rows, (r + 1) * rows)
            total = near[...] + far[...].astype(F32)
            kept = jnp.where(active_ref[at, :] > 0, total, 0.0).astype(BF)
            grad[at, :] = kept
            sums += jnp.sum(kept.astype(F32), axis=0, keepdims=True)
        bias_ref[...] = sums

    enc_ref[...] = dot(x_ref[...], grad[...], 1, 0).astype(BF)


def enc_call(x, active, after, top, bottom):
    depth, rows = x.shape
    lats = active.shape[1]
    step = 1024
    return call(
        enc_kernel,
        "enc_grad",
        (depth // step,),
        [
            pl.BlockSpec((step, rows), lambda i: (i, 0)),
            pl.BlockSpec((rows, lats), lambda i: (0, 0)),
            pl.BlockSpec(memory_space=pl.ANY),
        ]
        + [pl.BlockSpec((rows // 2, lats), lambda i: (0, 0))] * 4,
        [
            pl.BlockSpec((step, lats), lambda i: (i, 0)),
            pl.BlockSpec((1, lats), lambda i: (0, 0)),
        ],
        [jax.ShapeDtypeStruct((depth, lats), BF), jax.ShapeDtypeStruct((1, lats), F32)],
        (x, active, after, *top, *bottom),
        2 * rows * depth * lats,
        7e6,
        [pltpu.VMEM((rows, lats), BF)],
    )


def swap(value):
    return lax.ppermute(value, "c", [(0, 1), (1, 0)])


def pair_kernel(own_ref, got_ref, after_ref, sum_ref, low_ref):
    total = own_ref[...] + got_ref[...].astype(F32)
    sum_ref[...] = total
    low_ref[...] = total.astype(BF)


def pair_call(own, got, after):
    whole = pl.BlockSpec(own.shape, lambda i: (0, 0))
    return call(
        pair_kernel,
        "pair_sum",
        (1,),
        [whole, whole, pl.BlockSpec(memory_space=pl.ANY)],
        [whole, whole],
        [jax.ShapeDtypeStruct(own.shape, kind) for kind in (F32, BF)],
        (own, got, after),
        own.size,
        12 * own.size,
    )


EVEN = (1, 0, 3, 2)
ODD = (3, 2, 1, 0)


def pair(value, tables):
    moves = [(z * 2 + c, tables[c][z] * 2 + c) for z in range(SIDE) for c in range(2)]
    return lax.ppermute(value, ("z", "c"), moves)


def z_sum(part, low, after=None):
    got = pair(low, (EVEN, ODD))
    if after is None:
        first = part.astype(F32) + got.astype(F32)
        return first, pair(first.astype(BF), (ODD, EVEN))
    first, low = pair_call(part, got, after)
    return first, pair(low, (ODD, EVEN))


def shift(value, second, step):
    moves = []
    for x in range(SIDE):
        for y in range(SIDE):
            for c in range(2):
                along_x = (c == 1) != second
                to = ((x + step) % SIDE, y) if along_x else (x, (y + step) % SIDE)
                moves.append(((x * SIDE + y) * 2 + c, (to[0] * SIDE + to[1]) * 2 + c))
    return lax.ppermute(value, ("x", "y", "c"), moves)


def plus(a, b):
    return (a + b.astype(F32)).astype(BF)


def ring_sum(cuts):
    far_a, far_b, up_a, up_b, down_a, down_b, own = cuts
    met_a, met_b = shift(far_a, False, 1), shift(far_b, False, 3)
    from_b, from_a = shift(up_b, False, 1), shift(down_a, False, 3)
    ring_a = shift(plus(up_a, met_a), False, 1)
    ring_b = shift(plus(down_b, met_b), False, 3)
    return own, (ring_a, from_a, from_b, ring_b)


def ring_gather(a, b):
    below_a, above_b = shift(a, False, 1), shift(b, False, 3)
    below_b, above_a = shift(b, False, 1), shift(a, False, 3)
    far_a, far_b = shift(below_a, False, 1), shift(above_b, False, 3)
    return a, b, below_a, below_b, far_a, far_b, above_a, above_b


def scatter(parts):
    return [parts[0]] + [shift(parts[k], True, k) for k in (1, 2, 3)]


def spread(value):
    return [value] + [shift(value, True, k) for k in (1, 2, 3)]


def per_device(mlp_inputs, enc_weight, enc_bias, active, dec_weight, target):
    rows = mlp_inputs.shape[0]
    x, y, c = (lax.axis_index(a) for a in "xyc")
    first, second = jnp.where(c == 1, x, y), jnp.where(c == 1, y, x)
    place = jnp.stack([x, y, c, first, second]).astype(jnp.int32)
    scale = 1.0 / math.sqrt(rows)

    top, bottom, dec_sent, tgt_own, tgt_sent = pre_call(
        place, mlp_inputs, enc_weight, dec_weight, target
    )
    top, bottom = z_sum(top, top), z_sum(bottom, bottom)
    dec_got = swap(dec_sent)
    tgt_got = swap(tgt_sent)
    dec_own, done = pick_call(place, dec_weight, bottom[0])
    lat = [
        latent_call(0, top, active, enc_bias, top[0]),
        latent_call(1, bottom, active, enc_bias, done),
    ]
    lat_sib = [swap(half) for half in lat]

    own, parts = ring_sum(rebuild_call(place, lat, lat_sib, dec_own, dec_got))
    parts = scatter(sum_call(place, own, parts))
    err = error_call(scale, place, tgt_own, tgt_got, parts)
    x_turned, lat_turned, done = turn_call(mlp_inputs, lat, err)
    own_turned, got_turned, done = turn_dec_call(dec_own, dec_got, done)
    parts = ring_gather(*join_call(place, spread(err), done))

    err, grad_got = back_sib_call(place, parts, got_turned)
    grad_got = swap(grad_got)
    top, low_top, bottom, low_bottom, err = total_call(
        back_own_call(place, err, own_turned), grad_got, err
    )
    dec_grad, done = dec_call(place, lat_turned, err)
    top, bottom = z_sum(top, low_top, done), z_sum(bottom, low_bottom, done)
    dec_grad, done = dec_call(place, lat_turned, swap(err), dec_grad)
    enc_grad, bias_grad = enc_call(x_turned, active, done, top, bottom)
    return enc_grad, bias_grad.reshape(-1), dec_grad


def solution(mesh):
    grid = Mesh(mesh.devices.reshape(4, 4, 4, 2), ("z", "x", "y", "c"))
    lat = ("x", "y", "c")
    in_specs = (
        P(None, "z"),
        P("z", lat),
        P(lat),
        P(None, lat),
        P(None, lat, "z"),
        P(None, lat, "z"),
    )
    out_specs = (P("z", lat), P(lat), P(None, lat, "z"))
    return jax.shard_map(
        per_device, mesh=grid, in_specs=in_specs, out_specs=out_specs, check_vma=False
    )
```
